128 devices in a mesh: gx: 4 (over x), gy: 4 (over z), gz: 8 (over y, core).
Axes of the slice: x: 4, y: 4, z: 4, core: 2. Of those that a mesh axis runs over, the one named last changes fastest.
Arguments:
- sources: bfloat16 [8, 32, 32, 27, 128], P('gx', 'gy', 'gz'), may hold values from -6 to 6
- geometry: float32 [8, 32, 32, 108], P('gx', 'gy', 'gz'), may hold values from 0.6 to 4.8
- rock_class: int32 [8, 32, 32], P('gx', 'gy', 'gz'), may hold values from 0 to 15
- permeability: float32 [16, 3], replicated, may hold values from 0.1 to 10
- mass_inv: float32 [108, 108], replicated, may hold values from -0.015 to 2.7, as said below
- div_map: float32 [27, 108], replicated, may hold values from -0.625 to 0.625
- trace_map: float32 [54, 108], replicated, may hold values from -0.625 to 0.625
- dirichlet: int32 [8, 32, 32, 3], P('gx', 'gy', 'gz'), may hold values 0 or 1
Outputs:
- traces: float32 [8, 32, 32, 27, 128], P('gx', 'gy', 'gz')
- flux: bfloat16 [8, 32, 32, 108, 128], P('gx', 'gy', 'gz')
The draws below stay inside these ranges and needn't reach their ends.
Inputs may be any that keep to these rules, and one draw needn't show every extreme that they name: `mass_inv`: symmetric; every diagonal entry exceeds the sum of the magnitudes of the other entries of its row.
All inputs are finite; a program needn't handle non-finite values. No bound on the sum of `dirichlet` on one device may be relied on, other than what follows from the above.
Results may differ from the reference program's by a relative error of at most 0.0029.
Values sent between devices are 32-bit elements; how exact they have to be, the bound alone decides.
A program may use at most 128 MiB of HBM per device.

```python
import math
import jax
import jax.numpy as jnp
from jax import lax

RHS = 128
CLASSES = 16
ITERS = 3
FLUX = 108
PRESS = 27
TRACE = 54
NX = 8
NY = 32
NZ = 32


def draw_geometry(key, part):
    key = jax.random.fold_in(key, 11)
    position = jnp.arange(NX, dtype=jnp.float32) / max(NX - 1, 1)
    rough = jnp.exp(jax.random.uniform(key, (NX, NY, NZ, FLUX), jnp.float32, jnp.log(0.6), jnp.log(1.6)))
    trend = jnp.exp(jnp.log(3.0) * position)
    return rough * trend[:, None, None, None]


def draw_mass_inv(key, part):
    key = jax.random.fold_in(key, 23)
    first_key, second_key = jax.random.split(key)
    spread = jax.random.uniform(first_key, (FLUX, FLUX), jnp.float32, -0.015, 0.015)
    middle = jax.random.uniform(second_key, (FLUX,), jnp.float32, 1.7, 2.7)
    symmetric = 0.5 * (spread + spread.T)
    unit_matrix = jnp.eye(FLUX, dtype=jnp.float32)
    return symmetric * (1.0 - unit_matrix) + unit_matrix * middle[None, :]


def place_ends(array, own_key, smallest, top_value):
    longest = array.shape.index(max(array.shape))
    spots = []
    for shift in (0, 1):
        where = [jax.random.randint(jax.random.fold_in(own_key, axis), (), 0, length) for axis, length in enumerate(array.shape)]
        where[longest] = (where[longest] + shift) % array.shape[longest]
        spots.append(tuple(where))
    return array.at[spots[0]].set(smallest).at[spots[1]].set(top_value)


def shard_levels(stream_key, shape, pieces, least, largest):
    loudness, own = 1.0, jax.random.fold_in(stream_key, 6)
    for dim, shards_of in pieces:
        steps = jnp.exp(jax.random.uniform(jax.random.fold_in(own, dim), (shards_of,), jnp.float32, least / len(pieces), largest / len(pieces)))
        loudness = loudness * jnp.repeat(steps, shape[dim] // shards_of).reshape([-1 if axis == dim else 1 for axis in range(len(shape))])
    return loudness


def centred(key, dims, width, reach, shards=(), kind=jnp.bfloat16):
    values = jax.random.normal(key, dims, jnp.float32) * width
    if len(shards) > 0:
        values = shard_levels(key, dims, shards, -0.22, 0.18) * values
    return jnp.clip(values, min=-reach, max=reach).astype(kind)


def setup_inputs(seed: int = 0) -> dict:
    splits = jax.random.split(jax.random.key(seed), 9)
    sources = centred(splits[0], (NX, NY, NZ, PRESS, RHS), 1.0, 6.0, ((0, 4), (1, 4), (2, 8)))
    geometry = draw_geometry(jax.random.fold_in(splits[8], 71), 0)
    rock_class = place_ends(jax.random.randint(splits[2], (NX, NY, NZ), 0, CLASSES), jax.random.fold_in(splits[2], 1), 0, CLASSES - 1).astype(jnp.int32)
    permeability = jnp.clip(jnp.exp(jax.random.uniform(splits[3], (CLASSES, 3), jnp.float32, math.log(0.1), math.log(10.0))), 0.1, 10.0)
    mass_inv = draw_mass_inv(jax.random.fold_in(splits[8], 71), 0)
    div_map = centred(splits[5], (PRESS, FLUX), FLUX ** -0.5, 0.625, (), jnp.float32)
    trace_map = centred(splits[6], (TRACE, FLUX), FLUX ** -0.5, 0.625, (), jnp.float32)
    dirichlet = place_ends((jax.random.randint(splits[7], (NX, NY, NZ, 3), 0, 8) < 1).astype(jnp.int32), jax.random.fold_in(splits[7], 1), 0, 1)
    return dict(sources=sources, geometry=geometry, rock_class=rock_class, permeability=permeability, mass_inv=mass_inv, div_map=div_map, trace_map=trace_map, dirichlet=dirichlet)


finest = lax.Precision.HIGHEST

def slab_blocks(geometry, rock_class, permeability, mass_inv, div_map, trace_map):
    flux_dofs = mass_inv.shape[0]
    elements = rock_class.size
    rooted = jnp.sqrt(permeability)[rock_class.reshape(elements).astype(jnp.int32)]
    scaling = geometry.reshape(elements, flux_dofs) * jnp.repeat(rooted, flux_dofs // 3, axis=1)
    joined = jnp.concatenate([div_map, trace_map], axis=0)
    scaled = joined[None, :, :] * scaling[:, None, :]
    applied = jnp.einsum('eai,ij->eaj', scaled, mass_inv, precision=finest)
    coupled = jnp.einsum('eaj,ebj->eab', applied, scaled, precision=finest)
    pressures = div_map.shape[0]
    schur = coupled[:, :pressures, :pressures]
    mixed = coupled[:, :pressures, pressures:]
    solved = jnp.linalg.solve(schur, mixed)
    condensed = coupled[:, pressures:, pressures:] - jnp.einsum('ept,eps->ets', mixed, solved, precision=finest)
    return (scaling, schur, mixed, solved, condensed)

def upper_roll(owned):
    return jnp.stack([jnp.roll(owned[:, :, :, normal], -1, axis=normal) for normal in range(3)], axis=3)

def return_roll(lower_side, upper_side):
    return lower_side + jnp.stack([jnp.roll(upper_side[:, :, :, normal], 1, axis=normal) for normal in range(3)], axis=3)

def reference(sources, geometry, rock_class, permeability, mass_inv, div_map, trace_map, dirichlet):
    blocks = lax.map(lambda slab: slab_blocks(slab[0], slab[1], permeability, mass_inv, div_map, trace_map), (geometry, rock_class))
    elements = NX * NY * NZ
    scaling, schur, mixed, solved, condensed = [item.reshape((elements,) + item.shape[2:]) for item in blocks]
    joined = jnp.concatenate([div_map, trace_map], axis=0)
    keep = (1 - dirichlet).astype(jnp.float32)[:, :, :, :, None, None]
    block_shape = (NX, NY, NZ)

    def element_vector(owned):
        columns = owned.shape[-1]
        return jnp.concatenate([owned.reshape(elements, -1, columns), upper_roll(owned).reshape(elements, -1, columns)], axis=1)

    def assemble(values):
        half = values.shape[1] // 2
        columns = values.shape[-1]
        return return_roll(values[:, :half].reshape(block_shape + (3, -1, columns)), values[:, half:].reshape(block_shape + (3, -1, columns)))
    diagonal = assemble(jnp.diagonal(condensed, axis1=1, axis2=2)[:, :, None])
    inverse = keep / diagonal
    group = 16 if RHS % 16 == 0 else RHS
    forcing_all = jnp.moveaxis(sources.astype(jnp.float32).reshape(NX, NY, NZ, PRESS, RHS // group, group), 4, 0)

    def inner(first, second):
        return lax.optimization_barrier(jnp.sum(first * second, axis=(0, 1, 2, 3, 4)))

    def solve_group(forcing):
        forcing = forcing.reshape(elements, PRESS, group)

        def operate(vector):
            return assemble(jnp.einsum('ets,esr->etr', condensed, element_vector(vector), precision=finest)) * keep
        residual = assemble(jnp.einsum('ept,epr->etr', solved, forcing, precision=finest)) * keep
        solution = jnp.zeros_like(residual)
        precond = inverse * residual
        direction = precond
        current = inner(residual, precond)
        for step in range(ITERS):
            image = operate(direction)
            alpha = current / inner(direction, image)
            solution = solution + alpha * direction
            residual = residual - alpha * image
            precond = inverse * residual
            following = inner(residual, precond)
            direction = precond + following / current * direction
            current = following
        values = element_vector(solution)
        pressure = -jnp.linalg.solve(schur, forcing + jnp.einsum('ept,etr->epr', mixed, values, precision=finest))
        summed = jnp.einsum('ai,ear->eir', joined, jnp.concatenate([pressure, values], axis=1), precision=finest)
        flux = -scaling[:, :, None] * jnp.einsum('ij,ejr->eir', mass_inv, scaling[:, :, None] * summed, precision=finest)
        return (solution.reshape(NX, NY, NZ, -1, group), flux.astype(jnp.bfloat16).reshape(NX, NY, NZ, -1, group))
    traces_all, flux_all = lax.map(solve_group, forcing_all)
    traces = jnp.moveaxis(traces_all, 0, 4).reshape(NX, NY, NZ, -1, RHS)
    flux = jnp.moveaxis(flux_all, 0, 4).reshape(NX, NY, NZ, -1, RHS)
    return (traces, flux)
```

```python
import functools

import jax
import jax.numpy as jnp
from jax import lax
from jax.experimental import pallas as pl
from jax.experimental.pallas import tpu as pltpu
from jax.sharding import PartitionSpec as P

MESH = pl.DeviceIdType.MESH
BF16 = jnp.bfloat16
F32 = jnp.float32

COLS = 128
PRESS = 27
FLUX = 108
BX, BY, BZ = 2, 8, 4
ELEMENTS = BX * BY * BZ

TR = 64
PR = 32

GROUP = 72
X_GROUPS = 0
Y_GROUPS = 12
Z_GROUPS = 21
GROUPS = 31
FIELD = GROUPS * GROUP

BLOCKED = 1e30


def dot3(a, b):
    return jnp.dot(a, b, precision=lax.Precision.HIGH, preferred_element_type=F32)


def lanes_of(shape):
    return lax.broadcasted_iota(jnp.int32, shape, len(shape) - 1)


def packed_pair(value):
    lane = lanes_of(value.shape)
    high = value.astype(BF16).astype(F32)
    low = value - high
    first = jnp.where(lane < 64, high, pltpu.roll(high, 64, 1))
    second = jnp.where(lane < 64, low, jnp.where(lane < 96, high, pltpu.roll(low, 32, 1)))
    return first.astype(BF16), second.astype(BF16)


def blocks_kernel(
    rock, geometry, permeability, mass_inv, div_map, trace_map,
    lmat, hmat,
    joined, joined_t, mass, scale, scale_t, fluxes, coupled, table, inverse,
):
    joined[...] = jnp.zeros_like(joined)
    mass[...] = jnp.zeros_like(mass)
    scale[...] = jnp.zeros_like(scale)
    inverse[...] = jnp.zeros_like(inverse)
    mass[0:FLUX, 0:FLUX] = mass_inv[...]
    for facet in range(6):
        joined[8 * facet : 8 * facet + 8, 0:FLUX] = trace_map[9 * facet : 9 * facet + 8, :]
        joined[48 + facet : 49 + facet, 0:FLUX] = trace_map[9 * facet + 8 : 9 * facet + 9, :]
    joined[TR : TR + PRESS, 0:FLUX] = div_map[...]
    joined_t[...] = jnp.transpose(joined[...])

    rooted = jnp.sqrt(permeability[...])
    lane = lanes_of((16, FLUX))
    per_class = jnp.where(
        lane < 36, rooted[:, 0:1], jnp.where(lane < 72, rooted[:, 1:2], rooted[:, 2:3])
    )
    table[0:16, 0:FLUX] = per_class
    for e in range(ELEMENTS):
        i, j, k = e // 32, (e // 4) % 8, e % 4
        row = table[pl.ds(rock[i, j, k], 1), :][:, 0:FLUX]
        scale[e : e + 1, 0:FLUX] = geometry[i, j, k : k + 1, :] * row
    scale_t[...] = jnp.transpose(scale[...])

    @pl.loop(0, ELEMENTS // 8)
    def build(step):
        turned = pltpu.roll(scale_t[...], lax.rem(128 - 8 * step, 128), 1)
        for pair in range(4):
            e = step * 8 + 2 * pair
            first = jnp.broadcast_to(turned[:, 2 * pair : 2 * pair + 1], (128, 128))
            second = jnp.broadcast_to(turned[:, 2 * pair + 1 : 2 * pair + 2], (128, 128))
            columns = jnp.concatenate([first, second], axis=1)
            both = jnp.concatenate([joined_t[...], joined_t[...]], axis=1)
            flux_side = columns * dot3(mass[...], columns * both)
            pair_coupled = dot3(joined[0:96, :], flux_side)
            fluxes[e] = flux_side[0:112, 0:128]
            fluxes[e + 1] = flux_side[0:112, 128:256]
            coupled[pl.ds(pl.multiple_of(e * 96, 96), 96), :] = pair_coupled[:, 0:128]
            coupled[pl.ds(pl.multiple_of((e + 1) * 96, 96), 96), :] = pair_coupled[:, 128:256]

    half = lanes_of((PR, 128)) < 64
    rows = lax.broadcasted_iota(jnp.int32, (PR, 128), 0)

    def with_schur(table_t):
        for pair in range(14):
            first = coupled[pl.ds(TR + 2 * pair, ELEMENTS, stride=96), :]
            second = coupled[pl.ds(TR + 2 * pair + 1, ELEMENTS, stride=96), :]
            turned = jnp.transpose(jnp.concatenate([first, second], axis=0))[TR : TR + PR, :]
            table_t[2 * pair] = turned
            table_t[2 * pair + 1] = pltpu.roll(turned, 64, 1)

        @pl.loop(0, PRESS)
        def eliminate(k):
            mine = rows == k
            pivot = 1.0 / table_t[k, pl.ds(k, 1), :]
            row = jnp.where(mine, 1.0, table_t[k]) * pivot
            for i in range(PRESS):
                factor = table_t[i, pl.ds(k, 1), :]
                table_t[i] = jnp.where(mine, 0.0, table_t[i]) - factor * row
            table_t[k] = row

        table_t[PRESS] = jnp.zeros((PR, 128), F32)
        for pair in range(14):
            both = jnp.where(half, table_t[2 * pair], pltpu.roll(table_t[2 * pair + 1], 64, 1))
            placed = jnp.concatenate(
                [jnp.zeros((TR, 128), F32), both, jnp.zeros((128 - TR - PR, 128), F32)], axis=0
            )
            turned = jnp.transpose(placed)
            inverse[pl.ds(2 * pair, ELEMENTS, stride=PR), :] = turned[0:ELEMENTS]
            inverse[pl.ds(2 * pair + 1, ELEMENTS, stride=PR), :] = turned[ELEMENTS:]

    pl.run_scoped(with_schur, pltpu.VMEM((28, PR, 128), F32))

    @pl.loop(0, ELEMENTS // 4)
    def finish(step):
        for u in range(4):
            e = step * 4 + u
            full = coupled[pl.ds(pl.multiple_of(e * 96, 96), 96), :]
            inv = inverse[pl.ds(pl.multiple_of(e * PR, PR), PR), :]
            padded = jnp.concatenate([full, jnp.zeros((32, 128), F32)], axis=0)
            solved = jnp.where(lanes_of((PR, 128)) < TR, dot3(inv, padded), inv)
            right = jnp.concatenate(
                [jnp.zeros((TR, 128), F32), solved, jnp.zeros((128 - TR - PR, 128), F32)], axis=0
            )
            flux_side = fluxes[e]
            left = jnp.concatenate([full[0:TR], flux_side], axis=0)
            term = dot3(left, right)
            traced = lanes_of((TR, 128)) < TR
            operator = jnp.where(traced, full[0:TR] - term[0:TR], term[0:TR])
            traced = lanes_of((112, 128)) < TR
            recovery = jnp.where(traced, term[TR:] - flux_side, term[TR:])
            one, two = packed_pair(operator)
            lmat[e, :, 0:128] = one
            lmat[e, :, 128:256] = two
            one, two = packed_pair(recovery)
            hmat[e, :, 0:128] = one
            hmat[e, :, 128:256] = two


def element_blocks(rock_class, geometry, permeability, mass_inv, div_map, trace_map):
    return pl.pallas_call(
        blocks_kernel,
        out_shape=(
            jax.ShapeDtypeStruct((ELEMENTS, TR, 256), BF16),
            jax.ShapeDtypeStruct((ELEMENTS, 112, 256), BF16),
        ),
        in_specs=[pl.BlockSpec(memory_space=pltpu.SMEM)] + [pl.BlockSpec(memory_space=pltpu.VMEM)] * 5,
        out_specs=[pl.BlockSpec(memory_space=pltpu.VMEM)] * 2,
        scratch_shapes=[
            pltpu.VMEM((128, 128), F32),
            pltpu.VMEM((128, 128), F32),
            pltpu.VMEM((128, 128), F32),
            pltpu.VMEM((128, 128), F32),
            pltpu.VMEM((128, 128), F32),
            pltpu.VMEM((ELEMENTS, 112, 128), F32),
            pltpu.VMEM((ELEMENTS * 96, 128), F32),
            pltpu.VMEM((16, 128), F32),
            pltpu.VMEM((ELEMENTS * PR, 128), F32),
        ],
        compiler_params=pltpu.CompilerParams(vmem_limit_bytes=48 * 1024 * 1024),
        name="blocks",
    )(rock_class, geometry, permeability, mass_inv, div_map, trace_map)


def facet_rows(g, i, jj, k):
    slot_x, slot_y, slot_z = jj * 4 + k, i * 4 + k, 2 * g + jj
    places = []
    for side in range(2):
        for group, slot in (
            (X_GROUPS + (i + side) * 4 + g, slot_x),
            (Y_GROUPS + 2 * g + jj + side, slot_y),
            (Z_GROUPS + 2 * (k + side) + i, slot_z),
        ):
            places.append((pl.multiple_of(group * GROUP + slot * 8, 8), group * GROUP + 64 + slot))
    return places


def gathered(field, places):
    row = lax.broadcasted_iota(jnp.int32, (8, COLS), 0)
    ninth = jnp.zeros((8, COLS), F32)
    pieces = []
    for facet, (main, extra) in enumerate(places):
        pieces.append(field[pl.ds(main, 8), :])
        line = jnp.broadcast_to(field[pl.ds(extra, 1), :], (8, COLS))
        ninth = jnp.where(row == facet, line, ninth)
    return pieces + [ninth]


def weights_of(pieces):
    vector = jnp.concatenate(pieces + [jnp.zeros((8, COLS), F32)], axis=0)
    high = vector.astype(BF16)
    low = (vector - high.astype(F32)).astype(BF16)
    return jnp.concatenate([high, low, high], axis=0)


def forcing_of(values):
    padded = jnp.concatenate([values.astype(F32), jnp.zeros((PR - PRESS, COLS), F32)], axis=0)
    padded = padded.astype(BF16)
    return jnp.concatenate([padded, padded], axis=0)


def scatter(values, low, up, places, lift=None):
    for facet, (main, extra) in enumerate(places):
        target = low if facet < 3 else up
        first = values[8 * facet : 8 * facet + 8]
        last = values[48 + facet : 49 + facet]
        if lift is not None and facet < 3:
            first = first + lift[facet]
            last = last + lift[facet]
        target[pl.ds(main, 8), :] = first
        target[pl.ds(extra, 1), :] = last


COPIES = 12


def solver_kernel(
    sizes, dirichlet, lmat, sources, out,
    low, up, inverse, fields, mine, parts_x, parts_y, parts_z,
    send, recv, send_sum, recv_sum,
):
    nx, ny, nz = sizes
    ix, iy, iz = lax.axis_index("gx"), lax.axis_index("gy"), lax.axis_index("gz")

    def at_x(step):
        return (lax.rem(ix + step + nx, nx), iy, iz)

    def at_y(step):
        return (ix, lax.rem(iy + step + ny, ny), iz)

    def at_z(step):
        return (ix, iy, lax.rem(iz + step + nz, nz))

    partners = (
        [at_x(s) for s in range(1, nx)] + [at_y(s) for s in range(1, ny)] + [at_z(s) for s in range(1, nz)]
    )
    barrier = pltpu.get_barrier_semaphore()
    for partner in partners:
        pl.semaphore_signal(barrier, inc=1, device_id=partner, device_id_type=MESH)

    def copy(buffer, stage, slot, source, target, count, device):
        return pltpu.make_async_remote_copy(
            src_ref=buffer.at[stage, pl.ds(source * GROUP, count * GROUP)],
            dst_ref=buffer.at[stage, pl.ds(target * GROUP, count * GROUP)],
            send_sem=send.at[stage, slot],
            recv_sem=recv.at[stage, slot],
            device_id=device,
            device_id_type=MESH,
        )

    def copy_x(stage, g):
        return [
            copy(low, stage, g, X_GROUPS + g, X_GROUPS + 8 + g, 1, at_x(-1)),
            copy(up, stage, 4 + g, X_GROUPS + 8 + g, X_GROUPS + g, 1, at_x(1)),
        ]

    def copy_yz(stage):
        return [
            copy(low, stage, 8, Y_GROUPS, Y_GROUPS + 8, 1, at_y(-1)),
            copy(up, stage, 9, Y_GROUPS + 8, Y_GROUPS, 1, at_y(1)),
            copy(low, stage, 10, Z_GROUPS, Z_GROUPS + 8, 2, at_z(-1)),
            copy(up, stage, 11, Z_GROUPS + 8, Z_GROUPS, 2, at_z(1)),
        ]

    def wait(stage):
        for g in range(4):
            for item in copy_x(stage, g):
                item.wait()
        for item in copy_yz(stage):
            item.wait()

    each = [(i, jj, k) for i in range(BX) for jj in range(2) for k in range(BZ)]

    def element_index(g, i, jj, k):
        return i * 32 + 2 * g * 4 + jj * 4 + k

    lane = lanes_of((TR, 256))
    row = lax.broadcasted_iota(jnp.int32, (TR, 256), 0)
    on_diagonal = (lane == row) | (lane == row + 128)
    ones = jnp.ones((256, COLS), BF16)

    pl.semaphore_wait(barrier, len(partners))

    @pl.loop(0, 4)
    def start(g):
        for i, jj, k in each:
            e = element_index(g, i, jj, k)
            places = facet_rows(g, i, jj, k)
            matrix = lmat[e]
            right = jnp.concatenate([jnp.zeros((192, COLS), BF16), forcing_of(sources[e])], axis=0)
            values = jnp.dot(matrix, right, preferred_element_type=F32)
            scatter(values, low.at[0], up.at[0], places)
            only = jnp.where(on_diagonal, matrix.astype(F32), 0.0).astype(BF16)
            diagonal = jnp.dot(only, ones, preferred_element_type=F32)
            lift = [
                dirichlet[i, 2 * g + jj, k, normal].astype(F32) * BLOCKED for normal in range(3)
            ]
            scatter(diagonal, low.at[1], up.at[1], places, lift)
        for stage in (0, 1):
            for item in copy_x(stage, g):
                item.start()

    for stage in (0, 1):
        for item in copy_yz(stage):
            item.start()
    for stage in (0, 1):
        wait(stage)

    zero = jnp.zeros((8, COLS), F32)

    def begin(group, total):
        for tile in range(9):
            place = pl.ds(pl.multiple_of(group * GROUP + tile * 8, 8), 8)
            diagonal = low[1, place, :] + up[1, place, :]
            scale = jnp.where(diagonal > 0.5 * BLOCKED, 0.0, 1.0 / diagonal)
            inverse[place, :] = scale
            residual = low[0, place, :] + up[0, place, :]
            precond = scale * residual
            fields[0, place, :] = precond
            total = total + residual * precond
        return total

    square = zero
    for first, owned, last in ((0, 8, 12), (12, 20, 21), (21, 29, 31)):
        square = lax.fori_loop(first, owned, begin, square)
        lax.fori_loop(owned, last, begin, zero)

    moments = [square]
    for step in range(3):
        stage = step + 2

        def apply(g, totals):
            totals = list(totals)
            for i, jj, k in each:
                e = element_index(g, i, jj, k)
                places = facet_rows(g, i, jj, k)
                pieces = gathered(fields.at[step], places)
                right = jnp.concatenate([weights_of(pieces), jnp.zeros((64, COLS), BF16)], axis=0)
                values = jnp.dot(lmat[e], right, preferred_element_type=F32)
                others = [pieces]
                if step > 0:
                    others.append(gathered(fields.at[step - 1], places))
                for which, other in enumerate(others):
                    for tile in range(7):
                        totals[which] = totals[which] + other[tile] * values[8 * tile : 8 * tile + 8]
                if step < 2:
                    scatter(values, low.at[stage], up.at[stage], places)
            if step < 2:
                for item in copy_x(stage, g):
                    item.start()
            return tuple(totals)

        totals = lax.fori_loop(0, 4, apply, (zero,) * (1 if step == 0 else 2))
        moments.extend(totals)
        if step < 2:
            for item in copy_yz(stage):
                item.start()
            wait(stage)

            @pl.loop(0, GROUPS)
            def advance(group):
                for tile in range(9):
                    place = pl.ds(pl.multiple_of(group * GROUP + tile * 8, 8), 8)
                    image = low[stage, place, :] + up[stage, place, :]
                    fields[step + 1, place, :] = inverse[place, :] * image - fields[step, place, :]

    sublane = lax.broadcasted_iota(jnp.int32, (8, COLS), 0)
    tile = zero
    for which, moment in enumerate(moments):
        line = jnp.broadcast_to(jnp.sum(moment, axis=0, keepdims=True), (8, COLS))
        tile = jnp.where(sublane == which, line, tile)

    offset = 0
    for stage, (count, at, parts) in enumerate(((nx, at_x, parts_x), (ny, at_y, parts_y), (nz, at_z, parts_z))):
        mine[stage] = tile
        copies = []
        for s in range(1, count):
            copies.append(
                pltpu.make_async_remote_copy(
                    src_ref=mine.at[stage],
                    dst_ref=parts.at[s - 1],
                    send_sem=send_sum.at[offset + s - 1],
                    recv_sem=recv_sum.at[offset + s - 1],
                    device_id=at(s),
                    device_id_type=MESH,
                )
            )
        for item in copies:
            item.start()
        for s, item in enumerate(copies):
            item.wait()
            tile = tile + parts[s]
        offset += count - 1

    b0, g00, g11, g01, g22, g12 = [tile[n : n + 1] for n in range(6)]
    b1 = g00 - b0
    b2 = g01 - b1
    g02 = g11
    l1, l2 = g01 / g00, g02 / g00
    h11, h12, h22 = g11 - l1 * g01, g12 - l1 * g02, g22 - l2 * g02
    d1, d2 = b1 - l1 * b0, b2 - l2 * b0
    sound = h11 > 2e-6 * g11
    m = jnp.where(sound, h12 / h11, 0.0)
    k22 = h22 - m * h12
    c2 = jnp.where(k22 > 2e-6 * g22, (d2 - m * d1) / k22, 0.0)
    c1 = jnp.where(sound, (d1 - h12 * c2) / h11, 0.0)
    c0 = (b0 - g01 * c1 - g02 * c2) / g00
    c0, c1, c2 = [jnp.broadcast_to(c, (8, COLS)) for c in (c0, c1, c2)]

    @pl.loop(0, GROUPS)
    def combine(group):
        for tile in range(9):
            place = pl.ds(pl.multiple_of(group * GROUP + tile * 8, 8), 8)
            out[place, :] = c0 * fields[0, place, :] + c1 * fields[1, place, :] + c2 * fields[2, place, :]


def solve(sizes, dirichlet, lmat, sources):
    partners = sum(sizes) - 3
    return pl.pallas_call(
        functools.partial(solver_kernel, sizes),
        out_shape=jax.ShapeDtypeStruct((FIELD, COLS), F32),
        in_specs=[pl.BlockSpec(memory_space=pltpu.SMEM)] + [pl.BlockSpec(memory_space=pltpu.VMEM)] * 2,
        out_specs=pl.BlockSpec(memory_space=pltpu.VMEM),
        scratch_shapes=[
            pltpu.VMEM((4, FIELD, COLS), F32),
            pltpu.VMEM((4, FIELD, COLS), F32),
            pltpu.VMEM((FIELD, COLS), F32),
            pltpu.VMEM((3, FIELD, COLS), F32),
            pltpu.VMEM((3, 8, COLS), F32),
            pltpu.VMEM((sizes[0] - 1, 8, COLS), F32),
            pltpu.VMEM((sizes[1] - 1, 8, COLS), F32),
            pltpu.VMEM((sizes[2] - 1, 8, COLS), F32),
            pltpu.SemaphoreType.DMA((4, COPIES)),
            pltpu.SemaphoreType.DMA((4, COPIES)),
            pltpu.SemaphoreType.DMA((partners,)),
            pltpu.SemaphoreType.DMA((partners,)),
        ],
        compiler_params=pltpu.CompilerParams(
            collective_id=0, has_side_effects=True, vmem_limit_bytes=48 * 1024 * 1024
        ),
        name="solver",
    )(dirichlet, lmat, sources)


def recover_kernel(field, hmat, sources, traces, flux):
    step = pl.program_id(0)
    i, g = step // 4, lax.rem(step, 4)
    for jj in range(2):
        for k in range(BZ):
            u = jj * 4 + k
            places = facet_rows(g, i, jj, k)
            pieces = gathered(field, places)
            ninth = pieces[6]
            for normal in range(3):
                traces[u, 9 * normal : 9 * normal + 8, :] = pieces[normal]
                traces[u, 9 * normal + 8 : 9 * normal + 9, :] = ninth[normal : normal + 1]
            right = jnp.concatenate([weights_of(pieces), forcing_of(sources[u])], axis=0)
            values = jnp.dot(hmat[u], right, preferred_element_type=F32)
            flux[u] = values[0:FLUX].astype(BF16)


def recover(field, hmat, sources):
    return pl.pallas_call(
        recover_kernel,
        grid=(ELEMENTS // 8,),
        out_shape=(
            jax.ShapeDtypeStruct((ELEMENTS, PRESS, COLS), F32),
            jax.ShapeDtypeStruct((ELEMENTS, FLUX, COLS), BF16),
        ),
        in_specs=[
            pl.BlockSpec((FIELD, COLS), lambda s: (0, 0)),
            pl.BlockSpec((8, 112, 256), lambda s: (s, 0, 0)),
            pl.BlockSpec((8, PRESS, COLS), lambda s: (s, 0, 0)),
        ],
        out_specs=[
            pl.BlockSpec((8, PRESS, COLS), lambda s: (s, 0, 0)),
            pl.BlockSpec((8, FLUX, COLS), lambda s: (s, 0, 0)),
        ],
        compiler_params=pltpu.CompilerParams(vmem_limit_bytes=32 * 1024 * 1024),
        name="recover",
    )(field, hmat, sources)


def body(sizes, sources, geometry, rock_class, permeability, mass_inv, div_map, trace_map, dirichlet):
    forcing = sources.reshape(ELEMENTS, PRESS, COLS)
    lmat, hmat = element_blocks(rock_class, geometry, permeability, mass_inv, div_map, trace_map)
    field = solve(sizes, dirichlet, lmat, forcing)
    traces, flux = recover(field, hmat, forcing)
    return (
        traces.reshape(BX, BY, BZ, PRESS, COLS),
        flux.reshape(BX, BY, BZ, FLUX, COLS),
    )


def solution(mesh):
    sizes = (mesh.shape["gx"], mesh.shape["gy"], mesh.shape["gz"])
    placed = (
        P("gx", "gy", "gz", None, None),
        P("gx", "gy", "gz", None),
        P("gx", "gy", "gz"),
        P(),
        P(),
        P(),
        P(),
        P("gx", "gy", "gz", None),
    )
    return jax.shard_map(
        functools.partial(body, sizes),
        mesh=mesh,
        in_specs=placed,
        out_specs=(P("gx", "gy", "gz", None, None), P("gx", "gy", "gz", None, None)),
        check_vma=False,
    )
```

```python
import functools

import jax
import jax.numpy as jnp
from jax import lax
from jax.experimental import pallas as pl
from jax.experimental.pallas import tpu as pltpu
from jax.sharding import PartitionSpec as P

MESH = pl.DeviceIdType.MESH
BF16 = jnp.bfloat16
F32 = jnp.float32

COLS = 128
PRESS = 27
FLUX = 108
BX, BY, BZ = 2, 8, 4
ELEMENTS = BX * BY * BZ

TR = 64
PR = 32
FR = 112
AR = TR + FR

GROUP = 72
Z_GROUP = 40
Y_START = 12 * GROUP
Z_START = Y_START + 9 * GROUP
FIELD = Z_START + 20 * Z_GROUP

BLOCKED = 1e30
MIB = 1024 * 1024

BATCH = 16


def lanes_of(shape):
    return lax.broadcasted_iota(jnp.int32, shape, len(shape) - 1)


def rows_of(shape):
    return lax.broadcasted_iota(jnp.int32, shape, len(shape) - 2)


def halves(value):
    high = value.astype(BF16)
    return high, (value - high.astype(F32)).astype(BF16)


def blocks_kernel(
    rock, dirichlet, geometry_hbm, permeability_hbm, mass_hbm, div_hbm, trace_hbm, sources_hbm,
    lmat, hmat, forcing, diagonals,
    geometry, permeability, mass_in, div_map, trace_map, sources,
    joined, joined_t, padded, scale_t, left_mass, left_joined,
    highs, lows, press, inverse, table, spread, columns, first, second, solved_in, right, sems,
):
    loads = [
        pltpu.make_async_copy(source, target, sems.at[n])
        for n, (source, target) in enumerate(
            (
                (trace_hbm, trace_map),
                (div_hbm, div_map),
                (mass_hbm, mass_in),
                (permeability_hbm, permeability),
                (geometry_hbm, geometry),
                (sources_hbm, sources),
            )
        )
    ]
    for item in loads:
        item.start()
    joined[...] = jnp.zeros_like(joined)
    padded[...] = jnp.zeros_like(padded)
    inverse[...] = jnp.zeros_like(inverse)
    for item in loads[:4]:
        item.wait()

    for facet in range(6):
        joined[8 * facet : 8 * facet + 8, 0:FLUX] = trace_map[9 * facet : 9 * facet + 8, :]
        joined[48 + facet : 49 + facet, 0:FLUX] = trace_map[9 * facet + 8 : 9 * facet + 9, :]
    joined[TR : TR + PRESS, 0:FLUX] = div_map[...]
    joined[TR + PR : TR + PR + PRESS, 0:FLUX] = div_map[...]
    joined_t[...] = jnp.transpose(joined[...])
    high, low = halves(joined[0 : TR + PR, :])
    left_joined[:, 0:128] = high
    left_joined[:, 128:256] = high
    left_joined[:, 256:384] = low
    padded[0:FLUX, 0:FLUX] = mass_in[...]
    high, low = halves(padded[0:FR, :])
    left_mass[:, 0:128] = high
    left_mass[:, 128:256] = high
    left_mass[:, 256:384] = low

    padded[...] = jnp.zeros_like(padded)
    padded[0:3, 0:16] = jnp.sqrt(permeability[...])
    rooted = jnp.transpose(padded[...])[0:16]
    lane = lanes_of((16, 128))
    table[0:16, :] = jnp.where(
        lane < 36, rooted[:, 0:1], jnp.where(lane < 72, rooted[:, 1:2], rooted[:, 2:3])
    )
    padded[...] = jnp.zeros_like(padded)
    loads[4].wait()
    for e in range(ELEMENTS):
        i, j, k = e // 32, (e // 4) % 8, e % 4
        row = table[pl.ds(rock[i, k, j], 1), :][:, 0:FLUX]
        padded[e : e + 1, 0:FLUX] = geometry[i, j, k : k + 1, :] * row
    scale_t[...] = jnp.transpose(padded[...])

    no_rows = jnp.zeros((128 - FR, 256), BF16)
    for pair in range(BATCH // 2):
        for part in range(3):
            first[pair, 128 * part + FR : 128 * part + 128, :] = no_rows
            second[pair, 128 * part + FR : 128 * part + 128, :] = no_rows

    @pl.loop(0, ELEMENTS // BATCH)
    def build(step):
        turned = pltpu.roll(scale_t[0:FR, :], lax.rem(128 - BATCH * step, 128), 1)
        for pair in range(BATCH // 2):
            for n in range(2):
                column = jnp.broadcast_to(turned[:, 2 * pair + n : 2 * pair + n + 1], (FR, 128))
                cut = slice(128 * n, 128 * n + 128)
                columns[pair, :, cut] = column
                high, low = halves(column * joined_t[0:FR, :])
                first[pair, 0:FR, cut] = high
                first[pair, 128 : 128 + FR, cut] = low
                first[pair, 256 : 256 + FR, cut] = high
        for pair in range(BATCH // 2):
            flux_side = columns[pair] * jnp.dot(left_mass[...], first[pair], preferred_element_type=F32)
            high, low = halves(flux_side)
            second[pair, 0:FR, :] = high
            second[pair, 128 : 128 + FR, :] = low
            second[pair, 256 : 256 + FR, :] = high
            for n in range(2):
                e = step * BATCH + 2 * pair + n
                cut = slice(128 * n, 128 * n + 128)
                highs[e, TR:AR, :] = high[:, cut]
                lows[e, TR:AR, :] = low[:, cut]
        for pair in range(BATCH // 2):
            coupled = jnp.dot(left_joined[...], second[pair], preferred_element_type=F32)
            high, low = halves(coupled[0:TR])
            for n in range(2):
                e = step * BATCH + 2 * pair + n
                cut = slice(128 * n, 128 * n + 128)
                highs[e, 0:TR, :] = high[:, cut]
                lows[e, 0:TR, :] = low[:, cut]
                press[pl.ds(pl.multiple_of(e * PR, PR), PR), :] = coupled[TR:, cut]

    low_half = lanes_of((PR, 128)) < 64
    row_of = rows_of((PR, 128))

    def invert(work):
        for pair in range(14):
            rows = [press[pl.ds(2 * pair + n, ELEMENTS, stride=PR), :] for n in range(2)]
            work[pair] = jnp.transpose(jnp.concatenate(rows, axis=0))[TR : TR + PR, :]

        for k in range(PRESS):
            owner, ahead = k // 2, (k + 1) // 2 % 14
            mine = row_of == k
            held = low_half if k % 2 == 0 else jnp.logical_not(low_half)
            source = work[owner]
            source = jnp.where(held, source, pltpu.roll(source, 64, 1))
            row = jnp.where(mine, 1.0, source) * (1.0 / source[k : k + 1, :])
            for pair in [ahead] + [p for p in range(14) if p != ahead]:
                value = work[pair]
                value = jnp.where(mine, 0.0, value) - value[k : k + 1, :] * row
                work[pair] = jnp.where(held, row, value) if pair == owner else value

        for pair in range(14):
            placed = jnp.concatenate(
                [work[pair], jnp.zeros((PR, 128), F32), work[pair], work[pair]], axis=0
            )
            turned = jnp.transpose(placed)
            inverse[pl.ds(2 * pair, ELEMENTS, stride=PR), :] = turned[0:ELEMENTS]
            inverse[pl.ds(2 * pair + 1, ELEMENTS, stride=PR), :] = turned[ELEMENTS:]

    pl.run_scoped(invert, pltpu.VMEM((14, PR, 128), F32))

    lane = lanes_of((TR, 256))
    unit = jnp.where((jnp.bitwise_and(lane, 63) == rows_of((TR, 256))) & (lane < 192), 1.0, 0.0)
    unit = unit.astype(BF16)
    for u in range(BATCH):
        solved_in[u, PR:TR, :] = jnp.zeros((PR, 128), BF16)
        right[u, 0:64, :] = unit
        right[u, 128:192, :] = unit
        right[u, 224:256, :] = jnp.zeros((PR, 256), BF16)
    lane = lanes_of((PR, 128))
    lane_t = lanes_of((TR, 128))
    on_diagonal = lane_t == rows_of((TR, 128))
    line = lanes_of((1, 128))
    lane_f = lanes_of((AR, 128))
    kept_high = (lane_f >= TR) & (lane_f < TR + PR)
    x_lanes = (line < 8) | (line == 48)
    y_lanes = ((line >= 8) & (line < 16)) | (line == 49)
    z_lanes = ((line >= 16) & (line < 24)) | (line == 50)

    @pl.loop(0, ELEMENTS // BATCH)
    def finish(step):
        for u in range(BATCH):
            e = step * BATCH + u
            high, low = halves(press[pl.ds(pl.multiple_of(e * PR, PR), PR), :])
            solved_in[u, 0:PR, :] = low
            solved_in[u, TR : TR + PR, :] = high
            solved_in[u, TR + PR :, :] = high
        for u in range(BATCH):
            e = step * BATCH + u
            inv = inverse[pl.ds(pl.multiple_of(e * PR, PR), PR), :]
            left = jnp.where(lane < TR + PR, inv, inv - inv.astype(BF16).astype(F32)).astype(BF16)
            solved = jnp.dot(left, solved_in[u], preferred_element_type=F32)
            for part, other in enumerate((pltpu.roll(solved, TR, 1), inv)):
                high, low = halves(-jnp.where(lane < TR, solved, other))
                cut = slice(128 * part, 128 * part + 128)
                right[u, 64:96, cut] = high
                right[u, 96:128, cut] = low
                right[u, 192:224, cut] = high
        for u in range(BATCH):
            e = step * BATCH + u
            left = jnp.concatenate([highs[e], lows[e]], axis=1)
            result = jnp.dot(left, right[u], preferred_element_type=F32)
            both, rest = result[:, 0:128], result[:, 128:256]
            diagonals[pl.ds(e, 1), :] = jnp.sum(
                jnp.where(on_diagonal, both[0:TR], 0.0), axis=0, keepdims=True
            )
            both = both.astype(BF16)
            rest = jnp.where(kept_high, rest, rest - rest.astype(BF16).astype(F32)).astype(BF16)
            lmat[e, :, 0:128] = both[0:TR]
            lmat[e, :, 128:256] = rest[0:TR]
            hmat[e, :, 0:128] = both[TR:]
            hmat[e, :, 128:256] = rest[TR:]

    for e in range(ELEMENTS):
        i, j, k = e // 32, (e // 4) % 8, e % 4
        lift = [dirichlet[i, normal, k, j].astype(F32) * BLOCKED for normal in range(3)]
        diagonals[e : e + 1, :] = diagonals[e : e + 1, :] + jnp.where(
            x_lanes, lift[0], jnp.where(y_lanes, lift[1], jnp.where(z_lanes, lift[2], 0.0))
        )

    loads[5].wait()
    for part in range(4):
        spread[...] = sources[432 * part : 432 * part + 432, :].astype(F32)
        for jj in range(4):
            for k in range(BZ):
                e = part * 16 + jj * 4 + k
                values = spread[pl.ds(108 * jj + k, PRESS, stride=4), :]
                values = jnp.concatenate([values, jnp.zeros((PR - PRESS, COLS), F32)], axis=0)
                forcing[e] = values.astype(BF16)


def element_blocks(rock_class, dirichlet, geometry, permeability, mass_inv, div_map, trace_map, sources):
    smem, hbm, vmem = [
        pl.BlockSpec(memory_space=space) for space in (pltpu.SMEM, pltpu.HBM, pltpu.VMEM)
    ]
    return pl.pallas_call(
        blocks_kernel,
        out_shape=(
            jax.ShapeDtypeStruct((ELEMENTS, TR, 256), BF16),
            jax.ShapeDtypeStruct((ELEMENTS, FR, 256), BF16),
            jax.ShapeDtypeStruct((ELEMENTS, PR, COLS), BF16),
            jax.ShapeDtypeStruct((ELEMENTS, 128), F32),
        ),
        in_specs=[smem] * 2 + [hbm] * 6,
        out_specs=[vmem] * 4,
        scratch_shapes=[
            pltpu.VMEM(geometry.shape, F32),
            pltpu.VMEM(permeability.shape, F32),
            pltpu.VMEM(mass_inv.shape, F32),
            pltpu.VMEM(div_map.shape, F32),
            pltpu.VMEM(trace_map.shape, F32),
            pltpu.VMEM(sources.shape, BF16),
            pltpu.VMEM((128, 128), F32),
            pltpu.VMEM((128, 128), F32),
            pltpu.VMEM((128, 128), F32),
            pltpu.VMEM((128, 128), F32),
            pltpu.VMEM((FR, 384), BF16),
            pltpu.VMEM((TR + PR, 384), BF16),
            pltpu.VMEM((ELEMENTS, AR, 128), BF16),
            pltpu.VMEM((ELEMENTS, AR, 128), BF16),
            pltpu.VMEM((ELEMENTS * PR, 128), F32),
            pltpu.VMEM((ELEMENTS * PR, 128), F32),
            pltpu.VMEM((16, 128), F32),
            pltpu.VMEM((432, 128), F32),
            pltpu.VMEM((BATCH // 2, FR, 256), F32),
            pltpu.VMEM((BATCH // 2, 384, 256), BF16),
            pltpu.VMEM((BATCH // 2, 384, 256), BF16),
            pltpu.VMEM((BATCH, 128, 128), BF16),
            pltpu.VMEM((BATCH, 256, 256), BF16),
            pltpu.SemaphoreType.DMA((6,)),
        ],
        compiler_params=pltpu.CompilerParams(vmem_limit_bytes=28 * MIB),
        name="blocks",
    )(rock_class, dirichlet, geometry, permeability, mass_inv, div_map, trace_map, sources)


def facet_rows(g, i, jj, k):
    places = []
    for side in range(2):
        for start, size, slot in (
            (((i + side) * 4 + g) * GROUP, 64, jj * 4 + k),
            (Y_START + (2 * g + jj + side) * GROUP, 64, i * 4 + k),
            (Z_START + ((k + side) * 4 + g) * Z_GROUP, 32, i * 2 + jj),
        ):
            places.append((pl.multiple_of(start + slot * 8, 8), start + size + slot))
    return places


def gathered(field, places):
    row = rows_of((8, COLS))
    ninth = jnp.zeros((8, COLS), F32)
    pieces = []
    for facet, (main, extra) in enumerate(places):
        pieces.append(field[pl.ds(main, 8), :])
        line = jnp.broadcast_to(field[pl.ds(extra, 1), :], (8, COLS))
        ninth = jnp.where(row == facet, line, ninth)
    return pieces + [ninth]


def scatter(values, low, up, places):
    for facet, (main, extra) in enumerate(places):
        target = low if facet < 3 else up
        target[pl.ds(main, 8), :] = values[8 * facet : 8 * facet + 8]
        target[pl.ds(extra, 1), :] = values[48 + facet : 49 + facet]


EACH = [(i, jj, k) for i in range(BX) for jj in range(2) for k in range(BZ)]


def element_index(g, i, jj, k):
    return i * 32 + g * 8 + jj * 4 + k


def solver_kernel(
    sizes, diagonals, lmat, forcing, vectors, scales,
    low, up, inverse, fields, weights, near, turned, mine, parts_x, parts_y, parts_z,
    send, recv, send_y, recv_y, send_d, recv_d, send_sum, recv_sum,
):
    nx, ny, nz = sizes
    ix, iy, iz = lax.axis_index("gx"), lax.axis_index("gy"), lax.axis_index("gz")

    def at_x(step):
        return (lax.rem(ix + step + nx, nx), iy, iz)

    def at_y(step):
        return (ix, lax.rem(iy + step + ny, ny), iz)

    def at_z(step):
        return (ix, iy, lax.rem(iz + step + nz, nz))

    partners = (
        [at_x(s) for s in range(1, nx)] + [at_y(s) for s in range(1, ny)] + [at_z(s) for s in range(1, nz)]
    )
    barrier = pltpu.get_barrier_semaphore()
    for partner in partners:
        pl.semaphore_signal(barrier, inc=1, device_id=partner, device_id_type=MESH)

    zero = jnp.zeros((8, COLS), F32)
    for u in range(len(EACH)):
        weights[u, 3 * TR : 4 * TR, :] = jnp.zeros((TR, COLS), BF16)

    @pl.loop(0, 16)
    def clear(group):
        for stage in range(3):
            start = Z_START + 32 + group * Z_GROUP
            low[stage, pl.ds(pl.multiple_of(start, 8), 8), :] = zero
            up[stage, pl.ds(pl.multiple_of(start + 4 * Z_GROUP, 8), 8), :] = zero

    @pl.loop(0, 20)
    def clear_inverse(group):
        inverse[pl.ds(pl.multiple_of(Z_START + 32 + group * Z_GROUP, 8), 8), :] = zero

    def remote(source, target, sent, received, device):
        return pltpu.make_async_remote_copy(
            src_ref=source, dst_ref=target, send_sem=sent, recv_sem=received,
            device_id=device, device_id_type=MESH,
        )

    def field_copy(buffer, stage, source, target, count, sent, received, device):
        return remote(
            buffer.at[stage, pl.ds(pl.multiple_of(source, 8), count)],
            buffer.at[stage, pl.ds(pl.multiple_of(target, 8), count)],
            sent, received, device,
        )

    def copies_xz(stage, g):
        x, z = g * GROUP, Z_START + g * Z_GROUP
        x_last, z_last = x + 8 * GROUP, z + 16 * Z_GROUP
        return [
            field_copy(low, stage, x, x_last, GROUP, send.at[stage, 0, g], recv.at[stage, 0, g], at_x(-1)),
            field_copy(up, stage, x_last, x, GROUP, send.at[stage, 1, g], recv.at[stage, 1, g], at_x(1)),
            field_copy(low, stage, z, z_last, Z_GROUP, send.at[stage, 2, g], recv.at[stage, 2, g], at_z(-1)),
            field_copy(up, stage, z_last, z, Z_GROUP, send.at[stage, 3, g], recv.at[stage, 3, g], at_z(1)),
        ]

    def copy_y(stage, side):
        first, last = Y_START, Y_START + 8 * GROUP
        if side == 0:
            return field_copy(low, stage, first, last, GROUP, send_y.at[stage, 0], recv_y.at[stage, 0], at_y(-1))
        return field_copy(up, stage, last, first, GROUP, send_y.at[stage, 1], recv_y.at[stage, 1], at_y(1))

    pl.semaphore_wait(barrier, len(partners))

    half = ELEMENTS // 2
    near_copies = [
        remote(diagonals.at[pl.ds(half, half)], near.at[0, pl.ds(0, half)], send_d.at[0], recv_d.at[0], at_x(1)),
        remote(diagonals.at[pl.ds(0, half)], near.at[1, pl.ds(0, half)], send_d.at[1], recv_d.at[1], at_x(-1)),
        remote(diagonals, near.at[2], send_d.at[2], recv_d.at[2], at_y(1)),
        remote(diagonals, near.at[3], send_d.at[3], recv_d.at[3], at_y(-1)),
        remote(diagonals, near.at[4], send_d.at[4], recv_d.at[4], at_z(1)),
        remote(diagonals, near.at[5], send_d.at[5], recv_d.at[5], at_z(-1)),
    ]
    for item in near_copies:
        item.start()

    def order(n):
        return lax.rem(3 * n, 4)

    def send_chunk(stage, n):
        for item in copies_xz(stage, order(n)):
            item.start()
        for side in range(2):
            @pl.when(n == side)
            def _():
                copy_y(stage, side).start()

    @pl.loop(0, 4)
    def start(n):
        g = order(n)
        for i, jj, k in EACH:
            e = element_index(g, i, jj, k)
            right = jnp.concatenate([jnp.zeros((TR, COLS), BF16), forcing[e], forcing[e]], axis=0)
            values = -jnp.dot(lmat[e, :, 128:256], right, preferred_element_type=F32)
            scatter(values, low.at[0], up.at[0], facet_rows(g, i, jj, k))
        send_chunk(0, n)

    for item in near_copies:
        item.wait()
    lane, row = lanes_of((ELEMENTS, 128)), rows_of((ELEMENTS, 128))
    x_lanes = (lane < 8) | (lane == 48)
    y_lanes = ((lane >= 8) & (lane < 16)) | (lane == 49)

    def uppers(value):
        return jnp.where(lane < 24, pltpu.roll(value, 104, 1), pltpu.roll(value, 125, 1))

    def reciprocal(total):
        return jnp.where(total > 0.5 * BLOCKED, 0.0, 1.0 / total)

    own = diagonals[...]
    own_up = uppers(own)
    from_x = jnp.concatenate([uppers(near[0])[0:half], own_up[0:half]], axis=0)
    first_y, first_z = jnp.bitwise_and(row, 31) < 4, jnp.bitwise_and(row, 3) == 0
    from_y = jnp.where(first_y, pltpu.roll(uppers(near[2]), 36, 0), pltpu.roll(own_up, 4, 0))
    from_z = jnp.where(first_z, pltpu.roll(uppers(near[4]), 61, 0), pltpu.roll(own_up, 1, 0))
    lower_sum = own + jnp.where(x_lanes, from_x, jnp.where(y_lanes, from_y, from_z))
    above_x = jnp.concatenate([near[1, 0:half, :], near[1, 0:half, :]], axis=0)
    above_y, above_z = pltpu.roll(near[3], 28, 0), pltpu.roll(near[5], 3, 0)
    upper_sum = own_up + jnp.where(x_lanes, above_x, jnp.where(y_lanes, above_y, above_z))
    flipped = jnp.transpose(jnp.concatenate([reciprocal(lower_sum), reciprocal(upper_sum)], axis=0))
    turned[0:24, :] = flipped[0:24]
    turned[24:32, :] = flipped[48:56]

    @pl.loop(0, 4)
    def expand(g):
        rolled = pltpu.roll(turned[...], lax.rem(128 - 8 * g, 128), 1)
        for i, jj, k in EACH:
            column = i * 32 + jj * 4 + k
            places = facet_rows(g, i, jj, k)
            for side in range(2):
                normals = [0, 1, 2] if side == 0 else [n for n, last in enumerate((i == 1, jj == 1, k == 3)) if last]
                if not normals:
                    continue
                at = 64 * side + column
                ninth = jnp.broadcast_to(rolled[24:32, at : at + 1], (8, COLS))
                for normal in normals:
                    main, extra = places[3 * side + normal]
                    inverse[pl.ds(main, 8), :] = jnp.broadcast_to(
                        rolled[8 * normal : 8 * normal + 8, at : at + 1], (8, COLS)
                    )
                    inverse[pl.ds(extra, 1), :] = ninth[normal : normal + 1]

    def update(step, g, total):
        spans = [((plane * 4 + g) * GROUP, 9, plane < 2) for plane in range(3)]
        spans += [(Y_START + (2 * g + plane) * GROUP, 9, plane < 2) for plane in range(3)]
        spans += [(Z_START + (plane * 4 + g) * Z_GROUP, 5, plane < 4) for plane in range(5)]
        for begin, tiles, owned in spans:
            for tile in range(tiles):
                place = pl.ds(pl.multiple_of(begin + tile * 8, 8), 8)
                value = low[step, place, :] + up[step, place, :]
                scaled = inverse[place, :] * value
                if step == 0:
                    fields[0, place, :] = scaled
                    if owned:
                        total = total + value * scaled
                else:
                    fields[step, place, :] = scaled - fields[step - 1, place, :]
        return total

    def operate(step, n, totals):
        g = order(n)
        totals = list(totals)
        for item in copies_xz(step, g):
            item.wait_recv()
        for side in range(2):
            @pl.when(n == 1 - side)
            def _():
                copy_y(step, side).wait_recv()
        totals[0] = update(step, g, totals[0])
        for u, (i, jj, k) in enumerate(EACH):
            pieces = gathered(fields.at[step], facet_rows(g, i, jj, k))
            vector = jnp.concatenate(pieces + [jnp.zeros((8, COLS), F32)], axis=0)
            vectors[step, element_index(g, i, jj, k)] = vector
            high, low_part = halves(vector)
            weights[u, 0:TR, :] = high
            weights[u, TR : 2 * TR, :] = low_part
            weights[u, 2 * TR : 3 * TR, :] = high
        for u, (i, jj, k) in enumerate(EACH):
            e = element_index(g, i, jj, k)
            values = jnp.dot(lmat[e], weights[u], preferred_element_type=F32)
            for which in range(1 if step == 0 else 2):
                products = vectors[step - which, e] * values
                parts = [products[8 * tile : 8 * tile + 8] for tile in range(7)]
                part = (parts[0] + parts[1]) + (parts[2] + parts[3])
                part = part + ((parts[4] + parts[5]) + parts[6])
                totals[1 + which] = totals[1 + which] + part
            if step < 2:
                scatter(values, low.at[step + 1], up.at[step + 1], facet_rows(g, i, jj, k))
        if step < 2:
            send_chunk(step + 1, n)
        return tuple(totals)

    moments = []
    for step in range(3):
        totals = lax.fori_loop(0, 4, functools.partial(operate, step), (zero,) * 3)
        moments += [totals[:2], totals[1:], totals[1:]][step]

    sublane = rows_of((8, COLS))
    tile = zero
    for which, moment in enumerate(moments):
        line = jnp.broadcast_to(jnp.sum(moment, axis=0, keepdims=True), (8, COLS))
        tile = jnp.where(sublane == which, line, tile)

    offset = 0
    for stage, (count, at, parts) in enumerate(((nx, at_x, parts_x), (ny, at_y, parts_y), (nz, at_z, parts_z))):
        mine[stage] = tile
        copies = [
            remote(mine.at[stage], parts.at[s - 1], send_sum.at[offset + s - 1], recv_sum.at[offset + s - 1], at(s))
            for s in range(1, count)
        ]
        for item in copies:
            item.start()
        for s, item in enumerate(copies):
            item.wait()
            tile = tile + parts[s]
        offset += count - 1

    b0, g00, g11, g01, g22, g12 = [tile[n : n + 1] for n in range(6)]
    b1 = g00 - b0
    b2 = g01 - b1
    g02 = g11
    l1, l2 = g01 / g00, g02 / g00
    h11, h12, h22 = g11 - l1 * g01, g12 - l1 * g02, g22 - l2 * g02
    d1, d2 = b1 - l1 * b0, b2 - l2 * b0
    sound = h11 > 2e-6 * g11
    m = jnp.where(sound, h12 / h11, 0.0)
    k22 = h22 - m * h12
    c2 = jnp.where(k22 > 2e-6 * g22, (d2 - m * d1) / k22, 0.0)
    c1 = jnp.where(sound, (d1 - h12 * c2) / h11, 0.0)
    c0 = (b0 - g01 * c1 - g02 * c2) / g00
    for n, c in enumerate((c0, c1, c2)):
        scales[8 * n : 8 * n + 8, :] = jnp.broadcast_to(c, (8, COLS))

    @pl.loop(0, 4)
    def drain(g):
        for stage in range(3):
            for item in copies_xz(stage, g):
                item.wait_send()

    for stage in range(3):
        for side in range(2):
            copy_y(stage, side).wait_send()


def solve(sizes, diagonals, lmat, forcing):
    partners = sum(sizes) - 3
    return pl.pallas_call(
        functools.partial(solver_kernel, sizes),
        out_shape=(
            jax.ShapeDtypeStruct((3, ELEMENTS, TR, COLS), F32),
            jax.ShapeDtypeStruct((24, COLS), F32),
        ),
        in_specs=[pl.BlockSpec(memory_space=pltpu.VMEM)] * 3,
        out_specs=[pl.BlockSpec(memory_space=pltpu.VMEM)] * 2,
        scratch_shapes=[
            pltpu.VMEM((3, FIELD, COLS), F32),
            pltpu.VMEM((3, FIELD, COLS), F32),
            pltpu.VMEM((FIELD, COLS), F32),
            pltpu.VMEM((3, FIELD, COLS), F32),
            pltpu.VMEM((len(EACH), 256, COLS), BF16),
            pltpu.VMEM((6, ELEMENTS, 128), F32),
            pltpu.VMEM((32, 128), F32),
            pltpu.VMEM((3, 8, COLS), F32),
            pltpu.VMEM((sizes[0] - 1, 8, COLS), F32),
            pltpu.VMEM((sizes[1] - 1, 8, COLS), F32),
            pltpu.VMEM((sizes[2] - 1, 8, COLS), F32),
            pltpu.SemaphoreType.DMA((3, 4, 4)),
            pltpu.SemaphoreType.DMA((3, 4, 4)),
            pltpu.SemaphoreType.DMA((3, 2)),
            pltpu.SemaphoreType.DMA((3, 2)),
            pltpu.SemaphoreType.DMA((6,)),
            pltpu.SemaphoreType.DMA((6,)),
            pltpu.SemaphoreType.DMA((partners,)),
            pltpu.SemaphoreType.DMA((partners,)),
        ],
        compiler_params=pltpu.CompilerParams(
            collective_id=0, has_side_effects=True, vmem_limit_bytes=20 * MIB
        ),
        name="solver",
    )(diagonals, lmat, forcing)


def recover_kernel(
    vectors, scales, hmat, forcing, traces_hbm, flux_hbm, weights, traces, flux, spread, sems
):
    rows_t, rows_f = 8 * PRESS, 8 * FLUX
    pitch = 5
    first = rows_of((8, COLS)) < 4

    def copies(n):
        slot = n % 2
        return [
            pltpu.make_async_copy(
                traces.at[slot], traces_hbm.at[pl.ds(n * rows_t, rows_t)], sems.at[slot, 0]
            ),
            pltpu.make_async_copy(flux.at[slot], flux_hbm.at[pl.ds(n * rows_f, rows_f)], sems.at[slot, 1]),
        ]

    for n in range(8):
        slot = n % 2
        if n >= 2:
            for item in copies(n - 2):
                item.wait()
        for u in range(8):
            e = 8 * n + u
            tiles = []
            for tile in range(7):
                place = slice(8 * tile, 8 * tile + 8)
                tiles.append(
                    scales[0:8, :] * vectors[0, e, place, :]
                    + scales[8:16, :] * vectors[1, e, place, :]
                    + scales[16:24, :] * vectors[2, e, place, :]
                )
            start = 108 * (u // 4) + u % 4
            for normal in range(3):
                traces[slot, pl.ds(start + 36 * normal, 8, stride=4), :] = tiles[normal]
                line = start + 36 * normal + 32
                traces[slot, line : line + 1, :] = tiles[6][normal : normal + 1]
            high, low = halves(jnp.concatenate(tiles + [jnp.zeros((8, COLS), F32)], axis=0))
            weights[u, 0:TR, :] = high
            weights[u, TR : 2 * TR, :] = low
            weights[u, 2 * TR : 3 * TR, :] = high
            weights[u, 3 * TR : 3 * TR + PR, :] = forcing[e]
            weights[u, 3 * TR + PR :, :] = forcing[e]
        for u in range(8):
            values = jnp.dot(hmat[8 * n + u], weights[u], preferred_element_type=F32)
            spread[pl.ds(FLUX * pitch * (u // 4) + u % 4, FLUX, stride=pitch), :] = -values[0:FLUX]
        for quad in range(FLUX // 2):
            tiles = []
            for half in range(2):
                at = pitch * (4 * quad + 2 * half)
                tiles.append(jnp.where(first, spread[at : at + 8, :], spread[at + 1 : at + 9, :]))
            flux[slot, 16 * quad : 16 * quad + 16, :] = jnp.concatenate(tiles, axis=0).astype(BF16)
        for item in copies(n):
            item.start()
    for n in (6, 7):
        for item in copies(n):
            item.wait()


def recover(vectors, scales, hmat, forcing):
    vmem, hbm = pl.BlockSpec(memory_space=pltpu.VMEM), pl.BlockSpec(memory_space=pltpu.HBM)
    return pl.pallas_call(
        recover_kernel,
        out_shape=(
            jax.ShapeDtypeStruct((ELEMENTS * PRESS, COLS), F32),
            jax.ShapeDtypeStruct((ELEMENTS * FLUX, COLS), BF16),
        ),
        in_specs=[vmem] * 4,
        out_specs=[hbm] * 2,
        scratch_shapes=[
            pltpu.VMEM((8, 256, COLS), BF16),
            pltpu.VMEM((2, 8 * PRESS, COLS), F32),
            pltpu.VMEM((2, 8 * FLUX, COLS), BF16),
            pltpu.VMEM((5 * 2 * FLUX + 8, COLS), F32),
            pltpu.SemaphoreType.DMA((2, 2)),
        ],
        compiler_params=pltpu.CompilerParams(vmem_limit_bytes=16 * MIB),
        name="recover",
    )(vectors, scales, hmat, forcing)


def body(sizes, sources, geometry, rock_class, permeability, mass_inv, div_map, trace_map, dirichlet):
    interleaved = sources.transpose(0, 1, 3, 2, 4).reshape(ELEMENTS * PRESS, COLS)
    lmat, hmat, forcing, diagonals = element_blocks(
        rock_class.transpose(0, 2, 1), dirichlet.transpose(0, 3, 2, 1), geometry, permeability.T,
        mass_inv, div_map, trace_map, interleaved,
    )
    vectors, scales = solve(sizes, diagonals, lmat, forcing)
    traces, flux = recover(vectors, scales, hmat, forcing)
    return (
        traces.reshape(BX, BY, PRESS, BZ, COLS).transpose(0, 1, 3, 2, 4),
        flux.reshape(BX, BY, FLUX, BZ, COLS).transpose(0, 1, 3, 2, 4),
    )


def solution(mesh):
    sizes = (mesh.shape["gx"], mesh.shape["gy"], mesh.shape["gz"])
    placed = (
        P("gx", "gy", "gz", None, None),
        P("gx", "gy", "gz", None),
        P("gx", "gy", "gz"),
        P(),
        P(),
        P(),
        P(),
        P("gx", "gy", "gz", None),
    )
    return jax.shard_map(
        functools.partial(body, sizes),
        mesh=mesh,
        in_specs=placed,
        out_specs=(P("gx", "gy", "gz", None, None), P("gx", "gy", "gz", None, None)),
        check_vma=False,
    )
```

```python
import functools

import jax
import jax.numpy as jnp
from jax import lax
from jax.experimental import pallas as pl
from jax.experimental.pallas import tpu as pltpu
from jax.sharding import PartitionSpec as P

MESH = pl.DeviceIdType.MESH
BF16 = jnp.bfloat16
F32 = jnp.float32

COLS = 128
PRESS = 27
FLUX = 108
BX, BY, BZ = 2, 8, 4
ELEMENTS = BX * BY * BZ

TR = 64
PR = 32
FR = 112
AR = TR + FR

GROUP = 72
Z_GROUP = 40
Y_START = 12 * GROUP
Z_START = Y_START + 9 * GROUP
FIELD = Z_START + 20 * Z_GROUP

BLOCKED = 1e30
MIB = 1024 * 1024

BATCH = 16

GRANT = 62 * MIB


def lanes_of(shape):
    return lax.broadcasted_iota(jnp.int32, shape, len(shape) - 1)


def rows_of(shape):
    return lax.broadcasted_iota(jnp.int32, shape, len(shape) - 2)


def halves(value):
    high = value.astype(BF16)
    return high, (value - high.astype(F32)).astype(BF16)


def packed_pair(value):
    first, second = value[:, 0:128], value[:, 128:256]
    lane = lanes_of(second.shape)
    kept = (lane >= TR) & (lane < TR + PR)
    return first, jnp.where(kept, second, second - second.astype(BF16).astype(F32)).astype(BF16)


def local_blocks(arguments, results, scratch, sems):
    sources_hbm, geometry_hbm, rock_hbm, permeability_hbm, mass_hbm, div_hbm, trace_hbm, dirichlet_hbm = arguments
    diagonals, highs, lows, duals, right = results
    (
        geometry, rock, permeability, mass_in, div_map, trace_map, dirichlet, sources,
        joined, joined_t, padded, scale_t, left_mass, left_joined,
        press, inverse, table, spread, columns, first, second, solved_in, work,
    ) = scratch
    loads = [
        pltpu.make_async_copy(source, target, sems.at[n])
        for n, (source, target) in enumerate(
            (
                (trace_hbm, trace_map),
                (div_hbm, div_map),
                (mass_hbm, mass_in),
                (permeability_hbm, permeability),
                (rock_hbm, rock),
                (geometry_hbm, geometry),
                (dirichlet_hbm, dirichlet),
                (sources_hbm, sources),
            )
        )
    ]
    for item in loads:
        item.start()
    joined[...] = jnp.zeros_like(joined)
    padded[...] = jnp.zeros_like(padded)
    inverse[...] = jnp.zeros_like(inverse)
    for item in loads[:4]:
        item.wait()

    for facet in range(6):
        joined[8 * facet : 8 * facet + 8, 0:FLUX] = trace_map[9 * facet : 9 * facet + 8, :]
        joined[48 + facet : 49 + facet, 0:FLUX] = trace_map[9 * facet + 8 : 9 * facet + 9, :]
    joined[TR : TR + PRESS, 0:FLUX] = div_map[...]
    joined[TR + PR : TR + PR + PRESS, 0:FLUX] = div_map[...]
    joined_t[...] = jnp.transpose(joined[...])
    high, low = halves(joined[0 : TR + PR, :])
    left_joined[:, 0:128] = high
    left_joined[:, 128:256] = high
    left_joined[:, 256:384] = low
    padded[0:FLUX, 0:FLUX] = mass_in[...]
    high, low = halves(padded[0:FR, :])
    left_mass[:, 0:128] = high
    left_mass[:, 128:256] = high
    left_mass[:, 256:384] = low

    padded[...] = jnp.zeros_like(padded)
    padded[0:3, 0:16] = jnp.sqrt(permeability[...])
    rooted = jnp.transpose(padded[...])[0:16]
    lane = lanes_of((16, 128))
    table[0:16, :] = jnp.where(
        lane < 36, rooted[:, 0:1], jnp.where(lane < 72, rooted[:, 1:2], rooted[:, 2:3])
    )
    padded[...] = jnp.zeros_like(padded)
    loads[4].wait()
    loads[5].wait()
    for e in range(ELEMENTS):
        i, j, k = e // 32, (e // 4) % 8, e % 4
        row = table[pl.ds(rock[i, k, j], 1), :][:, 0:FLUX]
        padded[e : e + 1, 0:FLUX] = geometry[i, j, k : k + 1, :] * row
    scale_t[...] = jnp.transpose(padded[...])

    no_rows = jnp.zeros((128 - FR, 256), BF16)
    for pair in range(BATCH // 2):
        for part in range(3):
            first[pair, 128 * part + FR : 128 * part + 128, :] = no_rows
            second[pair, 128 * part + FR : 128 * part + 128, :] = no_rows

    on_diagonal = lanes_of((TR, 128)) == rows_of((TR, 128))

    @pl.loop(0, ELEMENTS // BATCH)
    def build(step):
        turned = pltpu.roll(scale_t[0:FR, :], lax.rem(128 - BATCH * step, 128), 1)
        for pair in range(BATCH // 2):
            for n in range(2):
                column = jnp.broadcast_to(turned[:, 2 * pair + n : 2 * pair + n + 1], (FR, 128))
                cut = slice(128 * n, 128 * n + 128)
                columns[pair, :, cut] = column
                high, low = halves(column * joined_t[0:FR, :])
                first[pair, 0:FR, cut] = high
                first[pair, 128 : 128 + FR, cut] = low
                first[pair, 256 : 256 + FR, cut] = high
        for pair in range(BATCH // 2):
            flux_side = columns[pair] * jnp.dot(left_mass[...], first[pair], preferred_element_type=F32)
            high, low = halves(flux_side)
            second[pair, 0:FR, :] = high
            second[pair, 128 : 128 + FR, :] = low
            second[pair, 256 : 256 + FR, :] = high
            for n in range(2):
                e = step * BATCH + 2 * pair + n
                cut = slice(128 * n, 128 * n + 128)
                highs[e, TR:AR, :] = high[:, cut]
                lows[e, TR:AR, :] = low[:, cut]
        for pair in range(BATCH // 2):
            coupled = jnp.dot(left_joined[...], second[pair], preferred_element_type=F32)
            high, low = halves(coupled[0:TR])
            for n in range(2):
                e = step * BATCH + 2 * pair + n
                cut = slice(128 * n, 128 * n + 128)
                highs[e, 0:TR, :] = high[:, cut]
                lows[e, 0:TR, :] = low[:, cut]
                diagonals[pl.ds(e, 1), :] = jnp.sum(
                    jnp.where(on_diagonal, coupled[0:TR, cut], 0.0), axis=0, keepdims=True
                )
                press[pl.ds(pl.multiple_of(e * PR, PR), PR), :] = coupled[TR:, cut]

    low_half = lanes_of((PR, 128)) < 64
    row_of = rows_of((PR, 128))

    for pair in range(14):
        rows = [press[pl.ds(2 * pair + n, ELEMENTS, stride=PR), :] for n in range(2)]
        work[pair] = jnp.transpose(jnp.concatenate(rows, axis=0))[TR : TR + PR, :]

    for k in range(PRESS):
        owner, ahead = k // 2, (k + 1) // 2 % 14
        mine = row_of == k
        held = low_half if k % 2 == 0 else jnp.logical_not(low_half)
        source = work[owner]
        source = jnp.where(held, source, pltpu.roll(source, 64, 1))
        row = jnp.where(mine, 1.0, source) * (1.0 / source[k : k + 1, :])
        for pair in [ahead] + [p for p in range(14) if p != ahead]:
            value = work[pair]
            value = jnp.where(mine, 0.0, value) - value[k : k + 1, :] * row
            work[pair] = jnp.where(held, row, value) if pair == owner else value

    for pair in range(14):
        placed = jnp.concatenate(
            [work[pair], jnp.zeros((PR, 128), F32), work[pair], work[pair]], axis=0
        )
        turned = jnp.transpose(placed)
        inverse[pl.ds(2 * pair, ELEMENTS, stride=PR), :] = turned[0:ELEMENTS]
        inverse[pl.ds(2 * pair + 1, ELEMENTS, stride=PR), :] = turned[ELEMENTS:]


    lane = lanes_of((TR, 256))
    unit = jnp.where((jnp.bitwise_and(lane, 63) == rows_of((TR, 256))) & (lane < 192), 1.0, 0.0)
    unit = unit.astype(BF16)
    for u in range(BATCH):
        solved_in[u, PR:TR, :] = jnp.zeros((PR, 128), BF16)
        right[u, 0:64, :] = unit
        right[u, 128:192, :] = unit
        right[u, 224:256, :] = jnp.zeros((PR, 256), BF16)
    lane = lanes_of((PR, 128))
    line = lanes_of((1, 128))
    x_lanes = (line < 8) | (line == 48)
    y_lanes = ((line >= 8) & (line < 16)) | (line == 49)
    z_lanes = ((line >= 16) & (line < 24)) | (line == 50)

    @pl.loop(0, ELEMENTS // BATCH)
    def finish(step):
        for u in range(BATCH):
            e = step * BATCH + u
            high, low = halves(press[pl.ds(pl.multiple_of(e * PR, PR), PR), :])
            solved_in[u, 0:PR, :] = low
            solved_in[u, TR : TR + PR, :] = high
            solved_in[u, TR + PR :, :] = high
        for u in range(BATCH):
            e = step * BATCH + u
            inv = inverse[pl.ds(pl.multiple_of(e * PR, PR), PR), :]
            left = jnp.where(lane < TR + PR, inv, inv - inv.astype(BF16).astype(F32)).astype(BF16)
            solved = jnp.dot(left, solved_in[u], preferred_element_type=F32)
            taken = press[pl.ds(pl.multiple_of(e * PR, PR), PR), :] * solved
            diagonals[pl.ds(e, 1), :] = diagonals[pl.ds(e, 1), :] - jnp.sum(taken, axis=0, keepdims=True)
            for part, other in enumerate((pltpu.roll(solved, TR, 1), inv)):
                high, low = halves(-jnp.where(lane < TR, solved, other))
                cut = slice(128 * part, 128 * part + 128)
                duals[e, 0:PR, cut] = high
                duals[e, PR:TR, cut] = low

    loads[6].wait()
    for e in range(ELEMENTS):
        i, j, k = e // 32, (e // 4) % 8, e % 4
        lift = [dirichlet[i, normal, k, j].astype(F32) * BLOCKED for normal in range(3)]
        diagonals[e : e + 1, :] = diagonals[e : e + 1, :] + jnp.where(
            x_lanes, lift[0], jnp.where(y_lanes, lift[1], jnp.where(z_lanes, lift[2], 0.0))
        )

    return loads[7]


def spread_forcing(sources, spread, forcing):
    for part in range(4):
        spread[...] = sources[432 * part : 432 * part + 432, :].astype(F32)
        for jj in range(4):
            for k in range(BZ):
                e = part * 16 + jj * 4 + k
                values = spread[pl.ds(108 * jj + k, PRESS, stride=4), :]
                values = jnp.concatenate([values, jnp.zeros((PR - PRESS, COLS), F32)], axis=0)
                forcing[e] = values.astype(BF16)


def facet_rows(g, i, jj, k):
    places = []
    for side in range(2):
        for start, size, slot in (
            (((i + side) * 4 + g) * GROUP, 64, jj * 4 + k),
            (Y_START + (2 * g + jj + side) * GROUP, 64, i * 4 + k),
            (Z_START + ((k + side) * 4 + g) * Z_GROUP, 32, i * 2 + jj),
        ):
            places.append((pl.multiple_of(start + slot * 8, 8), start + size + slot))
    return places


def gathered(field, places):
    row = rows_of((8, COLS))
    ninth = jnp.zeros((8, COLS), F32)
    pieces = []
    for facet, (main, extra) in enumerate(places):
        pieces.append(field[pl.ds(main, 8), :])
        line = jnp.broadcast_to(field[pl.ds(extra, 1), :], (8, COLS))
        ninth = jnp.where(row == facet, line, ninth)
    return pieces + [ninth]


def scatter(values, low, up, places):
    for facet, (main, extra) in enumerate(places):
        target = low if facet < 3 else up
        target[pl.ds(main, 8), :] = values[8 * facet : 8 * facet + 8]
        target[pl.ds(extra, 1), :] = values[48 + facet : 49 + facet]


EACH = [(i, jj, k) for i in range(BX) for jj in range(2) for k in range(BZ)]


def element_index(g, i, jj, k):
    return i * 32 + g * 8 + jj * 4 + k


def solver_kernel(sizes, *refs):
    arguments, (lam_hbm, hmat_hbm, forcing_hbm) = refs[:8], refs[8:11]
    (
        lmat, hmat, forcing, diagonals, highs, lows, duals, right,
        low, up, inverse, fields, vectors, weights, lam, near, turned, mine, parts_a, parts_b,
        load_sems, out_sems, send, recv, send_y, recv_y, send_d, recv_d, send_sum, recv_sum,
    ) = refs[11:41]
    local_scratch = refs[41:]
    nx, ny, nz = sizes
    ix, iy, iz = lax.axis_index("gx"), lax.axis_index("gy"), lax.axis_index("gz")

    def at_x(step):
        return (lax.rem(ix + step + nx, nx), iy, iz)

    def at_y(step):
        return (ix, lax.rem(iy + step + ny, ny), iz)

    def at_z(step):
        return (ix, iy, lax.rem(iz + step + nz, nz))

    def at_xy(a, b):
        return (lax.rem(ix + a, nx), lax.rem(iy + b, ny), iz)

    rings = [
        [at_xy(a, b) for a in range(nx) for b in range(ny) if (a, b) != (0, 0)],
        [at_z(s) for s in range(1, nz)],
    ]
    partners = rings[0] + rings[1]
    barrier = pltpu.get_barrier_semaphore()
    for partner in partners:
        pl.semaphore_signal(barrier, inc=1, device_id=partner, device_id_type=MESH)

    zero = jnp.zeros((8, COLS), F32)
    for u in range(len(EACH)):
        weights[u, 3 * TR : 4 * TR, :] = jnp.zeros((TR, COLS), BF16)

    @pl.loop(0, 16)
    def clear(group):
        for stage in range(3):
            start = Z_START + 32 + group * Z_GROUP
            low[stage, pl.ds(pl.multiple_of(start, 8), 8), :] = zero
            up[stage, pl.ds(pl.multiple_of(start + 4 * Z_GROUP, 8), 8), :] = zero

    @pl.loop(0, 20)
    def clear_inverse(group):
        inverse[pl.ds(pl.multiple_of(Z_START + 32 + group * Z_GROUP, 8), 8), :] = zero

    def remote(source, target, sent, received, device):
        return pltpu.make_async_remote_copy(
            src_ref=source, dst_ref=target, send_sem=sent, recv_sem=received,
            device_id=device, device_id_type=MESH,
        )

    def field_copy(buffer, stage, source, target, count, sent, received, device):
        return remote(
            buffer.at[stage, pl.ds(pl.multiple_of(source, 8), count)],
            buffer.at[stage, pl.ds(pl.multiple_of(target, 8), count)],
            sent, received, device,
        )

    def copies_xz(stage, g):
        x, z = g * GROUP, Z_START + g * Z_GROUP
        x_last, z_last = x + 8 * GROUP, z + 16 * Z_GROUP
        return [
            field_copy(low, stage, x, x_last, GROUP, send.at[stage, 0, g], recv.at[stage, 0, g], at_x(-1)),
            field_copy(up, stage, x_last, x, GROUP, send.at[stage, 1, g], recv.at[stage, 1, g], at_x(1)),
            field_copy(low, stage, z, z_last, Z_GROUP, send.at[stage, 2, g], recv.at[stage, 2, g], at_z(-1)),
            field_copy(up, stage, z_last, z, Z_GROUP, send.at[stage, 3, g], recv.at[stage, 3, g], at_z(1)),
        ]

    def copy_y(stage, side):
        first, last = Y_START, Y_START + 8 * GROUP
        if side == 0:
            return field_copy(low, stage, first, last, GROUP, send_y.at[stage, 0], recv_y.at[stage, 0], at_y(-1))
        return field_copy(up, stage, last, first, GROUP, send_y.at[stage, 1], recv_y.at[stage, 1], at_y(1))

    sources_load = local_blocks(
        arguments, (diagonals, highs, lows, duals, right), local_scratch, load_sems
    )
    pl.semaphore_wait(barrier, len(partners))

    half = ELEMENTS // 2
    near_copies = [
        remote(diagonals.at[pl.ds(half, half)], near.at[0, pl.ds(0, half)], send_d.at[0], recv_d.at[0], at_x(1)),
        remote(diagonals.at[pl.ds(0, half)], near.at[1, pl.ds(0, half)], send_d.at[1], recv_d.at[1], at_x(-1)),
        remote(diagonals, near.at[2], send_d.at[2], recv_d.at[2], at_y(1)),
        remote(diagonals, near.at[3], send_d.at[3], recv_d.at[3], at_y(-1)),
        remote(diagonals, near.at[4], send_d.at[4], recv_d.at[4], at_z(1)),
        remote(diagonals, near.at[5], send_d.at[5], recv_d.at[5], at_z(-1)),
    ]
    for item in near_copies:
        item.start()

    def order(n):
        return lax.rem(3 * n, 4)

    def send_chunk(stage, n):
        for item in copies_xz(stage, order(n)):
            item.start()
        for side in range(2):
            @pl.when(n == side)
            def _():
                copy_y(stage, side).start()

    sources_load.wait()
    spread_forcing(local_scratch[7], local_scratch[17], forcing)
    out_copies = [pltpu.make_async_copy(forcing, forcing_hbm, out_sems.at[0])]
    out_copies[0].start()

    def fill_right(u, e):
        right[u, 64:96, :] = duals[e, 0:PR, :]
        right[u, 96:128, :] = duals[e, PR:TR, :]
        right[u, 192:224, :] = duals[e, 0:PR, :]

    @pl.loop(0, 4)
    def start(n):
        g = order(n)
        for u, (i, jj, k) in enumerate(EACH):
            fill_right(u, element_index(g, i, jj, k))
        for u, (i, jj, k) in enumerate(EACH):
            e = element_index(g, i, jj, k)
            left = jnp.concatenate([highs[e, 0:TR, :], lows[e, 0:TR, :]], axis=1)
            both, rest = packed_pair(jnp.dot(left, right[u], preferred_element_type=F32))
            lmat[e, :, 0:128] = both.astype(BF16)
            lmat[e, :, 128:256] = rest
        for i, jj, k in EACH:
            e = element_index(g, i, jj, k)
            given = jnp.concatenate([jnp.zeros((TR, COLS), BF16), forcing[e], forcing[e]], axis=0)
            values = -jnp.dot(lmat[e, :, 128:256], given, preferred_element_type=F32)
            scatter(values, low.at[0], up.at[0], facet_rows(g, i, jj, k))
        send_chunk(0, n)

    for item in near_copies:
        item.wait()
    lane, row = lanes_of((ELEMENTS, 128)), rows_of((ELEMENTS, 128))
    x_lanes = (lane < 8) | (lane == 48)
    y_lanes = ((lane >= 8) & (lane < 16)) | (lane == 49)

    def uppers(value):
        return jnp.where(lane < 24, pltpu.roll(value, 104, 1), pltpu.roll(value, 125, 1))

    def reciprocal(total):
        return jnp.where(total > 0.5 * BLOCKED, 0.0, 1.0 / total)

    own = diagonals[...]
    own_up = uppers(own)
    from_x = jnp.concatenate([uppers(near[0])[0:half], own_up[0:half]], axis=0)
    first_y, first_z = jnp.bitwise_and(row, 31) < 4, jnp.bitwise_and(row, 3) == 0
    from_y = jnp.where(first_y, pltpu.roll(uppers(near[2]), 36, 0), pltpu.roll(own_up, 4, 0))
    from_z = jnp.where(first_z, pltpu.roll(uppers(near[4]), 61, 0), pltpu.roll(own_up, 1, 0))
    lower_sum = own + jnp.where(x_lanes, from_x, jnp.where(y_lanes, from_y, from_z))
    above_x = jnp.concatenate([near[1, 0:half, :], near[1, 0:half, :]], axis=0)
    above_y, above_z = pltpu.roll(near[3], 28, 0), pltpu.roll(near[5], 3, 0)
    upper_sum = own_up + jnp.where(x_lanes, above_x, jnp.where(y_lanes, above_y, above_z))
    flipped = jnp.transpose(jnp.concatenate([reciprocal(lower_sum), reciprocal(upper_sum)], axis=0))
    turned[0:24, :] = flipped[0:24]
    turned[24:32, :] = flipped[48:56]

    @pl.loop(0, 4)
    def expand(g):
        rolled = pltpu.roll(turned[...], lax.rem(128 - 8 * g, 128), 1)
        for i, jj, k in EACH:
            column = i * 32 + jj * 4 + k
            places = facet_rows(g, i, jj, k)
            for side in range(2):
                normals = [0, 1, 2] if side == 0 else [n for n, last in enumerate((i == 1, jj == 1, k == 3)) if last]
                if not normals:
                    continue
                at = 64 * side + column
                ninth = jnp.broadcast_to(rolled[24:32, at : at + 1], (8, COLS))
                for normal in normals:
                    main, extra = places[3 * side + normal]
                    inverse[pl.ds(main, 8), :] = jnp.broadcast_to(
                        rolled[8 * normal : 8 * normal + 8, at : at + 1], (8, COLS)
                    )
                    inverse[pl.ds(extra, 1), :] = ninth[normal : normal + 1]

    def update(step, g, total):
        spans = [((plane * 4 + g) * GROUP, 9, plane < 2) for plane in range(3)]
        spans += [(Y_START + (2 * g + plane) * GROUP, 9, plane < 2) for plane in range(3)]
        spans += [(Z_START + (plane * 4 + g) * Z_GROUP, 5, plane < 4) for plane in range(5)]
        for begin, tiles, owned in spans:
            for tile in range(tiles):
                place = pl.ds(pl.multiple_of(begin + tile * 8, 8), 8)
                value = low[step, place, :] + up[step, place, :]
                scaled = inverse[place, :] * value
                if step == 0:
                    fields[0, place, :] = scaled
                    if owned:
                        total = total + value * scaled
                else:
                    fields[step, place, :] = scaled - fields[step - 1, place, :]
        return total

    def operate(step, n, totals):
        g = order(n)
        totals = list(totals)
        for item in copies_xz(step, g):
            item.wait_recv()
        for side in range(2):
            @pl.when(n == 1 - side)
            def _():
                copy_y(step, side).wait_recv()
        totals[0] = update(step, g, totals[0])
        for u, (i, jj, k) in enumerate(EACH):
            pieces = gathered(fields.at[step], facet_rows(g, i, jj, k))
            vector = jnp.concatenate(pieces + [jnp.zeros((8, COLS), F32)], axis=0)
            vectors[step, element_index(g, i, jj, k)] = vector
            high, low_part = halves(vector)
            weights[u, 0:TR, :] = high
            weights[u, TR : 2 * TR, :] = low_part
            weights[u, 2 * TR : 3 * TR, :] = high
        for u, (i, jj, k) in enumerate(EACH):
            e = element_index(g, i, jj, k)
            values = jnp.dot(lmat[e], weights[u], preferred_element_type=F32)
            for which in range(1 if step == 0 else 2):
                products = vectors[step - which, e] * values
                parts = [products[8 * tile : 8 * tile + 8] for tile in range(7)]
                part = (parts[0] + parts[1]) + (parts[2] + parts[3])
                part = part + ((parts[4] + parts[5]) + parts[6])
                totals[1 + which] = totals[1 + which] + part
            if step < 2:
                scatter(values, low.at[step + 1], up.at[step + 1], facet_rows(g, i, jj, k))
        if step < 2:
            send_chunk(step + 1, n)
        return tuple(totals)

    moments = []
    for step in range(3):
        totals = lax.fori_loop(0, 4, functools.partial(operate, step), (zero,) * 3)
        moments += [totals[:2], totals[1:], totals[1:]][step]

    sublane = rows_of((8, COLS))
    tile = zero
    for which, moment in enumerate(moments):
        line = jnp.broadcast_to(jnp.sum(moment, axis=0, keepdims=True), (8, COLS))
        tile = jnp.where(sublane == which, line, tile)

    def recovery(batch):
        for u in range(BATCH):
            e = batch * BATCH + u
            fill_right(u, e)
        for u in range(BATCH):
            e = batch * BATCH + u
            left = jnp.concatenate([highs[e, TR:AR, :], lows[e, TR:AR, :]], axis=1)
            both, rest = packed_pair(jnp.dot(left, right[u], preferred_element_type=F32))
            hmat[e, :, 0:128] = both.astype(BF16)
            hmat[e, :, 128:256] = rest

    batches = ELEMENTS // BATCH
    for stage, (ring, parts) in enumerate(zip(rings, (parts_a, parts_b))):
        mine[stage] = tile
        for n, partner in enumerate(ring):
            remote(mine.at[stage], parts.at[n], send_sum.at[stage], recv_sum.at[stage], partner).start()
        span = (0, batches // 2) if stage == 0 else (batches // 2, batches)
        pl.loop(*span)(recovery)
        place = pl.ds(span[0] * BATCH, (span[1] - span[0]) * BATCH)
        out_copies.append(pltpu.make_async_copy(hmat.at[place], hmat_hbm.at[place], out_sems.at[1 + stage]))
        out_copies[-1].start()
        pltpu.make_async_copy(parts, parts, recv_sum.at[stage]).wait()
        terms = [tile] + [parts[n] for n in range(len(ring))]
        while len(terms) > 1:
            terms = [sum(terms[n : n + 2][1:], terms[n]) for n in range(0, len(terms), 2)]
        tile = terms[0]
        pltpu.make_async_copy(parts, parts, send_sum.at[stage]).wait()

    b0, g00, g11, g01, g22, g12 = [tile[n : n + 1] for n in range(6)]
    b1 = g00 - b0
    b2 = g01 - b1
    g02 = g11
    l1, l2 = g01 / g00, g02 / g00
    h11, h12, h22 = g11 - l1 * g01, g12 - l1 * g02, g22 - l2 * g02
    d1, d2 = b1 - l1 * b0, b2 - l2 * b0
    sound = h11 > 2e-6 * g11
    m = jnp.where(sound, h12 / h11, 0.0)
    k22 = h22 - m * h12
    c2 = jnp.where(k22 > 2e-6 * g22, (d2 - m * d1) / k22, 0.0)
    c1 = jnp.where(sound, (d1 - h12 * c2) / h11, 0.0)
    c0 = (b0 - g01 * c1 - g02 * c2) / g00
    c0, c1, c2 = [jnp.broadcast_to(c, (8, COLS)) for c in (c0, c1, c2)]

    for part in range(2):
        @pl.loop(32 * part, 32 * part + 32)
        def combine(e):
            for tile in range(7):
                place = slice(8 * tile, 8 * tile + 8)
                lam[e, place, :] = (
                    c0 * vectors[0, e, place, :] + c1 * vectors[1, e, place, :] + c2 * vectors[2, e, place, :]
                )

        place = pl.ds(32 * part, 32)
        out_copies.append(pltpu.make_async_copy(lam.at[place], lam_hbm.at[place], out_sems.at[3 + part]))
        out_copies[-1].start()

    @pl.loop(0, 4)
    def drain(g):
        for stage in range(3):
            for item in copies_xz(stage, g):
                item.wait_send()

    for stage in range(3):
        for side in range(2):
            copy_y(stage, side).wait_send()


    for item in out_copies:
        item.wait()


def solve(sizes, *arguments):
    hbm = pl.BlockSpec(memory_space=pltpu.HBM)
    _, geometry, rock, permeability, mass_inv, div_map, trace_map, dirichlet = arguments
    dma = pltpu.SemaphoreType.DMA
    return pl.pallas_call(
        functools.partial(solver_kernel, sizes),
        out_shape=(
            jax.ShapeDtypeStruct((ELEMENTS, 56, COLS), F32),
            jax.ShapeDtypeStruct((ELEMENTS, FR, 256), BF16),
            jax.ShapeDtypeStruct((ELEMENTS, PR, COLS), BF16),
        ),
        in_specs=[hbm] * 8,
        out_specs=[hbm] * 3,
        scratch_shapes=[
            pltpu.VMEM((ELEMENTS, TR, 256), BF16),
            pltpu.VMEM((ELEMENTS, FR, 256), BF16),
            pltpu.VMEM((ELEMENTS, PR, COLS), BF16),
            pltpu.VMEM((ELEMENTS, 128), F32),
            pltpu.VMEM((ELEMENTS, AR, 128), BF16),
            pltpu.VMEM((ELEMENTS, AR, 128), BF16),
            pltpu.VMEM((ELEMENTS, TR, 256), BF16),
            pltpu.VMEM((BATCH, 256, 256), BF16),
            pltpu.VMEM((3, FIELD, COLS), F32),
            pltpu.VMEM((3, FIELD, COLS), F32),
            pltpu.VMEM((FIELD, COLS), F32),
            pltpu.VMEM((3, FIELD, COLS), F32),
            pltpu.VMEM((3, ELEMENTS, TR, COLS), F32),
            pltpu.VMEM((len(EACH), 256, COLS), BF16),
            pltpu.VMEM((ELEMENTS, 56, COLS), F32),
            pltpu.VMEM((6, ELEMENTS, 128), F32),
            pltpu.VMEM((32, 128), F32),
            pltpu.VMEM((2, 8, COLS), F32),
            pltpu.VMEM((sizes[0] * sizes[1] - 1, 8, COLS), F32),
            pltpu.VMEM((sizes[2] - 1, 8, COLS), F32),
            dma((8,)), dma((5,)),
            dma((3, 4, 4)), dma((3, 4, 4)), dma((3, 2)), dma((3, 2)), dma((6,)), dma((6,)), dma((2,)), dma((2,)),
            pltpu.VMEM(geometry.shape, F32),
            pltpu.SMEM(rock.shape, jnp.int32),
            pltpu.VMEM(permeability.shape, F32),
            pltpu.VMEM(mass_inv.shape, F32),
            pltpu.VMEM(div_map.shape, F32),
            pltpu.VMEM(trace_map.shape, F32),
            pltpu.SMEM(dirichlet.shape, jnp.int32),
            pltpu.VMEM((ELEMENTS * PRESS, COLS), BF16),
            pltpu.VMEM((128, 128), F32),
            pltpu.VMEM((128, 128), F32),
            pltpu.VMEM((128, 128), F32),
            pltpu.VMEM((128, 128), F32),
            pltpu.VMEM((FR, 384), BF16),
            pltpu.VMEM((TR + PR, 384), BF16),
            pltpu.VMEM((ELEMENTS * PR, 128), F32),
            pltpu.VMEM((ELEMENTS * PR, 128), F32),
            pltpu.VMEM((16, 128), F32),
            pltpu.VMEM((432, 128), F32),
            pltpu.VMEM((BATCH // 2, FR, 256), F32),
            pltpu.VMEM((BATCH // 2, 384, 256), BF16),
            pltpu.VMEM((BATCH // 2, 384, 256), BF16),
            pltpu.VMEM((BATCH, 128, 128), BF16),
            pltpu.VMEM((14, PR, 128), F32),
        ],
        compiler_params=pltpu.CompilerParams(
            collective_id=0, has_side_effects=True, vmem_limit_bytes=GRANT
        ),
        name="solver",
    )(*arguments)


def recover_kernel(lam_hbm, hmat_hbm, forcing_hbm, traces_hbm, flux_hbm,
                   lam, hmat, forcing, traces, flux, weights, spread, load_sems, out_sems):
    pitch = 5
    first = rows_of((8, COLS)) < 4
    parts = ELEMENTS // BATCH
    rows_t, rows_f = BATCH * PRESS, BATCH * FLUX

    def loads(n):
        place = pl.ds(n * BATCH, BATCH)
        return [
            pltpu.make_async_copy(source.at[place], target.at[place], load_sems.at[n, which])
            for which, (source, target) in enumerate(
                ((lam_hbm, lam), (hmat_hbm, hmat), (forcing_hbm, forcing))
            )
        ]

    def stores(n):
        return [
            pltpu.make_async_copy(
                source.at[pl.ds(n * rows, rows)], target.at[pl.ds(n * rows, rows)], out_sems.at[n, which]
            )
            for which, (source, target, rows) in enumerate(
                ((traces, traces_hbm, rows_t), (flux, flux_hbm, rows_f))
            )
        ]

    for n in range(parts):
        for item in loads(n):
            item.start()

    @pl.loop(0, parts)
    def part(n):
        for item in loads(n):
            item.wait()
        for u in range(BATCH):
            e = n * BATCH + u
            tiles = [lam[e, 8 * tile : 8 * tile + 8, :] for tile in range(7)]
            start = n * rows_t + 108 * (u // 4) + u % 4
            for normal in range(3):
                traces[pl.ds(start + 36 * normal, 8, stride=4), :] = tiles[normal]
                traces[pl.ds(start + 36 * normal + 32, 1), :] = tiles[6][normal : normal + 1]
            high, low = halves(jnp.concatenate(tiles + [jnp.zeros((8, COLS), F32)], axis=0))
            weights[u, 0:TR, :] = high
            weights[u, TR : 2 * TR, :] = low
            weights[u, 2 * TR : 3 * TR, :] = high
            weights[u, 3 * TR : 3 * TR + PR, :] = forcing[e]
            weights[u, 3 * TR + PR :, :] = forcing[e]
        for u in range(BATCH):
            values = jnp.dot(hmat[n * BATCH + u], weights[u], preferred_element_type=F32)
            spread[pl.ds(FLUX * pitch * (u // 4) + u % 4, FLUX, stride=pitch), :] = -values[0:FLUX]
        for quad in range(BATCH * FLUX // 16):
            tiles = []
            for half in range(2):
                at = pitch * (4 * quad + 2 * half)
                tiles.append(jnp.where(first, spread[at : at + 8, :], spread[at + 1 : at + 9, :]))
            place = pl.ds(pl.multiple_of(n * rows_f + 16 * quad, 16), 16)
            flux[place, :] = jnp.concatenate(tiles, axis=0).astype(BF16)
        for item in stores(n):
            item.start()

    for n in range(parts):
        for item in stores(n):
            item.wait()


def recover(lam, hmat, forcing):
    hbm = pl.BlockSpec(memory_space=pltpu.HBM)
    out_shape = (
        jax.ShapeDtypeStruct((ELEMENTS * PRESS, COLS), F32),
        jax.ShapeDtypeStruct((ELEMENTS * FLUX, COLS), BF16),
    )
    return pl.pallas_call(
        recover_kernel,
        out_shape=out_shape,
        in_specs=[hbm] * 3,
        out_specs=[hbm] * 2,
        scratch_shapes=[
            pltpu.VMEM(item.shape, item.dtype) for item in (lam, hmat, forcing) + out_shape
        ] + [
            pltpu.VMEM((BATCH, 256, COLS), BF16),
            pltpu.VMEM((5 * BATCH * FLUX // 4 + 8, COLS), F32),
            pltpu.SemaphoreType.DMA((ELEMENTS // BATCH, 3)),
            pltpu.SemaphoreType.DMA((ELEMENTS // BATCH, 2)),
        ],
        compiler_params=pltpu.CompilerParams(vmem_limit_bytes=GRANT),
        name="recover",
    )(lam, hmat, forcing)


def body(sizes, sources, geometry, rock_class, permeability, mass_inv, div_map, trace_map, dirichlet):
    interleaved = sources.transpose(0, 1, 3, 2, 4).reshape(ELEMENTS * PRESS, COLS)
    lam, hmat, forcing = solve(
        sizes, interleaved, geometry, rock_class.transpose(0, 2, 1), permeability.T,
        mass_inv, div_map, trace_map, dirichlet.transpose(0, 3, 2, 1),
    )
    traces, flux = recover(lam, hmat, forcing)
    return (
        traces.reshape(BX, BY, PRESS, BZ, COLS).transpose(0, 1, 3, 2, 4),
        flux.reshape(BX, BY, FLUX, BZ, COLS).transpose(0, 1, 3, 2, 4),
    )


def solution(mesh):
    sizes = (mesh.shape["gx"], mesh.shape["gy"], mesh.shape["gz"])
    placed = (
        P("gx", "gy", "gz", None, None),
        P("gx", "gy", "gz", None),
        P("gx", "gy", "gz"),
        P(),
        P(),
        P(),
        P(),
        P("gx", "gy", "gz", None),
    )
    return jax.shard_map(
        functools.partial(body, sizes),
        mesh=mesh,
        in_specs=placed,
        out_specs=(P("gx", "gy", "gz", None, None), P("gx", "gy", "gz", None, None)),
        check_vma=False,
    )
```

```python
import functools

import jax
import jax.numpy as jnp
from jax import lax
from jax.experimental import pallas as pl
from jax.experimental.pallas import tpu as pltpu
from jax.sharding import PartitionSpec as P

MESH = pl.DeviceIdType.MESH
BF16 = jnp.bfloat16
F32 = jnp.float32

COLS = 128
PRESS = 27
FLUX = 108
BX, BY, BZ = 2, 8, 4
ELEMENTS = BX * BY * BZ

TR = 64
PR = 32
FR = 112
AR = TR + FR

GROUP = 72
Z_GROUP = 40
Y_START = 12 * GROUP
Z_START = Y_START + 9 * GROUP
FIELD = Z_START + 20 * Z_GROUP

BLOCKED = 1e30
MIB = 1024 * 1024

BATCH = 16
WIDE = 32

GRANT = 62 * MIB


def lanes_of(shape):
    return lax.broadcasted_iota(jnp.int32, shape, len(shape) - 1)


def rows_of(shape):
    return lax.broadcasted_iota(jnp.int32, shape, len(shape) - 2)


def halves(value):
    high = value.astype(BF16)
    return high, (value - high.astype(F32)).astype(BF16)


def packed_pair(value):
    first, second = value[:, 0:128], value[:, 128:256]
    lane = lanes_of(second.shape)
    kept = (lane >= TR) & (lane < TR + PR)
    return first, jnp.where(kept, second, second - second.astype(BF16).astype(F32)).astype(BF16)


def operand_loads(arguments, scratch, sems):
    sources_hbm, geometry_hbm, rock_hbm, permeability_hbm, mass_hbm, div_hbm, trace_hbm, dirichlet_hbm = arguments
    geometry, rock, permeability, mass_in, div_map, trace_map, dirichlet, sources = scratch[:8]
    loads = [
        pltpu.make_async_copy(source, target, sems.at[n])
        for n, (source, target) in enumerate(
            (
                (trace_hbm, trace_map),
                (div_hbm, div_map),
                (mass_hbm, mass_in),
                (permeability_hbm, permeability),
                (rock_hbm, rock),
                (geometry_hbm, geometry),
                (dirichlet_hbm, dirichlet),
                (sources_hbm, sources),
            )
        )
    ]
    for item in loads:
        item.start()
    return loads


def local_blocks(loads, results, scratch):
    forcing, diagonals, highs, lows, duals, right = results
    (
        geometry, rock, permeability, mass_in, div_map, trace_map, dirichlet, sources, lifts,
        joined, joined_t, padded, scale_t, left_mass, left_joined,
        press, inverse, table, spread, columns, first, second, solved_in, work,
    ) = scratch
    joined[...] = jnp.zeros_like(joined)
    padded[...] = jnp.zeros_like(padded)
    inverse[...] = jnp.zeros_like(inverse)
    for item in loads[:4]:
        item.wait()

    for facet in range(6):
        joined[8 * facet : 8 * facet + 8, 0:FLUX] = trace_map[9 * facet : 9 * facet + 8, :]
        joined[48 + facet : 49 + facet, 0:FLUX] = trace_map[9 * facet + 8 : 9 * facet + 9, :]
    joined[TR : TR + PRESS, 0:FLUX] = div_map[...]
    joined[TR + PR : TR + PR + PRESS, 0:FLUX] = div_map[...]
    joined_t[...] = jnp.transpose(joined[...])
    high, low = halves(joined[0 : TR + PR, :])
    left_joined[:, 0:128] = high
    left_joined[:, 128:256] = high
    left_joined[:, 256:384] = low
    padded[0:FLUX, 0:FLUX] = mass_in[...]
    high, low = halves(padded[0:FR, :])
    left_mass[:, 0:128] = high
    left_mass[:, 128:256] = high
    left_mass[:, 256:384] = low

    padded[...] = jnp.zeros_like(padded)
    padded[0:3, 0:16] = jnp.sqrt(permeability[...])
    rooted = jnp.transpose(padded[...])[0:16]
    lane = lanes_of((16, 128))
    table[0:16, :] = jnp.where(
        lane < 36, rooted[:, 0:1], jnp.where(lane < 72, rooted[:, 1:2], rooted[:, 2:3])
    )
    padded[...] = jnp.zeros_like(padded)
    loads[4].wait()
    loads[5].wait()
    for e in range(ELEMENTS):
        i, j, k = e // 32, (e // 4) % 8, e % 4
        row = table[pl.ds(rock[i, k, j], 1), :][:, 0:FLUX]
        padded[e : e + 1, 0:FLUX] = geometry[i, j, k : k + 1, :] * row
    scale_t[...] = jnp.transpose(padded[...])

    no_rows = jnp.zeros((128 - FR, 256), BF16)
    for pair in range(WIDE // 2):
        for part in range(3):
            first[pair, 128 * part + FR : 128 * part + 128, :] = no_rows
            second[pair, 128 * part + FR : 128 * part + 128, :] = no_rows

    on_diagonal = lanes_of((TR, 128)) == rows_of((TR, 128))

    @pl.loop(0, ELEMENTS // WIDE)
    def build(step):
        turned = pltpu.roll(scale_t[0:FR, :], lax.rem(128 - WIDE * step, 128), 1)
        for pair in range(WIDE // 2):
            for n in range(2):
                column = jnp.broadcast_to(turned[:, 2 * pair + n : 2 * pair + n + 1], (FR, 128))
                cut = slice(128 * n, 128 * n + 128)
                columns[pair, :, cut] = column
                high, low = halves(column * joined_t[0:FR, :])
                first[pair, 0:FR, cut] = high
                first[pair, 128 : 128 + FR, cut] = low
                first[pair, 256 : 256 + FR, cut] = high
        for pair in range(WIDE // 2):
            flux_side = columns[pair] * jnp.dot(left_mass[...], first[pair], preferred_element_type=F32)
            high, low = halves(flux_side)
            second[pair, 0:FR, :] = high
            second[pair, 128 : 128 + FR, :] = low
            second[pair, 256 : 256 + FR, :] = high
            for n in range(2):
                e = step * WIDE + 2 * pair + n
                cut = slice(128 * n, 128 * n + 128)
                highs[e, TR:AR, :] = high[:, cut]
                lows[e, TR:AR, :] = low[:, cut]
        for pair in range(WIDE // 2):
            coupled = jnp.dot(left_joined[...], second[pair], preferred_element_type=F32)
            high, low = halves(coupled[0:TR])
            for n in range(2):
                e = step * WIDE + 2 * pair + n
                cut = slice(128 * n, 128 * n + 128)
                highs[e, 0:TR, :] = high[:, cut]
                lows[e, 0:TR, :] = low[:, cut]
                diagonals[pl.ds(e, 1), :] = jnp.sum(
                    jnp.where(on_diagonal, coupled[0:TR, cut], 0.0), axis=0, keepdims=True
                )
                press[pl.ds(pl.multiple_of(e * PR, PR), PR), :] = coupled[TR:, cut]

    low_half = lanes_of((PR, 128)) < 64
    row_of = rows_of((PR, 128))

    early = lanes_of((ELEMENTS, 128)) < TR + PR
    for quad in range(7):
        rows = [press[pl.ds(4 * quad + n, ELEMENTS, stride=PR), :] for n in range(4)]
        stacked = [jnp.where(early, rows[0], rows[2]), jnp.where(early, rows[1], rows[3])]
        flipped = jnp.transpose(jnp.concatenate(stacked, axis=0))
        work[2 * quad] = flipped[TR : TR + PR, :]
        work[2 * quad + 1] = flipped[TR + PR :, :]

    loads[6].wait()
    loads[7].wait()
    line = lanes_of((1, 128))
    x_lanes = (line < 8) | (line == 48)
    y_lanes = ((line >= 8) & (line < 16)) | (line == 49)
    z_lanes = ((line >= 16) & (line < 24)) | (line == 50)
    for part in range(4):
        spread[part] = sources[432 * part : 432 * part + 432, :].astype(F32)

    def beside(e):
        i, j, k = e // 32, (e // 4) % 8, e % 4
        values = spread[e // 16, pl.ds(108 * (j % 4) + k, PRESS, stride=4), :]
        values = jnp.concatenate([values, jnp.zeros((PR - PRESS, COLS), F32)], axis=0)
        forcing[e] = values.astype(BF16)
        lift = [dirichlet[i, normal, k, j].astype(F32) * BLOCKED for normal in range(3)]
        lifts[e : e + 1, :] = jnp.where(
            x_lanes, lift[0], jnp.where(y_lanes, lift[1], jnp.where(z_lanes, lift[2], 0.0))
        )

    for owner in range(13):
        k = 2 * owner
        mine, next_one = row_of == k, row_of == k + 1
        source = work[owner]
        other = pltpu.roll(source, 64, 1)
        one, two = jnp.where(low_half, source, other), jnp.where(low_half, other, source)
        a, b = one[k : k + 1, :], one[k + 1 : k + 2, :]
        c, d = two[k : k + 1, :], two[k + 1 : k + 2, :]
        scale = 1.0 / (a * d - b * c)
        one = jnp.where(mine, 1.0, jnp.where(next_one, 0.0, one))
        two = jnp.where(mine, 0.0, jnp.where(next_one, 1.0, two))
        row_one = (d * scale) * one - (b * scale) * two
        row_two = (a * scale) * two - (c * scale) * one
        both = mine | next_one
        for pair in [owner + 1] + [p for p in range(14) if p not in (owner, owner + 1)]:
            value = work[pair]
            rest = jnp.where(both, 0.0, value) - value[k : k + 1, :] * row_one
            work[pair] = rest - value[k + 1 : k + 2, :] * row_two
        work[owner] = jnp.where(low_half, row_one, row_two)
        for e in range(5 * owner, min(5 * owner + 5, ELEMENTS)):
            beside(e)

    k = PRESS - 1
    mine = row_of == k
    source = work[13]
    source = jnp.where(low_half, source, pltpu.roll(source, 64, 1))
    row = jnp.where(mine, 1.0, source) * (1.0 / source[k : k + 1, :])
    for pair in range(13):
        value = work[pair]
        work[pair] = jnp.where(mine, 0.0, value) - value[k : k + 1, :] * row
    work[13] = jnp.where(low_half, row, 0.0)

    for pair in range(14):
        placed = jnp.concatenate(
            [work[pair], jnp.zeros((PR, 128), F32), work[pair], work[pair]], axis=0
        )
        turned = jnp.transpose(placed)
        inverse[pl.ds(2 * pair, ELEMENTS, stride=PR), :] = turned[0:ELEMENTS]
        inverse[pl.ds(2 * pair + 1, ELEMENTS, stride=PR), :] = turned[ELEMENTS:]


    lane = lanes_of((TR, 256))
    unit = jnp.where((jnp.bitwise_and(lane, 63) == rows_of((TR, 256))) & (lane < 192), 1.0, 0.0)
    unit = unit.astype(BF16)
    for u in range(WIDE):
        solved_in[u, PR:TR, :] = jnp.zeros((PR, 128), BF16)
    for u in range(BATCH):
        right[u, 0:64, :] = unit
        right[u, 128:192, :] = unit
        right[u, 224:256, :] = jnp.zeros((PR, 256), BF16)
    lane = lanes_of((PR, 128))

    @pl.loop(0, ELEMENTS // WIDE)
    def finish(step):
        for u in range(WIDE):
            e = step * WIDE + u
            high, low = halves(press[pl.ds(pl.multiple_of(e * PR, PR), PR), :])
            solved_in[u, 0:PR, :] = low
            solved_in[u, TR : TR + PR, :] = high
            solved_in[u, TR + PR :, :] = high
        for u in range(WIDE):
            e = step * WIDE + u
            inv = inverse[pl.ds(pl.multiple_of(e * PR, PR), PR), :]
            left = jnp.where(lane < TR + PR, inv, inv - inv.astype(BF16).astype(F32)).astype(BF16)
            solved = jnp.dot(left, solved_in[u], preferred_element_type=F32)
            taken = press[pl.ds(pl.multiple_of(e * PR, PR), PR), :] * solved
            diagonals[pl.ds(e, 1), :] = diagonals[pl.ds(e, 1), :] - jnp.sum(taken, axis=0, keepdims=True)
            for part, other in enumerate((pltpu.roll(solved, TR, 1), inv)):
                high, low = halves(-jnp.where(lane < TR, solved, other))
                cut = slice(128 * part, 128 * part + 128)
                duals[e, 0:PR, cut] = high
                duals[e, PR:TR, cut] = low

    diagonals[...] = diagonals[...] + lifts[...]


def facet_rows(g, i, jj, k):
    places = []
    for side in range(2):
        for start, size, slot in (
            (((i + side) * 4 + g) * GROUP, 64, jj * 4 + k),
            (Y_START + (2 * g + jj + side) * GROUP, 64, i * 4 + k),
            (Z_START + ((k + side) * 4 + g) * Z_GROUP, 32, i * 2 + jj),
        ):
            places.append((pl.multiple_of(start + slot * 8, 8), start + size + slot))
    return places


def gathered(field, places):
    row = rows_of((8, COLS))
    ninth = jnp.zeros((8, COLS), F32)
    pieces = []
    for facet, (main, extra) in enumerate(places):
        pieces.append(field[pl.ds(main, 8), :])
        line = jnp.broadcast_to(field[pl.ds(extra, 1), :], (8, COLS))
        ninth = jnp.where(row == facet, line, ninth)
    return pieces + [ninth]


def scatter(values, low, up, places):
    for facet, (main, extra) in enumerate(places):
        target = low if facet < 3 else up
        target[pl.ds(main, 8), :] = values[8 * facet : 8 * facet + 8]
        target[pl.ds(extra, 1), :] = values[48 + facet : 49 + facet]


EACH = [(i, jj, k) for i in range(BX) for jj in range(2) for k in range(BZ)]


def element_index(g, i, jj, k):
    return i * 32 + g * 8 + jj * 4 + k


def solver_kernel(sizes, *refs):
    arguments, (lam_hbm, hmat_hbm, forcing_hbm) = refs[:8], refs[8:11]
    (
        lmat, hmat, forcing, diagonals, highs, lows, duals, right,
        low, up, inverse, fields, vectors, weights, lam, near, turned, mine, parts_a, parts_b,
        load_sems, out_sems, send, recv, send_y, recv_y, send_d, recv_d, send_sum, recv_sum,
    ) = refs[11:41]
    local_scratch = refs[41:]
    loads = operand_loads(arguments, local_scratch, load_sems)
    nx, ny, nz = sizes
    ix, iy, iz = lax.axis_index("gx"), lax.axis_index("gy"), lax.axis_index("gz")

    def at_x(step):
        return (lax.rem(ix + step + nx, nx), iy, iz)

    def at_y(step):
        return (ix, lax.rem(iy + step + ny, ny), iz)

    def at_z(step):
        return (ix, iy, lax.rem(iz + step + nz, nz))

    def at_xy(a, b):
        return (lax.rem(ix + a, nx), lax.rem(iy + b, ny), iz)

    def far(step, count):
        return -min(step, count - step)

    plane = [(a, b) for a in range(nx) for b in range(ny) if (a, b) != (0, 0)]
    plane.sort(key=lambda at: far(at[0], nx) + far(at[1], ny))
    rings = [
        [at_xy(a, b) for a, b in plane],
        [at_z(s) for s in sorted(range(1, nz), key=lambda s: far(s, nz))],
    ]
    partners = rings[0] + rings[1]
    barrier = pltpu.get_barrier_semaphore()
    for partner in partners:
        pl.semaphore_signal(barrier, inc=1, device_id=partner, device_id_type=MESH)

    zero = jnp.zeros((8, COLS), F32)
    for u in range(len(EACH)):
        weights[u, 3 * TR : 4 * TR, :] = jnp.zeros((TR, COLS), BF16)

    @pl.loop(0, 16)
    def clear(group):
        for stage in range(3):
            start = Z_START + 32 + group * Z_GROUP
            low[stage, pl.ds(pl.multiple_of(start, 8), 8), :] = zero
            up[stage, pl.ds(pl.multiple_of(start + 4 * Z_GROUP, 8), 8), :] = zero

    @pl.loop(0, 20)
    def clear_inverse(group):
        inverse[pl.ds(pl.multiple_of(Z_START + 32 + group * Z_GROUP, 8), 8), :] = zero

    def remote(source, target, sent, received, device):
        return pltpu.make_async_remote_copy(
            src_ref=source, dst_ref=target, send_sem=sent, recv_sem=received,
            device_id=device, device_id_type=MESH,
        )

    def field_copy(buffer, stage, source, target, count, sent, received, device):
        return remote(
            buffer.at[stage, pl.ds(pl.multiple_of(source, 8), count)],
            buffer.at[stage, pl.ds(pl.multiple_of(target, 8), count)],
            sent, received, device,
        )

    def copies_xz(stage, g):
        x, z = g * GROUP, Z_START + g * Z_GROUP
        x_last, z_last = x + 8 * GROUP, z + 16 * Z_GROUP
        return [
            field_copy(low, stage, x, x_last, GROUP, send.at[stage, 0, g], recv.at[stage, 0, g], at_x(-1)),
            field_copy(up, stage, x_last, x, GROUP, send.at[stage, 1, g], recv.at[stage, 1, g], at_x(1)),
            field_copy(low, stage, z, z_last, Z_GROUP, send.at[stage, 2, g], recv.at[stage, 2, g], at_z(-1)),
            field_copy(up, stage, z_last, z, Z_GROUP, send.at[stage, 3, g], recv.at[stage, 3, g], at_z(1)),
        ]

    def copy_y(stage, side):
        first, last = Y_START, Y_START + 8 * GROUP
        if side == 0:
            return field_copy(low, stage, first, last, GROUP, send_y.at[stage, 0], recv_y.at[stage, 0], at_y(-1))
        return field_copy(up, stage, last, first, GROUP, send_y.at[stage, 1], recv_y.at[stage, 1], at_y(1))

    local_blocks(loads, (forcing, diagonals, highs, lows, duals, right), local_scratch)
    pl.semaphore_wait(barrier, len(partners))

    half = ELEMENTS // 2
    near_copies = [
        remote(diagonals.at[pl.ds(half, half)], near.at[0, pl.ds(0, half)], send_d.at[0], recv_d.at[0], at_x(1)),
        remote(diagonals.at[pl.ds(0, half)], near.at[1, pl.ds(0, half)], send_d.at[1], recv_d.at[1], at_x(-1)),
        remote(diagonals, near.at[2], send_d.at[2], recv_d.at[2], at_y(1)),
        remote(diagonals, near.at[3], send_d.at[3], recv_d.at[3], at_y(-1)),
        remote(diagonals, near.at[4], send_d.at[4], recv_d.at[4], at_z(1)),
        remote(diagonals, near.at[5], send_d.at[5], recv_d.at[5], at_z(-1)),
    ]
    for item in near_copies:
        item.start()

    def order(n):
        return lax.rem(3 * n, 4)

    def send_chunk(stage, n):
        for item in copies_xz(stage, order(n)):
            item.start()
        for side in range(2):
            @pl.when(n == side)
            def _():
                copy_y(stage, side).start()

    out_copies = [pltpu.make_async_copy(forcing, forcing_hbm, out_sems.at[0])]
    out_copies[0].start()

    def fill_right(u, e):
        right[u, 64:96, :] = duals[e, 0:PR, :]
        right[u, 96:128, :] = duals[e, PR:TR, :]
        right[u, 192:224, :] = duals[e, 0:PR, :]

    @pl.loop(0, 4)
    def start(n):
        g = order(n)
        for u, (i, jj, k) in enumerate(EACH):
            fill_right(u, element_index(g, i, jj, k))
        for u, (i, jj, k) in enumerate(EACH):
            e = element_index(g, i, jj, k)
            left = jnp.concatenate([highs[e, 0:TR, :], lows[e, 0:TR, :]], axis=1)
            both, rest = packed_pair(jnp.dot(left, right[u], preferred_element_type=F32))
            lmat[e, :, 0:128] = both.astype(BF16)
            lmat[e, :, 128:256] = rest
        for i, jj, k in EACH:
            e = element_index(g, i, jj, k)
            given = jnp.concatenate([jnp.zeros((TR, COLS), BF16), forcing[e], forcing[e]], axis=0)
            values = -jnp.dot(lmat[e, :, 128:256], given, preferred_element_type=F32)
            scatter(values, low.at[0], up.at[0], facet_rows(g, i, jj, k))
        send_chunk(0, n)

    for item in near_copies:
        item.wait()
    lane, row = lanes_of((ELEMENTS, 128)), rows_of((ELEMENTS, 128))
    x_lanes = (lane < 8) | (lane == 48)
    y_lanes = ((lane >= 8) & (lane < 16)) | (lane == 49)

    def uppers(value):
        return jnp.where(lane < 24, pltpu.roll(value, 104, 1), pltpu.roll(value, 125, 1))

    def reciprocal(total):
        return jnp.where(total > 0.5 * BLOCKED, 0.0, 1.0 / total)

    own = diagonals[...]
    own_up = uppers(own)
    from_x = jnp.concatenate([uppers(near[0])[0:half], own_up[0:half]], axis=0)
    first_y, first_z = jnp.bitwise_and(row, 31) < 4, jnp.bitwise_and(row, 3) == 0
    from_y = jnp.where(first_y, pltpu.roll(uppers(near[2]), 36, 0), pltpu.roll(own_up, 4, 0))
    from_z = jnp.where(first_z, pltpu.roll(uppers(near[4]), 61, 0), pltpu.roll(own_up, 1, 0))
    lower_sum = own + jnp.where(x_lanes, from_x, jnp.where(y_lanes, from_y, from_z))
    above_x = jnp.concatenate([near[1, 0:half, :], near[1, 0:half, :]], axis=0)
    above_y, above_z = pltpu.roll(near[3], 28, 0), pltpu.roll(near[5], 3, 0)
    upper_sum = own_up + jnp.where(x_lanes, above_x, jnp.where(y_lanes, above_y, above_z))
    flipped = jnp.transpose(jnp.concatenate([reciprocal(lower_sum), reciprocal(upper_sum)], axis=0))
    turned[0:24, :] = flipped[0:24]
    turned[24:32, :] = flipped[48:56]

    @pl.loop(0, 4)
    def expand(g):
        rolled = pltpu.roll(turned[...], lax.rem(128 - 8 * g, 128), 1)
        for i, jj, k in EACH:
            column = i * 32 + jj * 4 + k
            places = facet_rows(g, i, jj, k)
            for side in range(2):
                normals = [0, 1, 2] if side == 0 else [n for n, last in enumerate((i == 1, jj == 1, k == 3)) if last]
                if not normals:
                    continue
                at = 64 * side + column
                ninth = jnp.broadcast_to(rolled[24:32, at : at + 1], (8, COLS))
                for normal in normals:
                    main, extra = places[3 * side + normal]
                    inverse[pl.ds(main, 8), :] = jnp.broadcast_to(
                        rolled[8 * normal : 8 * normal + 8, at : at + 1], (8, COLS)
                    )
                    inverse[pl.ds(extra, 1), :] = ninth[normal : normal + 1]

    def update(step, g, total):
        spans = [((plane * 4 + g) * GROUP, 9, plane < 2) for plane in range(3)]
        spans += [(Y_START + (2 * g + plane) * GROUP, 9, plane < 2) for plane in range(3)]
        spans += [(Z_START + (plane * 4 + g) * Z_GROUP, 5, plane < 4) for plane in range(5)]
        for begin, tiles, owned in spans:
            for tile in range(tiles):
                place = pl.ds(pl.multiple_of(begin + tile * 8, 8), 8)
                value = low[step, place, :] + up[step, place, :]
                scaled = inverse[place, :] * value
                if step == 0:
                    fields[0, place, :] = scaled
                    if owned:
                        total = total + value * scaled
                else:
                    fields[step, place, :] = scaled - fields[step - 1, place, :]
        return total

    def operate(step, n, totals):
        g = order(n)
        totals = list(totals)
        for item in copies_xz(step, g):
            item.wait_recv()
        for side in range(2):
            @pl.when(n == 1 - side)
            def _():
                copy_y(step, side).wait_recv()
        totals[0] = update(step, g, totals[0])
        for u, (i, jj, k) in enumerate(EACH):
            pieces = gathered(fields.at[step], facet_rows(g, i, jj, k))
            vector = jnp.concatenate(pieces + [jnp.zeros((8, COLS), F32)], axis=0)
            vectors[step, element_index(g, i, jj, k)] = vector
            high, low_part = halves(vector)
            weights[u, 0:TR, :] = high
            weights[u, TR : 2 * TR, :] = low_part
            weights[u, 2 * TR : 3 * TR, :] = high
        for u, (i, jj, k) in enumerate(EACH):
            e = element_index(g, i, jj, k)
            values = jnp.dot(lmat[e], weights[u], preferred_element_type=F32)
            for which in range(1 if step == 0 else 2):
                products = vectors[step - which, e] * values
                parts = [products[8 * tile : 8 * tile + 8] for tile in range(7)]
                part = (parts[0] + parts[1]) + (parts[2] + parts[3])
                part = part + ((parts[4] + parts[5]) + parts[6])
                totals[1 + which] = totals[1 + which] + part
            if step < 2:
                scatter(values, low.at[step + 1], up.at[step + 1], facet_rows(g, i, jj, k))
        if step < 2:
            send_chunk(step + 1, n)
        return tuple(totals)

    moments = []
    for step in range(3):
        totals = lax.fori_loop(0, 4, functools.partial(operate, step), (zero,) * 3)
        moments += [totals[:2], totals[1:], totals[1:]][step]

    sublane = rows_of((8, COLS))
    tile = zero
    for which, moment in enumerate(moments):
        line = jnp.broadcast_to(jnp.sum(moment, axis=0, keepdims=True), (8, COLS))
        tile = jnp.where(sublane == which, line, tile)

    def recovery(batch):
        for u in range(BATCH):
            e = batch * BATCH + u
            fill_right(u, e)
        for u in range(BATCH):
            e = batch * BATCH + u
            left = jnp.concatenate([highs[e, TR:AR, :], lows[e, TR:AR, :]], axis=1)
            both, rest = packed_pair(jnp.dot(left, right[u], preferred_element_type=F32))
            hmat[e, :, 0:128] = both.astype(BF16)
            hmat[e, :, 128:256] = rest

    def drain():
        @pl.loop(0, 4)
        def _(g):
            for stage in range(3):
                for item in copies_xz(stage, g):
                    item.wait_send()

        for stage in range(3):
            for side in range(2):
                copy_y(stage, side).wait_send()

    batches = ELEMENTS // BATCH
    for stage, (ring, parts) in enumerate(zip(rings, (parts_a, parts_b))):
        mine[stage] = tile
        for n, partner in enumerate(ring):
            remote(mine.at[stage], parts.at[n], send_sum.at[stage], recv_sum.at[stage], partner).start()
        span = (0, batches // 2) if stage == 0 else (batches // 2, batches)
        pl.loop(*span)(recovery)
        place = pl.ds(span[0] * BATCH, (span[1] - span[0]) * BATCH)
        out_copies.append(pltpu.make_async_copy(hmat.at[place], hmat_hbm.at[place], out_sems.at[1 + stage]))
        out_copies[-1].start()
        if stage == 1:
            drain()
        pltpu.make_async_copy(parts, parts, recv_sum.at[stage]).wait()
        terms = [tile] + [parts[n] for n in range(len(ring))]
        while len(terms) > 1:
            terms = [sum(terms[n : n + 2][1:], terms[n]) for n in range(0, len(terms), 2)]
        tile = terms[0]
        pltpu.make_async_copy(parts, parts, send_sum.at[stage]).wait()

    b0, g00, g11, g01, g22, g12 = [tile[n : n + 1] for n in range(6)]
    b1 = g00 - b0
    b2 = g01 - b1
    g02 = g11
    l1, l2 = g01 / g00, g02 / g00
    h11, h12, h22 = g11 - l1 * g01, g12 - l1 * g02, g22 - l2 * g02
    d1, d2 = b1 - l1 * b0, b2 - l2 * b0
    sound = h11 > 2e-6 * g11
    m = jnp.where(sound, h12 / h11, 0.0)
    k22 = h22 - m * h12
    c2 = jnp.where(k22 > 2e-6 * g22, (d2 - m * d1) / k22, 0.0)
    c1 = jnp.where(sound, (d1 - h12 * c2) / h11, 0.0)
    c0 = (b0 - g01 * c1 - g02 * c2) / g00
    c0, c1, c2 = [jnp.broadcast_to(c, (8, COLS)) for c in (c0, c1, c2)]

    for part in range(2):
        @pl.loop(8 * part, 8 * part + 8)
        def combine(step):
            for u in range(4):
                e = 4 * step + u
                for tile in range(7):
                    place = slice(8 * tile, 8 * tile + 8)
                    lam[e, place, :] = (
                        c0 * vectors[0, e, place, :] + c1 * vectors[1, e, place, :] + c2 * vectors[2, e, place, :]
                    )

        place = pl.ds(32 * part, 32)
        out_copies.append(pltpu.make_async_copy(lam.at[place], lam_hbm.at[place], out_sems.at[3 + part]))
        out_copies[-1].start()

    for item in out_copies:
        item.wait()


def solve(sizes, *arguments):
    hbm = pl.BlockSpec(memory_space=pltpu.HBM)
    _, geometry, rock, permeability, mass_inv, div_map, trace_map, dirichlet = arguments
    dma = pltpu.SemaphoreType.DMA
    return pl.pallas_call(
        functools.partial(solver_kernel, sizes),
        out_shape=(
            jax.ShapeDtypeStruct((ELEMENTS, 56, COLS), F32),
            jax.ShapeDtypeStruct((ELEMENTS, FR, 256), BF16),
            jax.ShapeDtypeStruct((ELEMENTS, PR, COLS), BF16),
        ),
        in_specs=[hbm] * 8,
        out_specs=[hbm] * 3,
        scratch_shapes=[
            pltpu.VMEM((ELEMENTS, TR, 256), BF16),
            pltpu.VMEM((ELEMENTS, FR, 256), BF16),
            pltpu.VMEM((ELEMENTS, PR, COLS), BF16),
            pltpu.VMEM((ELEMENTS, 128), F32),
            pltpu.VMEM((ELEMENTS, AR, 128), BF16),
            pltpu.VMEM((ELEMENTS, AR, 128), BF16),
            pltpu.VMEM((ELEMENTS, TR, 256), BF16),
            pltpu.VMEM((BATCH, 256, 256), BF16),
            pltpu.VMEM((3, FIELD, COLS), F32),
            pltpu.VMEM((3, FIELD, COLS), F32),
            pltpu.VMEM((FIELD, COLS), F32),
            pltpu.VMEM((3, FIELD, COLS), F32),
            pltpu.VMEM((3, ELEMENTS, TR, COLS), F32),
            pltpu.VMEM((len(EACH), 256, COLS), BF16),
            pltpu.VMEM((ELEMENTS, 56, COLS), F32),
            pltpu.VMEM((6, ELEMENTS, 128), F32),
            pltpu.VMEM((32, 128), F32),
            pltpu.VMEM((2, 8, COLS), F32),
            pltpu.VMEM((sizes[0] * sizes[1] - 1, 8, COLS), F32),
            pltpu.VMEM((sizes[2] - 1, 8, COLS), F32),
            dma((8,)), dma((5,)),
            dma((3, 4, 4)), dma((3, 4, 4)), dma((3, 2)), dma((3, 2)), dma((6,)), dma((6,)), dma((2,)), dma((2,)),
            pltpu.VMEM(geometry.shape, F32),
            pltpu.SMEM(rock.shape, jnp.int32),
            pltpu.VMEM(permeability.shape, F32),
            pltpu.VMEM(mass_inv.shape, F32),
            pltpu.VMEM(div_map.shape, F32),
            pltpu.VMEM(trace_map.shape, F32),
            pltpu.SMEM(dirichlet.shape, jnp.int32),
            pltpu.VMEM((ELEMENTS * PRESS, COLS), BF16),
            pltpu.VMEM((ELEMENTS, 128), F32),
            pltpu.VMEM((128, 128), F32),
            pltpu.VMEM((128, 128), F32),
            pltpu.VMEM((128, 128), F32),
            pltpu.VMEM((128, 128), F32),
            pltpu.VMEM((FR, 384), BF16),
            pltpu.VMEM((TR + PR, 384), BF16),
            pltpu.VMEM((ELEMENTS * PR, 128), F32),
            pltpu.VMEM((ELEMENTS * PR, 128), F32),
            pltpu.VMEM((16, 128), F32),
            pltpu.VMEM((4, 432, 128), F32),
            pltpu.VMEM((WIDE // 2, FR, 256), F32),
            pltpu.VMEM((WIDE // 2, 384, 256), BF16),
            pltpu.VMEM((WIDE // 2, 384, 256), BF16),
            pltpu.VMEM((WIDE, 128, 128), BF16),
            pltpu.VMEM((14, PR, 128), F32),
        ],
        compiler_params=pltpu.CompilerParams(
            collective_id=0, has_side_effects=True, vmem_limit_bytes=GRANT
        ),
        name="solver",
    )(*arguments)


def recover_kernel(lam_hbm, hmat_hbm, forcing_hbm, traces_hbm, flux_hbm,
                   lam, hmat, forcing, traces, flux, weights, spread, load_sems, out_sems):
    pitch = 5
    first = rows_of((8, COLS)) < 4
    parts = ELEMENTS // BATCH
    rows_t, rows_f = BATCH * PRESS, BATCH * FLUX

    def loads(n):
        place = pl.ds(n * BATCH, BATCH)
        return [
            pltpu.make_async_copy(source.at[place], target.at[place], load_sems.at[n, which])
            for which, (source, target) in enumerate(
                ((lam_hbm, lam), (hmat_hbm, hmat), (forcing_hbm, forcing))
            )
        ]

    def stores(n):
        return [
            pltpu.make_async_copy(
                source.at[pl.ds(n * rows, rows)], target.at[pl.ds(n * rows, rows)], out_sems.at[n, which]
            )
            for which, (source, target, rows) in enumerate(
                ((traces, traces_hbm, rows_t), (flux, flux_hbm, rows_f))
            )
        ]

    for n in range(parts):
        for item in loads(n):
            item.start()

    @pl.loop(0, parts)
    def part(n):
        for item in loads(n):
            item.wait()
        for u in range(BATCH):
            e = n * BATCH + u
            tiles = [lam[e, 8 * tile : 8 * tile + 8, :] for tile in range(7)]
            start = n * rows_t + 108 * (u // 4) + u % 4
            for normal in range(3):
                traces[pl.ds(start + 36 * normal, 8, stride=4), :] = tiles[normal]
                traces[pl.ds(start + 36 * normal + 32, 1), :] = tiles[6][normal : normal + 1]
            high, low = halves(jnp.concatenate(tiles + [jnp.zeros((8, COLS), F32)], axis=0))
            weights[u, 0:TR, :] = high
            weights[u, TR : 2 * TR, :] = low
            weights[u, 2 * TR : 3 * TR, :] = high
            weights[u, 3 * TR : 3 * TR + PR, :] = forcing[e]
            weights[u, 3 * TR + PR :, :] = forcing[e]
        for u in range(BATCH):
            values = jnp.dot(hmat[n * BATCH + u], weights[u], preferred_element_type=F32)
            spread[pl.ds(FLUX * pitch * (u // 4) + u % 4, FLUX, stride=pitch), :] = -values[0:FLUX]
        for quad in range(BATCH * FLUX // 16):
            tiles = []
            for half in range(2):
                at = pitch * (4 * quad + 2 * half)
                tiles.append(jnp.where(first, spread[at : at + 8, :], spread[at + 1 : at + 9, :]))
            place = pl.ds(pl.multiple_of(n * rows_f + 16 * quad, 16), 16)
            flux[place, :] = jnp.concatenate(tiles, axis=0).astype(BF16)
        for item in stores(n):
            item.start()

    for n in range(parts):
        for item in stores(n):
            item.wait()


def recover(lam, hmat, forcing):
    hbm = pl.BlockSpec(memory_space=pltpu.HBM)
    out_shape = (
        jax.ShapeDtypeStruct((ELEMENTS * PRESS, COLS), F32),
        jax.ShapeDtypeStruct((ELEMENTS * FLUX, COLS), BF16),
    )
    return pl.pallas_call(
        recover_kernel,
        out_shape=out_shape,
        in_specs=[hbm] * 3,
        out_specs=[hbm] * 2,
        scratch_shapes=[
            pltpu.VMEM(item.shape, item.dtype) for item in (lam, hmat, forcing) + out_shape
        ] + [
            pltpu.VMEM((BATCH, 256, COLS), BF16),
            pltpu.VMEM((5 * BATCH * FLUX // 4 + 8, COLS), F32),
            pltpu.SemaphoreType.DMA((ELEMENTS // BATCH, 3)),
            pltpu.SemaphoreType.DMA((ELEMENTS // BATCH, 2)),
        ],
        compiler_params=pltpu.CompilerParams(vmem_limit_bytes=GRANT),
        name="recover",
    )(lam, hmat, forcing)


def body(sizes, sources, geometry, rock_class, permeability, mass_inv, div_map, trace_map, dirichlet):
    interleaved = sources.transpose(0, 1, 3, 2, 4).reshape(ELEMENTS * PRESS, COLS)
    lam, hmat, forcing = solve(
        sizes, interleaved, geometry, rock_class.transpose(0, 2, 1), permeability.T,
        mass_inv, div_map, trace_map, dirichlet.transpose(0, 3, 2, 1),
    )
    traces, flux = recover(lam, hmat, forcing)
    return (
        traces.reshape(BX, BY, PRESS, BZ, COLS).transpose(0, 1, 3, 2, 4),
        flux.reshape(BX, BY, FLUX, BZ, COLS).transpose(0, 1, 3, 2, 4),
    )


def solution(mesh):
    sizes = (mesh.shape["gx"], mesh.shape["gy"], mesh.shape["gz"])
    placed = (
        P("gx", "gy", "gz", None, None),
        P("gx", "gy", "gz", None),
        P("gx", "gy", "gz"),
        P(),
        P(),
        P(),
        P(),
        P("gx", "gy", "gz", None),
    )
    return jax.shard_map(
        functools.partial(body, sizes),
        mesh=mesh,
        in_specs=placed,
        out_specs=(P("gx", "gy", "gz", None, None), P("gx", "gy", "gz", None, None)),
        check_vma=False,
    )
```

```python
import functools

import jax
import jax.numpy as jnp
from jax import lax
from jax.experimental import pallas as pl
from jax.experimental.pallas import tpu as pltpu
from jax.sharding import PartitionSpec as P

MESH = pl.DeviceIdType.MESH
BF16 = jnp.bfloat16
F32 = jnp.float32

COLS = 128
PRESS = 27
FLUX = 108
BX, BY, BZ = 2, 8, 4
ELEMENTS = BX * BY * BZ

TR = 64
PR = 32
FR = 112
AR = TR + FR

GROUP = 72
Z_GROUP = 40
Y_START = 12 * GROUP
Z_START = Y_START + 9 * GROUP
FIELD = Z_START + 20 * Z_GROUP

BLOCKED = 1e30
MIB = 1024 * 1024

BATCH = 16
WIDE = 32

GRANT = 62 * MIB


def lanes_of(shape):
    return lax.broadcasted_iota(jnp.int32, shape, len(shape) - 1)


def rows_of(shape):
    return lax.broadcasted_iota(jnp.int32, shape, len(shape) - 2)


def halves(value):
    high = value.astype(BF16)
    return high, (value - high.astype(F32)).astype(BF16)


def packed_pair(value):
    first, second = value[:, 0:128], value[:, 128:256]
    lane = lanes_of(second.shape)
    kept = (lane >= TR) & (lane < TR + PR)
    return first, jnp.where(kept, second, second - second.astype(BF16).astype(F32)).astype(BF16)


def operand_loads(arguments, scratch, sems):
    sources_hbm, geometry_hbm, rock_hbm, permeability_hbm, mass_hbm, div_hbm, trace_hbm, dirichlet_hbm = arguments
    geometry, rock, permeability, mass_in, div_map, trace_map, dirichlet, sources = scratch[:8]
    loads = [
        pltpu.make_async_copy(source, target, sems.at[n])
        for n, (source, target) in enumerate(
            (
                (trace_hbm, trace_map),
                (div_hbm, div_map),
                (mass_hbm, mass_in),
                (permeability_hbm, permeability),
                (rock_hbm, rock),
                (geometry_hbm, geometry),
                (dirichlet_hbm, dirichlet),
                (sources_hbm, sources),
            )
        )
    ]
    for item in loads:
        item.start()
    return loads


def local_blocks(loads, results, scratch):
    forcing, diagonals, highs, lows, duals, right = results
    (
        geometry, rock, permeability, mass_in, div_map, trace_map, dirichlet, sources, lifts,
        joined, joined_t, padded, scale_t, left_mass, left_joined,
        press, inverse, table, spread, columns, first, second, solved_in, work,
    ) = scratch
    joined[...] = jnp.zeros_like(joined)
    padded[...] = jnp.zeros_like(padded)
    inverse[...] = jnp.zeros_like(inverse)
    for item in loads[:4]:
        item.wait()

    for facet in range(6):
        joined[8 * facet : 8 * facet + 8, 0:FLUX] = trace_map[9 * facet : 9 * facet + 8, :]
        joined[48 + facet : 49 + facet, 0:FLUX] = trace_map[9 * facet + 8 : 9 * facet + 9, :]
    joined[TR : TR + PRESS, 0:FLUX] = div_map[...]
    joined[TR + PR : TR + PR + PRESS, 0:FLUX] = div_map[...]
    joined_t[...] = jnp.transpose(joined[...])
    high, low = halves(joined[0 : TR + PR, :])
    left_joined[:, 0:128] = high
    left_joined[:, 128:256] = high
    left_joined[:, 256:384] = low
    padded[0:FLUX, 0:FLUX] = mass_in[...]
    high, low = halves(padded[0:FR, :])
    left_mass[:, 0:128] = high
    left_mass[:, 128:256] = high
    left_mass[:, 256:384] = low

    padded[...] = jnp.zeros_like(padded)
    padded[0:3, 0:16] = jnp.sqrt(permeability[...])
    rooted = jnp.transpose(padded[...])[0:16]
    lane = lanes_of((16, 128))
    table[0:16, :] = jnp.where(
        lane < 36, rooted[:, 0:1], jnp.where(lane < 72, rooted[:, 1:2], rooted[:, 2:3])
    )
    padded[...] = jnp.zeros_like(padded)
    loads[4].wait()
    loads[5].wait()
    for e in range(ELEMENTS):
        i, j, k = e // 32, (e // 4) % 8, e % 4
        row = table[pl.ds(rock[i, k, j], 1), :][:, 0:FLUX]
        padded[e : e + 1, 0:FLUX] = geometry[i, j, k : k + 1, :] * row
    scale_t[...] = jnp.transpose(padded[...])

    no_rows = jnp.zeros((128 - FR, 256), BF16)
    for pair in range(WIDE // 2):
        for part in range(3):
            first[pair, 128 * part + FR : 128 * part + 128, :] = no_rows
            second[pair, 128 * part + FR : 128 * part + 128, :] = no_rows

    on_diagonal = lanes_of((TR, 128)) == rows_of((TR, 128))

    @pl.loop(0, ELEMENTS // WIDE)
    def build(step):
        turned = pltpu.roll(scale_t[0:FR, :], lax.rem(128 - WIDE * step, 128), 1)
        for pair in range(WIDE // 2):
            for n in range(2):
                column = jnp.broadcast_to(turned[:, 2 * pair + n : 2 * pair + n + 1], (FR, 128))
                cut = slice(128 * n, 128 * n + 128)
                columns[pair, :, cut] = column
                high, low = halves(column * joined_t[0:FR, :])
                first[pair, 0:FR, cut] = high
                first[pair, 128 : 128 + FR, cut] = low
                first[pair, 256 : 256 + FR, cut] = high
        for pair in range(WIDE // 2):
            flux_side = columns[pair] * jnp.dot(left_mass[...], first[pair], preferred_element_type=F32)
            high, low = halves(flux_side)
            second[pair, 0:FR, :] = high
            second[pair, 128 : 128 + FR, :] = low
            second[pair, 256 : 256 + FR, :] = high
            for n in range(2):
                e = step * WIDE + 2 * pair + n
                cut = slice(128 * n, 128 * n + 128)
                highs[e, TR:AR, :] = high[:, cut]
                lows[e, TR:AR, :] = low[:, cut]
        for pair in range(WIDE // 2):
            coupled = jnp.dot(left_joined[...], second[pair], preferred_element_type=F32)
            high, low = halves(coupled[0:TR])
            for n in range(2):
                e = step * WIDE + 2 * pair + n
                cut = slice(128 * n, 128 * n + 128)
                highs[e, 0:TR, :] = high[:, cut]
                lows[e, 0:TR, :] = low[:, cut]
                diagonals[pl.ds(e, 1), :] = jnp.sum(
                    jnp.where(on_diagonal, coupled[0:TR, cut], 0.0), axis=0, keepdims=True
                )
                press[pl.ds(pl.multiple_of(e * PR, PR), PR), :] = coupled[TR:, cut]

    low_half = lanes_of((PR, 128)) < 64
    row_of = rows_of((PR, 128))

    early = lanes_of((ELEMENTS, 128)) < TR + PR
    for quad in range(7):
        rows = [press[pl.ds(4 * quad + n, ELEMENTS, stride=PR), :] for n in range(4)]
        stacked = [jnp.where(early, rows[0], rows[2]), jnp.where(early, rows[1], rows[3])]
        flipped = jnp.transpose(jnp.concatenate(stacked, axis=0))
        work[2 * quad] = flipped[TR : TR + PR, :]
        work[2 * quad + 1] = flipped[TR + PR :, :]

    loads[6].wait()
    loads[7].wait()
    line = lanes_of((1, 128))
    x_lanes = (line < 8) | (line == 48)
    y_lanes = ((line >= 8) & (line < 16)) | (line == 49)
    z_lanes = ((line >= 16) & (line < 24)) | (line == 50)
    for part in range(4):
        spread[part] = sources[432 * part : 432 * part + 432, :].astype(F32)

    def beside(e):
        i, j, k = e // 32, (e // 4) % 8, e % 4
        values = spread[e // 16, pl.ds(108 * (j % 4) + k, PRESS, stride=4), :]
        values = jnp.concatenate([values, jnp.zeros((PR - PRESS, COLS), F32)], axis=0)
        forcing[e] = values.astype(BF16)
        lift = [dirichlet[i, normal, k, j].astype(F32) * BLOCKED for normal in range(3)]
        lifts[e : e + 1, :] = jnp.where(
            x_lanes, lift[0], jnp.where(y_lanes, lift[1], jnp.where(z_lanes, lift[2], 0.0))
        )

    for owner in range(13):
        k = 2 * owner
        mine, next_one = row_of == k, row_of == k + 1
        source = work[owner]
        other = pltpu.roll(source, 64, 1)
        one, two = jnp.where(low_half, source, other), jnp.where(low_half, other, source)
        a, b = one[k : k + 1, :], one[k + 1 : k + 2, :]
        c, d = two[k : k + 1, :], two[k + 1 : k + 2, :]
        scale = 1.0 / (a * d - b * c)
        one = jnp.where(mine, 1.0, jnp.where(next_one, 0.0, one))
        two = jnp.where(mine, 0.0, jnp.where(next_one, 1.0, two))
        row_one = (d * scale) * one - (b * scale) * two
        row_two = (a * scale) * two - (c * scale) * one
        both = mine | next_one
        for pair in [owner + 1] + [p for p in range(14) if p not in (owner, owner + 1)]:
            value = work[pair]
            rest = jnp.where(both, 0.0, value) - value[k : k + 1, :] * row_one
            work[pair] = rest - value[k + 1 : k + 2, :] * row_two
        work[owner] = jnp.where(low_half, row_one, row_two)
        for e in range(5 * owner, min(5 * owner + 5, ELEMENTS)):
            beside(e)

    k = PRESS - 1
    mine = row_of == k
    source = work[13]
    source = jnp.where(low_half, source, pltpu.roll(source, 64, 1))
    row = jnp.where(mine, 1.0, source) * (1.0 / source[k : k + 1, :])
    for pair in range(13):
        value = work[pair]
        work[pair] = jnp.where(mine, 0.0, value) - value[k : k + 1, :] * row
    work[13] = jnp.where(low_half, row, 0.0)

    for pair in range(14):
        placed = jnp.concatenate(
            [work[pair], jnp.zeros((PR, 128), F32), work[pair], work[pair]], axis=0
        )
        turned = jnp.transpose(placed)
        inverse[pl.ds(2 * pair, ELEMENTS, stride=PR), :] = turned[0:ELEMENTS]
        inverse[pl.ds(2 * pair + 1, ELEMENTS, stride=PR), :] = turned[ELEMENTS:]


    lane = lanes_of((TR, 256))
    unit = jnp.where((jnp.bitwise_and(lane, 63) == rows_of((TR, 256))) & (lane < 192), 1.0, 0.0)
    unit = unit.astype(BF16)
    for u in range(WIDE):
        solved_in[u, PR:TR, :] = jnp.zeros((PR, 128), BF16)
    for u in range(BATCH):
        right[u, 0:64, :] = unit
        right[u, 128:192, :] = unit
        right[u, 224:256, :] = jnp.zeros((PR, 256), BF16)
    lane = lanes_of((PR, 128))

    @pl.loop(0, ELEMENTS // WIDE)
    def finish(step):
        for u in range(WIDE):
            e = step * WIDE + u
            high, low = halves(press[pl.ds(pl.multiple_of(e * PR, PR), PR), :])
            solved_in[u, 0:PR, :] = low
            solved_in[u, TR : TR + PR, :] = high
            solved_in[u, TR + PR :, :] = high
        for u in range(WIDE):
            e = step * WIDE + u
            inv = inverse[pl.ds(pl.multiple_of(e * PR, PR), PR), :]
            left = jnp.where(lane < TR + PR, inv, inv - inv.astype(BF16).astype(F32)).astype(BF16)
            solved = jnp.dot(left, solved_in[u], preferred_element_type=F32)
            taken = press[pl.ds(pl.multiple_of(e * PR, PR), PR), :] * solved
            diagonals[pl.ds(e, 1), :] = diagonals[pl.ds(e, 1), :] - jnp.sum(taken, axis=0, keepdims=True)
            for part, other in enumerate((pltpu.roll(solved, TR, 1), inv)):
                high, low = halves(-jnp.where(lane < TR, solved, other))
                cut = slice(128 * part, 128 * part + 128)
                duals[e, 0:PR, cut] = high
                duals[e, PR:TR, cut] = low

    diagonals[...] = diagonals[...] + lifts[...]


def j_of(g, jj):
    return (2 * g + 7 + jj) % 8 if isinstance(g, int) else lax.rem(2 * g + 7 + jj, 8)


def row_hint(row):
    return row if isinstance(row, int) else pl.multiple_of(row, 8)


def facet_rows(g, i, jj, k):
    places = []
    for side in range(2):
        for start, size, slot in (
            (((i + side) * 4 + g) * GROUP, 64, jj * 4 + k),
            (Y_START + (j_of(g, jj) + side) * GROUP, 64, i * 4 + k),
            (Z_START + ((k + side) * 4 + g) * Z_GROUP, 32, i * 2 + jj),
        ):
            places.append((row_hint(start + slot * 8), start + size + slot))
    return places


def gathered(field, places):
    row = rows_of((8, COLS))
    ninth = jnp.zeros((8, COLS), F32)
    pieces = []
    for facet, (main, extra) in enumerate(places):
        pieces.append(field[pl.ds(main, 8), :])
        line = jnp.broadcast_to(field[pl.ds(extra, 1), :], (8, COLS))
        ninth = jnp.where(row == facet, line, ninth)
    return pieces + [ninth]


def scatter(values, low, up, places):
    for facet, (main, extra) in enumerate(places):
        target = low if facet < 3 else up
        target[pl.ds(main, 8), :] = values[8 * facet : 8 * facet + 8]
        target[pl.ds(extra, 1), :] = values[48 + facet : 49 + facet]


EACH = [(i, jj, k) for i in range(BX) for jj in range(2) for k in range(BZ)]


def element_index(g, i, jj, k):
    return i * 32 + j_of(g, jj) * 4 + k


def solver_kernel(sizes, *refs):
    arguments, (lam_hbm, hmat_hbm, forcing_hbm) = refs[:8], refs[8:11]
    (
        lmat, hmat, forcing, diagonals, highs, lows, duals, right,
        low, up, inverse, fields, vectors, weights, lam, near, turned, mine, parts_a, parts_b,
        load_sems, out_sems, send, recv, send_y, recv_y, send_d, recv_d, send_sum, recv_sum,
    ) = refs[11:41]
    local_scratch = refs[41:]
    loads = operand_loads(arguments, local_scratch, load_sems)
    nx, ny, nz = sizes
    ix, iy, iz = lax.axis_index("gx"), lax.axis_index("gy"), lax.axis_index("gz")

    def at_x(step):
        return (lax.rem(ix + step + nx, nx), iy, iz)

    def at_y(step):
        return (ix, lax.rem(iy + step + ny, ny), iz)

    def at_z(step):
        return (ix, iy, lax.rem(iz + step + nz, nz))

    def at_xy(a, b):
        return (lax.rem(ix + a, nx), lax.rem(iy + b, ny), iz)

    def far(step, count):
        return -min(step, count - step)

    plane = [(a, b) for a in range(nx) for b in range(ny) if (a, b) != (0, 0)]
    plane.sort(key=lambda at: far(at[0], nx) + far(at[1], ny))
    rings = [
        [at_xy(a, b) for a, b in plane],
        [at_z(s) for s in sorted(range(1, nz), key=lambda s: far(s, nz))],
    ]
    partners = rings[0] + rings[1]
    barrier = pltpu.get_barrier_semaphore()
    for partner in partners:
        pl.semaphore_signal(barrier, inc=1, device_id=partner, device_id_type=MESH)

    zero = jnp.zeros((8, COLS), F32)
    for u in range(len(EACH)):
        weights[u, 3 * TR : 4 * TR, :] = jnp.zeros((TR, COLS), BF16)

    @pl.loop(0, 16)
    def clear(group):
        for stage in range(3):
            start = Z_START + 32 + group * Z_GROUP
            low[stage, pl.ds(pl.multiple_of(start, 8), 8), :] = zero
            up[stage, pl.ds(pl.multiple_of(start + 4 * Z_GROUP, 8), 8), :] = zero

    @pl.loop(0, 20)
    def clear_inverse(group):
        inverse[pl.ds(pl.multiple_of(Z_START + 32 + group * Z_GROUP, 8), 8), :] = zero

    def remote(source, target, sent, received, device):
        return pltpu.make_async_remote_copy(
            src_ref=source, dst_ref=target, send_sem=sent, recv_sem=received,
            device_id=device, device_id_type=MESH,
        )

    def field_copy(buffer, stage, source, target, count, sent, received, device):
        return remote(
            buffer.at[stage, pl.ds(row_hint(source), count)],
            buffer.at[stage, pl.ds(row_hint(target), count)],
            sent, received, device,
        )

    def copies_xz(stage, g):
        x, z = g * GROUP, Z_START + g * Z_GROUP
        x_last, z_last = x + 8 * GROUP, z + 16 * Z_GROUP
        return [
            field_copy(low, stage, x, x_last, GROUP, send.at[stage, 0, g], recv.at[stage, 0, g], at_x(-1)),
            field_copy(up, stage, x_last, x, GROUP, send.at[stage, 1, g], recv.at[stage, 1, g], at_x(1)),
            field_copy(low, stage, z, z_last, Z_GROUP, send.at[stage, 2, g], recv.at[stage, 2, g], at_z(-1)),
            field_copy(up, stage, z_last, z, Z_GROUP, send.at[stage, 3, g], recv.at[stage, 3, g], at_z(1)),
        ]

    def copy_y(stage, side):
        first, last = Y_START, Y_START + 8 * GROUP
        if side == 0:
            return field_copy(low, stage, first, last, GROUP, send_y.at[stage, 0], recv_y.at[stage, 0], at_y(-1))
        return field_copy(up, stage, last, first, GROUP, send_y.at[stage, 1], recv_y.at[stage, 1], at_y(1))

    local_blocks(loads, (forcing, diagonals, highs, lows, duals, right), local_scratch)
    pl.semaphore_wait(barrier, len(partners))

    half = ELEMENTS // 2
    near_copies = [
        remote(diagonals.at[pl.ds(half, half)], near.at[0, pl.ds(0, half)], send_d.at[0], recv_d.at[0], at_x(1)),
        remote(diagonals.at[pl.ds(0, half)], near.at[1, pl.ds(0, half)], send_d.at[1], recv_d.at[1], at_x(-1)),
        remote(diagonals, near.at[2], send_d.at[2], recv_d.at[2], at_y(1)),
        remote(diagonals, near.at[3], send_d.at[3], recv_d.at[3], at_y(-1)),
        remote(diagonals, near.at[4], send_d.at[4], recv_d.at[4], at_z(1)),
        remote(diagonals, near.at[5], send_d.at[5], recv_d.at[5], at_z(-1)),
    ]
    for item in near_copies:
        item.start()

    def send_chunk(stage, g):
        for item in copies_xz(stage, g):
            item.start()

        def both_y():
            for side in range(2):
                copy_y(stage, side).start()

        if isinstance(g, int):
            if g == 0:
                both_y()
        else:
            pl.when(g == 0)(both_y)

    out_copies = [pltpu.make_async_copy(forcing, forcing_hbm, out_sems.at[0])]
    out_copies[0].start()

    def fill_right(u, e):
        right[u, 64:96, :] = duals[e, 0:PR, :]
        right[u, 96:128, :] = duals[e, PR:TR, :]
        right[u, 192:224, :] = duals[e, 0:PR, :]

    @pl.loop(0, 4)
    def start(g):
        for u, (i, jj, k) in enumerate(EACH):
            fill_right(u, element_index(g, i, jj, k))
        for u, (i, jj, k) in enumerate(EACH):
            e = element_index(g, i, jj, k)
            left = jnp.concatenate([highs[e, 0:TR, :], lows[e, 0:TR, :]], axis=1)
            both, rest = packed_pair(jnp.dot(left, right[u], preferred_element_type=F32))
            lmat[e, :, 0:128] = both.astype(BF16)
            lmat[e, :, 128:256] = rest
        for i, jj, k in EACH:
            e = element_index(g, i, jj, k)
            given = jnp.concatenate([jnp.zeros((TR, COLS), BF16), forcing[e], forcing[e]], axis=0)
            values = -jnp.dot(lmat[e, :, 128:256], given, preferred_element_type=F32)
            scatter(values, low.at[0], up.at[0], facet_rows(g, i, jj, k))
        send_chunk(0, g)

    for item in near_copies:
        item.wait()
    lane, row = lanes_of((ELEMENTS, 128)), rows_of((ELEMENTS, 128))
    x_lanes = (lane < 8) | (lane == 48)
    y_lanes = ((lane >= 8) & (lane < 16)) | (lane == 49)

    def uppers(value):
        return jnp.where(lane < 24, pltpu.roll(value, 104, 1), pltpu.roll(value, 125, 1))

    def reciprocal(total):
        return jnp.where(total > 0.5 * BLOCKED, 0.0, 1.0 / total)

    own = diagonals[...]
    own_up = uppers(own)
    from_x = jnp.concatenate([uppers(near[0])[0:half], own_up[0:half]], axis=0)
    first_y, first_z = jnp.bitwise_and(row, 31) < 4, jnp.bitwise_and(row, 3) == 0
    from_y = jnp.where(first_y, pltpu.roll(uppers(near[2]), 36, 0), pltpu.roll(own_up, 4, 0))
    from_z = jnp.where(first_z, pltpu.roll(uppers(near[4]), 61, 0), pltpu.roll(own_up, 1, 0))
    lower_sum = own + jnp.where(x_lanes, from_x, jnp.where(y_lanes, from_y, from_z))
    above_x = jnp.concatenate([near[1, 0:half, :], near[1, 0:half, :]], axis=0)
    above_y, above_z = pltpu.roll(near[3], 28, 0), pltpu.roll(near[5], 3, 0)
    upper_sum = own_up + jnp.where(x_lanes, above_x, jnp.where(y_lanes, above_y, above_z))
    flipped = jnp.transpose(jnp.concatenate([reciprocal(lower_sum), reciprocal(upper_sum)], axis=0))
    turned[0:24, :] = flipped[0:24]
    turned[24:32, :] = flipped[48:56]

    rolled = turned[...]
    for g in range(4):
        for i, jj, k in EACH:
            column = element_index(g, i, jj, k)
            places = facet_rows(g, i, jj, k)
            for side in range(2):
                normals = [0, 1, 2] if side == 0 else [n for n, last in enumerate((i == 1, j_of(g, jj) == 7, k == 3)) if last]
                if not normals:
                    continue
                at = 64 * side + column
                ninth = jnp.broadcast_to(rolled[24:32, at : at + 1], (8, COLS))
                for normal in normals:
                    main, extra = places[3 * side + normal]
                    inverse[pl.ds(main, 8), :] = jnp.broadcast_to(
                        rolled[8 * normal : 8 * normal + 8, at : at + 1], (8, COLS)
                    )
                    inverse[pl.ds(extra, 1), :] = ninth[normal : normal + 1]

    def update(step, g, total):
        spans = [((plane * 4 + g) * GROUP, 9, plane < 2) for plane in range(3)]
        lowers = [j_of(g, jj) for jj in range(2)]
        spans += [(Y_START + plane * GROUP, 9, True) for plane in lowers]
        spans += [(Y_START + (j + 1) * GROUP, 9, False) for j in lowers if j + 1 not in lowers]
        spans += [(Z_START + (plane * 4 + g) * Z_GROUP, 5, plane < 4) for plane in range(5)]
        for begin, tiles, owned in spans:
            for tile in range(tiles):
                place = pl.ds(begin + tile * 8, 8)
                value = low[step, place, :] + up[step, place, :]
                scaled = inverse[place, :] * value
                if step == 0:
                    fields[0, place, :] = scaled
                    if owned:
                        total = total + value * scaled
                else:
                    fields[step, place, :] = scaled - fields[step - 1, place, :]
        return total

    def operate(step, g, totals):
        for item in copies_xz(step, g):
            item.wait_recv()
        if g == 0:
            for side in range(2):
                copy_y(step, side).wait_recv()
        totals[0] = update(step, g, totals[0])
        for u, (i, jj, k) in enumerate(EACH):
            pieces = gathered(fields.at[step], facet_rows(g, i, jj, k))
            vector = jnp.concatenate(pieces + [jnp.zeros((8, COLS), F32)], axis=0)
            vectors[step, element_index(g, i, jj, k)] = vector
            high, low_part = halves(vector)
            weights[u, 0:TR, :] = high
            weights[u, TR : 2 * TR, :] = low_part
            weights[u, 2 * TR : 3 * TR, :] = high
        for u, (i, jj, k) in enumerate(EACH):
            e = element_index(g, i, jj, k)
            values = jnp.dot(lmat[e], weights[u], preferred_element_type=F32)
            for which in range(1 if step == 0 else 2):
                products = vectors[step - which, e] * values
                parts = [products[8 * tile : 8 * tile + 8] for tile in range(7)]
                part = (parts[0] + parts[1]) + (parts[2] + parts[3])
                part = part + ((parts[4] + parts[5]) + parts[6])
                totals[1 + which] = totals[1 + which] + part
            if step < 2:
                scatter(values, low.at[step + 1], up.at[step + 1], facet_rows(g, i, jj, k))
        if step < 2:
            send_chunk(step + 1, g)

    moments = []
    for step in range(3):
        totals = [zero] * 3
        for g in range(4):
            operate(step, g, totals)
        moments += [totals[:2], totals[1:], totals[1:]][step]

    sublane = rows_of((8, COLS))
    tile = zero
    for which, moment in enumerate(moments):
        line = jnp.broadcast_to(jnp.sum(moment, axis=0, keepdims=True), (8, COLS))
        tile = jnp.where(sublane == which, line, tile)

    def recovery(batch):
        for u in range(BATCH):
            e = batch * BATCH + u
            fill_right(u, e)
        for u in range(BATCH):
            e = batch * BATCH + u
            left = jnp.concatenate([highs[e, TR:AR, :], lows[e, TR:AR, :]], axis=1)
            both, rest = packed_pair(jnp.dot(left, right[u], preferred_element_type=F32))
            hmat[e, :, 0:128] = both.astype(BF16)
            hmat[e, :, 128:256] = rest

    def drain():
        @pl.loop(0, 4)
        def _(g):
            for stage in range(3):
                for item in copies_xz(stage, g):
                    item.wait_send()

        for stage in range(3):
            for side in range(2):
                copy_y(stage, side).wait_send()

    batches = ELEMENTS // BATCH
    for stage, (ring, parts) in enumerate(zip(rings, (parts_a, parts_b))):
        mine[stage] = tile
        for n, partner in enumerate(ring):
            remote(mine.at[stage], parts.at[n], send_sum.at[stage], recv_sum.at[stage], partner).start()
        span = (0, batches // 2) if stage == 0 else (batches // 2, batches)
        pl.loop(*span)(recovery)
        place = pl.ds(span[0] * BATCH, (span[1] - span[0]) * BATCH)
        out_copies.append(pltpu.make_async_copy(hmat.at[place], hmat_hbm.at[place], out_sems.at[1 + stage]))
        out_copies[-1].start()
        if stage == 1:
            drain()
        pltpu.make_async_copy(parts, parts, recv_sum.at[stage]).wait()
        terms = [tile] + [parts[n] for n in range(len(ring))]
        while len(terms) > 1:
            terms = [sum(terms[n : n + 2][1:], terms[n]) for n in range(0, len(terms), 2)]
        tile = terms[0]
        pltpu.make_async_copy(parts, parts, send_sum.at[stage]).wait()

    b0, g00, g11, g01, g22, g12 = [tile[n : n + 1] for n in range(6)]
    b1 = g00 - b0
    b2 = g01 - b1
    g02 = g11
    l1, l2 = g01 / g00, g02 / g00
    h11, h12, h22 = g11 - l1 * g01, g12 - l1 * g02, g22 - l2 * g02
    d1, d2 = b1 - l1 * b0, b2 - l2 * b0
    sound = h11 > 2e-6 * g11
    m = jnp.where(sound, h12 / h11, 0.0)
    k22 = h22 - m * h12
    c2 = jnp.where(k22 > 2e-6 * g22, (d2 - m * d1) / k22, 0.0)
    c1 = jnp.where(sound, (d1 - h12 * c2) / h11, 0.0)
    c0 = (b0 - g01 * c1 - g02 * c2) / g00
    c0, c1, c2 = [jnp.broadcast_to(c, (8, COLS)) for c in (c0, c1, c2)]

    for part in range(2):
        @pl.loop(8 * part, 8 * part + 8)
        def combine(step):
            for u in range(4):
                e = 4 * step + u
                for tile in range(7):
                    place = slice(8 * tile, 8 * tile + 8)
                    lam[e, place, :] = (
                        c0 * vectors[0, e, place, :] + c1 * vectors[1, e, place, :] + c2 * vectors[2, e, place, :]
                    )

        place = pl.ds(32 * part, 32)
        out_copies.append(pltpu.make_async_copy(lam.at[place], lam_hbm.at[place], out_sems.at[3 + part]))
        out_copies[-1].start()

    for item in out_copies:
        item.wait()


def solve(sizes, *arguments):
    hbm = pl.BlockSpec(memory_space=pltpu.HBM)
    _, geometry, rock, permeability, mass_inv, div_map, trace_map, dirichlet = arguments
    dma = pltpu.SemaphoreType.DMA
    return pl.pallas_call(
        functools.partial(solver_kernel, sizes),
        out_shape=(
            jax.ShapeDtypeStruct((ELEMENTS, 56, COLS), F32),
            jax.ShapeDtypeStruct((ELEMENTS, FR, 256), BF16),
            jax.ShapeDtypeStruct((ELEMENTS, PR, COLS), BF16),
        ),
        in_specs=[hbm] * 8,
        out_specs=[hbm] * 3,
        scratch_shapes=[
            pltpu.VMEM((ELEMENTS, TR, 256), BF16),
            pltpu.VMEM((ELEMENTS, FR, 256), BF16),
            pltpu.VMEM((ELEMENTS, PR, COLS), BF16),
            pltpu.VMEM((ELEMENTS, 128), F32),
            pltpu.VMEM((ELEMENTS, AR, 128), BF16),
            pltpu.VMEM((ELEMENTS, AR, 128), BF16),
            pltpu.VMEM((ELEMENTS, TR, 256), BF16),
            pltpu.VMEM((BATCH, 256, 256), BF16),
            pltpu.VMEM((3, FIELD, COLS), F32),
            pltpu.VMEM((3, FIELD, COLS), F32),
            pltpu.VMEM((FIELD, COLS), F32),
            pltpu.VMEM((3, FIELD, COLS), F32),
            pltpu.VMEM((3, ELEMENTS, TR, COLS), F32),
            pltpu.VMEM((len(EACH), 256, COLS), BF16),
            pltpu.VMEM((ELEMENTS, 56, COLS), F32),
            pltpu.VMEM((6, ELEMENTS, 128), F32),
            pltpu.VMEM((32, 128), F32),
            pltpu.VMEM((2, 8, COLS), F32),
            pltpu.VMEM((sizes[0] * sizes[1] - 1, 8, COLS), F32),
            pltpu.VMEM((sizes[2] - 1, 8, COLS), F32),
            dma((8,)), dma((5,)),
            dma((3, 4, 4)), dma((3, 4, 4)), dma((3, 2)), dma((3, 2)), dma((6,)), dma((6,)), dma((2,)), dma((2,)),
            pltpu.VMEM(geometry.shape, F32),
            pltpu.SMEM(rock.shape, jnp.int32),
            pltpu.VMEM(permeability.shape, F32),
            pltpu.VMEM(mass_inv.shape, F32),
            pltpu.VMEM(div_map.shape, F32),
            pltpu.VMEM(trace_map.shape, F32),
            pltpu.SMEM(dirichlet.shape, jnp.int32),
            pltpu.VMEM((ELEMENTS * PRESS, COLS), BF16),
            pltpu.VMEM((ELEMENTS, 128), F32),
            pltpu.VMEM((128, 128), F32),
            pltpu.VMEM((128, 128), F32),
            pltpu.VMEM((128, 128), F32),
            pltpu.VMEM((128, 128), F32),
            pltpu.VMEM((FR, 384), BF16),
            pltpu.VMEM((TR + PR, 384), BF16),
            pltpu.VMEM((ELEMENTS * PR, 128), F32),
            pltpu.VMEM((ELEMENTS * PR, 128), F32),
            pltpu.VMEM((16, 128), F32),
            pltpu.VMEM((4, 432, 128), F32),
            pltpu.VMEM((WIDE // 2, FR, 256), F32),
            pltpu.VMEM((WIDE // 2, 384, 256), BF16),
            pltpu.VMEM((WIDE // 2, 384, 256), BF16),
            pltpu.VMEM((WIDE, 128, 128), BF16),
            pltpu.VMEM((14, PR, 128), F32),
        ],
        compiler_params=pltpu.CompilerParams(
            collective_id=0, has_side_effects=True, vmem_limit_bytes=GRANT
        ),
        name="solver",
    )(*arguments)


def recover_kernel(lam_hbm, hmat_hbm, forcing_hbm, traces_hbm, flux_hbm,
                   lam, hmat, forcing, traces, flux, weights, spread, load_sems, out_sems):
    pitch = 5
    first = rows_of((8, COLS)) < 4
    parts = ELEMENTS // BATCH
    rows_t, rows_f = BATCH * PRESS, BATCH * FLUX

    def loads(n):
        place = pl.ds(n * BATCH, BATCH)
        return [
            pltpu.make_async_copy(source.at[place], target.at[place], load_sems.at[n, which])
            for which, (source, target) in enumerate(
                ((lam_hbm, lam), (hmat_hbm, hmat), (forcing_hbm, forcing))
            )
        ]

    def stores(n):
        return [
            pltpu.make_async_copy(
                source.at[pl.ds(n * rows, rows)], target.at[pl.ds(n * rows, rows)], out_sems.at[n, which]
            )
            for which, (source, target, rows) in enumerate(
                ((traces, traces_hbm, rows_t), (flux, flux_hbm, rows_f))
            )
        ]

    for n in range(parts):
        for item in loads(n):
            item.start()

    @pl.loop(0, parts)
    def part(n):
        for item in loads(n):
            item.wait()
        for u in range(BATCH):
            e = n * BATCH + u
            tiles = [lam[e, 8 * tile : 8 * tile + 8, :] for tile in range(7)]
            start = n * rows_t + 108 * (u // 4) + u % 4
            for normal in range(3):
                traces[pl.ds(start + 36 * normal, 8, stride=4), :] = tiles[normal]
                traces[pl.ds(start + 36 * normal + 32, 1), :] = tiles[6][normal : normal + 1]
            high, low = halves(jnp.concatenate(tiles + [jnp.zeros((8, COLS), F32)], axis=0))
            weights[u, 0:TR, :] = high
            weights[u, TR : 2 * TR, :] = low
            weights[u, 2 * TR : 3 * TR, :] = high
            weights[u, 3 * TR : 3 * TR + PR, :] = forcing[e]
            weights[u, 3 * TR + PR :, :] = forcing[e]
        for u in range(BATCH):
            values = jnp.dot(hmat[n * BATCH + u], weights[u], preferred_element_type=F32)
            spread[pl.ds(FLUX * pitch * (u // 4) + u % 4, FLUX, stride=pitch), :] = -values[0:FLUX]
        for quad in range(BATCH * FLUX // 16):
            tiles = []
            for half in range(2):
                at = pitch * (4 * quad + 2 * half)
                tiles.append(jnp.where(first, spread[at : at + 8, :], spread[at + 1 : at + 9, :]))
            place = pl.ds(pl.multiple_of(n * rows_f + 16 * quad, 16), 16)
            flux[place, :] = jnp.concatenate(tiles, axis=0).astype(BF16)
        for item in stores(n):
            item.start()

    for n in range(parts):
        for item in stores(n):
            item.wait()


def recover(lam, hmat, forcing):
    hbm = pl.BlockSpec(memory_space=pltpu.HBM)
    out_shape = (
        jax.ShapeDtypeStruct((ELEMENTS * PRESS, COLS), F32),
        jax.ShapeDtypeStruct((ELEMENTS * FLUX, COLS), BF16),
    )
    return pl.pallas_call(
        recover_kernel,
        out_shape=out_shape,
        in_specs=[hbm] * 3,
        out_specs=[hbm] * 2,
        scratch_shapes=[
            pltpu.VMEM(item.shape, item.dtype) for item in (lam, hmat, forcing) + out_shape
        ] + [
            pltpu.VMEM((BATCH, 256, COLS), BF16),
            pltpu.VMEM((5 * BATCH * FLUX // 4 + 8, COLS), F32),
            pltpu.SemaphoreType.DMA((ELEMENTS // BATCH, 3)),
            pltpu.SemaphoreType.DMA((ELEMENTS // BATCH, 2)),
        ],
        compiler_params=pltpu.CompilerParams(vmem_limit_bytes=GRANT),
        name="recover",
    )(lam, hmat, forcing)


def body(sizes, sources, geometry, rock_class, permeability, mass_inv, div_map, trace_map, dirichlet):
    interleaved = sources.transpose(0, 1, 3, 2, 4).reshape(ELEMENTS * PRESS, COLS)
    lam, hmat, forcing = solve(
        sizes, interleaved, geometry, rock_class.transpose(0, 2, 1), permeability.T,
        mass_inv, div_map, trace_map, dirichlet.transpose(0, 3, 2, 1),
    )
    traces, flux = recover(lam, hmat, forcing)
    return (
        traces.reshape(BX, BY, PRESS, BZ, COLS).transpose(0, 1, 3, 2, 4),
        flux.reshape(BX, BY, FLUX, BZ, COLS).transpose(0, 1, 3, 2, 4),
    )


def solution(mesh):
    sizes = (mesh.shape["gx"], mesh.shape["gy"], mesh.shape["gz"])
    placed = (
        P("gx", "gy", "gz", None, None),
        P("gx", "gy", "gz", None),
        P("gx", "gy", "gz"),
        P(),
        P(),
        P(),
        P(),
        P("gx", "gy", "gz", None),
    )
    return jax.shard_map(
        functools.partial(body, sizes),
        mesh=mesh,
        in_specs=placed,
        out_specs=(P("gx", "gy", "gz", None, None), P("gx", "gy", "gz", None, None)),
        check_vma=False,
    )
```

```python
import functools

import jax
import jax.numpy as jnp
from jax import lax
from jax.experimental import pallas as pl
from jax.experimental.pallas import tpu as pltpu
from jax.sharding import PartitionSpec as P

MESH = pl.DeviceIdType.MESH
BF16 = jnp.bfloat16
F32 = jnp.float32

COLS = 128
PRESS = 27
FLUX = 108
BX, BY, BZ = 2, 8, 4
ELEMENTS = BX * BY * BZ

TR = 64
PR = 32
FR = 112
AR = TR + FR

GROUP = 72
Z_GROUP = 40
Y_START = 12 * GROUP
Z_START = Y_START + 9 * GROUP
FIELD = Z_START + 20 * Z_GROUP

BLOCKED = 1e30
MIB = 1024 * 1024

BATCH = 16
WIDE = 32

GRANT = 62 * MIB


def lanes_of(shape):
    return lax.broadcasted_iota(jnp.int32, shape, len(shape) - 1)


def rows_of(shape):
    return lax.broadcasted_iota(jnp.int32, shape, len(shape) - 2)


def halves(value):
    high = value.astype(BF16)
    return high, (value - high.astype(F32)).astype(BF16)


def packed_pair(value):
    first, second = value[:, 0:128], value[:, 128:256]
    lane = lanes_of(second.shape)
    kept = (lane >= TR) & (lane < TR + PR)
    return first, jnp.where(kept, second, second - second.astype(BF16).astype(F32)).astype(BF16)


def operand_loads(arguments, scratch, sems):
    sources_hbm, geometry_hbm, rock_hbm, permeability_hbm, mass_hbm, div_hbm, trace_hbm, dirichlet_hbm = arguments
    geometry, rock, permeability, mass_in, div_map, trace_map, dirichlet, sources = scratch[:8]
    loads = [
        pltpu.make_async_copy(source, target, sems.at[n])
        for n, (source, target) in enumerate(
            (
                (trace_hbm, trace_map),
                (div_hbm, div_map),
                (mass_hbm, mass_in),
                (permeability_hbm, permeability),
                (rock_hbm, rock),
                (geometry_hbm, geometry),
                (dirichlet_hbm, dirichlet),
                (sources_hbm, sources),
            )
        )
    ]
    for item in loads:
        item.start()
    return loads


def local_blocks(loads, results, scratch):
    forcing, diagonals, highs, lows, duals, right = results
    (
        geometry, rock, permeability, mass_in, div_map, trace_map, dirichlet, sources, lifts,
        joined, joined_t, padded, scale_t, left_mass, left_joined,
        press, inverse, table, spread, columns, first, second, solved_in, work,
    ) = scratch
    joined[...] = jnp.zeros_like(joined)
    padded[...] = jnp.zeros_like(padded)
    inverse[...] = jnp.zeros_like(inverse)
    for item in loads[:4]:
        item.wait()

    for facet in range(6):
        joined[8 * facet : 8 * facet + 8, 0:FLUX] = trace_map[9 * facet : 9 * facet + 8, :]
        joined[48 + facet : 49 + facet, 0:FLUX] = trace_map[9 * facet + 8 : 9 * facet + 9, :]
    joined[TR : TR + PRESS, 0:FLUX] = div_map[...]
    joined[TR + PR : TR + PR + PRESS, 0:FLUX] = div_map[...]
    joined_t[...] = jnp.transpose(joined[...])
    high, low = halves(joined[0 : TR + PR, :])
    left_joined[:, 0:128] = high
    left_joined[:, 128:256] = high
    left_joined[:, 256:384] = low
    padded[0:FLUX, 0:FLUX] = mass_in[...]
    high, low = halves(padded[0:FR, :])
    left_mass[:, 0:128] = high
    left_mass[:, 128:256] = high
    left_mass[:, 256:384] = low

    padded[...] = jnp.zeros_like(padded)
    padded[0:3, 0:16] = jnp.sqrt(permeability[...])
    rooted = jnp.transpose(padded[...])[0:16]
    lane = lanes_of((16, 128))
    table[0:16, :] = jnp.where(
        lane < 36, rooted[:, 0:1], jnp.where(lane < 72, rooted[:, 1:2], rooted[:, 2:3])
    )
    padded[...] = jnp.zeros_like(padded)
    loads[4].wait()
    loads[5].wait()
    for e in range(ELEMENTS):
        i, j, k = e // 32, (e // 4) % 8, e % 4
        row = table[pl.ds(rock[i, k, j], 1), :][:, 0:FLUX]
        padded[e : e + 1, 0:FLUX] = geometry[i, j, k : k + 1, :] * row
    scale_t[...] = jnp.transpose(padded[...])

    no_rows = jnp.zeros((128 - FR, 256), BF16)
    for pair in range(WIDE // 2):
        for part in range(3):
            first[pair, 128 * part + FR : 128 * part + 128, :] = no_rows
            second[pair, 128 * part + FR : 128 * part + 128, :] = no_rows

    on_diagonal = lanes_of((TR, 128)) == rows_of((TR, 128))

    @pl.loop(0, ELEMENTS // WIDE)
    def build(step):
        turned = pltpu.roll(scale_t[0:FR, :], lax.rem(128 - WIDE * step, 128), 1)
        for pair in range(WIDE // 2):
            for n in range(2):
                column = jnp.broadcast_to(turned[:, 2 * pair + n : 2 * pair + n + 1], (FR, 128))
                cut = slice(128 * n, 128 * n + 128)
                columns[pair, :, cut] = column
                high, low = halves(column * joined_t[0:FR, :])
                first[pair, 0:FR, cut] = high
                first[pair, 128 : 128 + FR, cut] = low
                first[pair, 256 : 256 + FR, cut] = high
        for pair in range(WIDE // 2):
            flux_side = columns[pair] * jnp.dot(left_mass[...], first[pair], preferred_element_type=F32)
            high, low = halves(flux_side)
            second[pair, 0:FR, :] = high
            second[pair, 128 : 128 + FR, :] = low
            second[pair, 256 : 256 + FR, :] = high
            for n in range(2):
                e = step * WIDE + 2 * pair + n
                cut = slice(128 * n, 128 * n + 128)
                highs[e, TR:AR, :] = high[:, cut]
                lows[e, TR:AR, :] = low[:, cut]
        for pair in range(WIDE // 2):
            coupled = jnp.dot(left_joined[...], second[pair], preferred_element_type=F32)
            high, low = halves(coupled[0:TR])
            for n in range(2):
                e = step * WIDE + 2 * pair + n
                cut = slice(128 * n, 128 * n + 128)
                highs[e, 0:TR, :] = high[:, cut]
                lows[e, 0:TR, :] = low[:, cut]
                diagonals[pl.ds(e, 1), :] = jnp.sum(
                    jnp.where(on_diagonal, coupled[0:TR, cut], 0.0), axis=0, keepdims=True
                )
                press[pl.ds(pl.multiple_of(e * PR, PR), PR), :] = coupled[TR:, cut]

    low_half = lanes_of((PR, 128)) < 64
    row_of = rows_of((PR, 128))

    early = lanes_of((ELEMENTS, 128)) < TR + PR
    for quad in range(7):
        rows = [press[pl.ds(4 * quad + n, ELEMENTS, stride=PR), :] for n in range(4)]
        stacked = [jnp.where(early, rows[0], rows[2]), jnp.where(early, rows[1], rows[3])]
        flipped = jnp.transpose(jnp.concatenate(stacked, axis=0))
        work[2 * quad] = flipped[TR : TR + PR, :]
        work[2 * quad + 1] = flipped[TR + PR :, :]

    loads[6].wait()
    loads[7].wait()
    line = lanes_of((1, 128))
    x_lanes = (line < 8) | (line == 48)
    y_lanes = ((line >= 8) & (line < 16)) | (line == 49)
    z_lanes = ((line >= 16) & (line < 24)) | (line == 50)
    for part in range(4):
        spread[part] = sources[432 * part : 432 * part + 432, :].astype(F32)

    def beside(e):
        i, j, k = e // 32, (e // 4) % 8, e % 4
        values = spread[e // 16, pl.ds(108 * (j % 4) + k, PRESS, stride=4), :]
        values = jnp.concatenate([values, jnp.zeros((PR - PRESS, COLS), F32)], axis=0)
        forcing[e] = values.astype(BF16)
        lift = [dirichlet[i, normal, k, j].astype(F32) * BLOCKED for normal in range(3)]
        lifts[e : e + 1, :] = jnp.where(
            x_lanes, lift[0], jnp.where(y_lanes, lift[1], jnp.where(z_lanes, lift[2], 0.0))
        )

    for owner in range(13):
        k = 2 * owner
        mine, next_one = row_of == k, row_of == k + 1
        source = work[owner]
        other = pltpu.roll(source, 64, 1)
        one, two = jnp.where(low_half, source, other), jnp.where(low_half, other, source)
        a, b = one[k : k + 1, :], one[k + 1 : k + 2, :]
        c, d = two[k : k + 1, :], two[k + 1 : k + 2, :]
        scale = 1.0 / (a * d - b * c)
        one = jnp.where(mine, 1.0, jnp.where(next_one, 0.0, one))
        two = jnp.where(mine, 0.0, jnp.where(next_one, 1.0, two))
        row_one = (d * scale) * one - (b * scale) * two
        row_two = (a * scale) * two - (c * scale) * one
        both = mine | next_one
        for pair in [owner + 1] + [p for p in range(14) if p not in (owner, owner + 1)]:
            value = work[pair]
            rest = jnp.where(both, 0.0, value) - value[k : k + 1, :] * row_one
            work[pair] = rest - value[k + 1 : k + 2, :] * row_two
        work[owner] = jnp.where(low_half, row_one, row_two)
        for e in range(5 * owner, min(5 * owner + 5, ELEMENTS)):
            beside(e)

    k = PRESS - 1
    mine = row_of == k
    source = work[13]
    source = jnp.where(low_half, source, pltpu.roll(source, 64, 1))
    row = jnp.where(mine, 1.0, source) * (1.0 / source[k : k + 1, :])
    for pair in range(13):
        value = work[pair]
        work[pair] = jnp.where(mine, 0.0, value) - value[k : k + 1, :] * row
    work[13] = jnp.where(low_half, row, 0.0)

    for pair in range(14):
        placed = jnp.concatenate(
            [work[pair], jnp.zeros((PR, 128), F32), work[pair], work[pair]], axis=0
        )
        turned = jnp.transpose(placed)
        inverse[pl.ds(2 * pair, ELEMENTS, stride=PR), :] = turned[0:ELEMENTS]
        inverse[pl.ds(2 * pair + 1, ELEMENTS, stride=PR), :] = turned[ELEMENTS:]


    lane = lanes_of((TR, 256))
    unit = jnp.where((jnp.bitwise_and(lane, 63) == rows_of((TR, 256))) & (lane < 192), 1.0, 0.0)
    unit = unit.astype(BF16)
    for u in range(WIDE):
        solved_in[u, PR:TR, :] = jnp.zeros((PR, 128), BF16)
    for u in range(BATCH):
        right[u, 0:64, :] = unit
        right[u, 128:192, :] = unit
        right[u, 224:256, :] = jnp.zeros((PR, 256), BF16)
    lane = lanes_of((PR, 128))

    @pl.loop(0, ELEMENTS // WIDE)
    def finish(step):
        for u in range(WIDE):
            e = step * WIDE + u
            high, low = halves(press[pl.ds(pl.multiple_of(e * PR, PR), PR), :])
            solved_in[u, 0:PR, :] = low
            solved_in[u, TR : TR + PR, :] = high
            solved_in[u, TR + PR :, :] = high
        for u in range(WIDE):
            e = step * WIDE + u
            inv = inverse[pl.ds(pl.multiple_of(e * PR, PR), PR), :]
            left = jnp.where(lane < TR + PR, inv, inv - inv.astype(BF16).astype(F32)).astype(BF16)
            solved = jnp.dot(left, solved_in[u], preferred_element_type=F32)
            taken = press[pl.ds(pl.multiple_of(e * PR, PR), PR), :] * solved
            diagonals[pl.ds(e, 1), :] = diagonals[pl.ds(e, 1), :] - jnp.sum(taken, axis=0, keepdims=True)
            for part, other in enumerate((pltpu.roll(solved, TR, 1), inv)):
                high, low = halves(-jnp.where(lane < TR, solved, other))
                cut = slice(128 * part, 128 * part + 128)
                duals[e, 0:PR, cut] = high
                duals[e, PR:TR, cut] = low

    diagonals[...] = diagonals[...] + lifts[...]


def j_of(g, jj):
    return (2 * g + 7 + jj) % 8 if isinstance(g, int) else lax.rem(2 * g + 7 + jj, 8)


def row_hint(row):
    return row if isinstance(row, int) else pl.multiple_of(row, 8)


def facet_rows(g, i, jj, k):
    places = []
    for side in range(2):
        for start, size, slot in (
            (((i + side) * 4 + g) * GROUP, 64, jj * 4 + k),
            (Y_START + (j_of(g, jj) + side) * GROUP, 64, i * 4 + k),
            (Z_START + ((k + side) * 4 + g) * Z_GROUP, 32, i * 2 + jj),
        ):
            places.append((row_hint(start + slot * 8), start + size + slot))
    return places


def gathered(field, places):
    row = rows_of((8, COLS))
    ninth = jnp.zeros((8, COLS), F32)
    pieces = []
    for facet, (main, extra) in enumerate(places):
        pieces.append(field[pl.ds(main, 8), :])
        line = jnp.broadcast_to(field[pl.ds(extra, 1), :], (8, COLS))
        ninth = jnp.where(row == facet, line, ninth)
    return pieces + [ninth]


def scatter(values, low, up, places):
    for facet, (main, extra) in enumerate(places):
        target = low if facet < 3 else up
        target[pl.ds(main, 8), :] = values[8 * facet : 8 * facet + 8]
        target[pl.ds(extra, 1), :] = values[48 + facet : 49 + facet]


EACH = [(i, jj, k) for i in range(BX) for jj in range(2) for k in range(BZ)]


def element_index(g, i, jj, k):
    return i * 32 + j_of(g, jj) * 4 + k


def solver_kernel(sizes, *refs):
    arguments, (lam_hbm, hmat_hbm, forcing_hbm) = refs[:8], refs[8:11]
    (
        lmat, hmat, forcing, diagonals, highs, lows, duals, right,
        low, up, inverse, fields, vectors, weights, lam, near, turned, mine, parts_a, parts_b,
        load_sems, out_sems, send, recv, send_y, recv_y, send_d, recv_d, send_sum, recv_sum,
    ) = refs[11:41]
    local_scratch = refs[41:]
    loads = operand_loads(arguments, local_scratch, load_sems)
    nx, ny, nz = sizes
    ix, iy, iz = lax.axis_index("gx"), lax.axis_index("gy"), lax.axis_index("gz")

    def at_x(step):
        return (lax.rem(ix + step + nx, nx), iy, iz)

    def at_y(step):
        return (ix, lax.rem(iy + step + ny, ny), iz)

    def at_z(step):
        return (ix, iy, lax.rem(iz + step + nz, nz))

    def at_xy(a, b):
        return (lax.rem(ix + a, nx), lax.rem(iy + b, ny), iz)

    def far(step, count):
        return -min(step, count - step)

    plane = [(a, b) for a in range(nx) for b in range(ny) if (a, b) != (0, 0)]
    plane.sort(key=lambda at: far(at[0], nx) + far(at[1], ny))
    rings = [
        [at_xy(a, b) for a, b in plane],
        [at_z(s) for s in sorted(range(1, nz), key=lambda s: far(s, nz))],
    ]
    partners = rings[0] + rings[1]
    barrier = pltpu.get_barrier_semaphore()
    for partner in partners:
        pl.semaphore_signal(barrier, inc=1, device_id=partner, device_id_type=MESH)

    zero = jnp.zeros((8, COLS), F32)
    for u in range(len(EACH)):
        weights[u, 3 * TR : 4 * TR, :] = jnp.zeros((TR, COLS), BF16)

    @pl.loop(0, 16)
    def clear(group):
        for stage in range(3):
            start = Z_START + 32 + group * Z_GROUP
            low[stage, pl.ds(pl.multiple_of(start, 8), 8), :] = zero
            up[stage, pl.ds(pl.multiple_of(start + 4 * Z_GROUP, 8), 8), :] = zero

    @pl.loop(0, 20)
    def clear_inverse(group):
        inverse[pl.ds(pl.multiple_of(Z_START + 32 + group * Z_GROUP, 8), 8), :] = zero

    def remote(source, target, sent, received, device):
        return pltpu.make_async_remote_copy(
            src_ref=source, dst_ref=target, send_sem=sent, recv_sem=received,
            device_id=device, device_id_type=MESH,
        )

    def field_copy(buffer, stage, source, target, count, sent, received, device):
        return remote(
            buffer.at[stage, pl.ds(row_hint(source), count)],
            buffer.at[stage, pl.ds(row_hint(target), count)],
            sent, received, device,
        )

    def copies_xz(stage, g):
        x, z = g * GROUP, Z_START + g * Z_GROUP
        x_last, z_last = x + 8 * GROUP, z + 16 * Z_GROUP
        return [
            field_copy(low, stage, x, x_last, GROUP, send.at[stage, 0, g], recv.at[stage, 0, g], at_x(-1)),
            field_copy(up, stage, x_last, x, GROUP, send.at[stage, 1, g], recv.at[stage, 1, g], at_x(1)),
            field_copy(low, stage, z, z_last, Z_GROUP, send.at[stage, 2, g], recv.at[stage, 2, g], at_z(-1)),
            field_copy(up, stage, z_last, z, Z_GROUP, send.at[stage, 3, g], recv.at[stage, 3, g], at_z(1)),
        ]

    def copy_y(stage, side):
        first, last = Y_START, Y_START + 8 * GROUP
        if side == 0:
            return field_copy(low, stage, first, last, GROUP, send_y.at[stage, 0], recv_y.at[stage, 0], at_y(-1))
        return field_copy(up, stage, last, first, GROUP, send_y.at[stage, 1], recv_y.at[stage, 1], at_y(1))

    local_blocks(loads, (forcing, diagonals, highs, lows, duals, right), local_scratch)
    pl.semaphore_wait(barrier, len(partners))

    half = ELEMENTS // 2
    near_copies = [
        remote(diagonals.at[pl.ds(half, half)], near.at[0, pl.ds(0, half)], send_d.at[0], recv_d.at[0], at_x(1)),
        remote(diagonals.at[pl.ds(0, half)], near.at[1, pl.ds(0, half)], send_d.at[1], recv_d.at[1], at_x(-1)),
        remote(diagonals, near.at[2], send_d.at[2], recv_d.at[2], at_y(1)),
        remote(diagonals, near.at[3], send_d.at[3], recv_d.at[3], at_y(-1)),
        remote(diagonals, near.at[4], send_d.at[4], recv_d.at[4], at_z(1)),
        remote(diagonals, near.at[5], send_d.at[5], recv_d.at[5], at_z(-1)),
    ]
    for item in near_copies:
        item.start()

    def send_chunk(stage, g):
        for item in copies_xz(stage, g):
            item.start()

        if g == 0:
            for side in range(2):
                copy_y(stage, side).start()

    out_copies = [pltpu.make_async_copy(forcing, forcing_hbm, out_sems.at[0])]
    out_copies[0].start()

    def fill_right(u, e):
        right[u, 64:96, :] = duals[e, 0:PR, :]
        right[u, 96:128, :] = duals[e, PR:TR, :]
        right[u, 192:224, :] = duals[e, 0:PR, :]

    def start(g):
        for u, (i, jj, k) in enumerate(EACH):
            fill_right(u, element_index(g, i, jj, k))
        for u, (i, jj, k) in enumerate(EACH):
            e = element_index(g, i, jj, k)
            left = jnp.concatenate([highs[e, 0:TR, :], lows[e, 0:TR, :]], axis=1)
            both, rest = packed_pair(jnp.dot(left, right[u], preferred_element_type=F32))
            lmat[e, :, 0:128] = both.astype(BF16)
            lmat[e, :, 128:256] = rest
        for i, jj, k in EACH:
            e = element_index(g, i, jj, k)
            given = jnp.concatenate([jnp.zeros((TR, COLS), BF16), forcing[e], forcing[e]], axis=0)
            values = -jnp.dot(lmat[e, :, 128:256], given, preferred_element_type=F32)
            scatter(values, low.at[0], up.at[0], facet_rows(g, i, jj, k))
        send_chunk(0, g)

    for g in range(4):
        start(g)

    for item in near_copies:
        item.wait()
    lane, row = lanes_of((ELEMENTS, 128)), rows_of((ELEMENTS, 128))
    x_lanes = (lane < 8) | (lane == 48)
    y_lanes = ((lane >= 8) & (lane < 16)) | (lane == 49)

    def uppers(value):
        return jnp.where(lane < 24, pltpu.roll(value, 104, 1), pltpu.roll(value, 125, 1))

    def reciprocal(total):
        return jnp.where(total > 0.5 * BLOCKED, 0.0, 1.0 / total)

    own = diagonals[...]
    own_up = uppers(own)
    from_x = jnp.concatenate([uppers(near[0])[0:half], own_up[0:half]], axis=0)
    first_y, first_z = jnp.bitwise_and(row, 31) < 4, jnp.bitwise_and(row, 3) == 0
    from_y = jnp.where(first_y, pltpu.roll(uppers(near[2]), 36, 0), pltpu.roll(own_up, 4, 0))
    from_z = jnp.where(first_z, pltpu.roll(uppers(near[4]), 61, 0), pltpu.roll(own_up, 1, 0))
    lower_sum = own + jnp.where(x_lanes, from_x, jnp.where(y_lanes, from_y, from_z))
    above_x = jnp.concatenate([near[1, 0:half, :], near[1, 0:half, :]], axis=0)
    above_y, above_z = pltpu.roll(near[3], 28, 0), pltpu.roll(near[5], 3, 0)
    upper_sum = own_up + jnp.where(x_lanes, above_x, jnp.where(y_lanes, above_y, above_z))
    flipped = jnp.transpose(jnp.concatenate([reciprocal(lower_sum), reciprocal(upper_sum)], axis=0))
    turned[0:24, :] = flipped[0:24]
    turned[24:32, :] = flipped[48:56]

    rolled = turned[...]
    for g in range(4):
        for i, jj, k in EACH:
            column = element_index(g, i, jj, k)
            places = facet_rows(g, i, jj, k)
            for side in range(2):
                normals = [0, 1, 2] if side == 0 else [n for n, last in enumerate((i == 1, j_of(g, jj) == 7, k == 3)) if last]
                if not normals:
                    continue
                at = 64 * side + column
                ninth = jnp.broadcast_to(rolled[24:32, at : at + 1], (8, COLS))
                for normal in normals:
                    main, extra = places[3 * side + normal]
                    inverse[pl.ds(main, 8), :] = jnp.broadcast_to(
                        rolled[8 * normal : 8 * normal + 8, at : at + 1], (8, COLS)
                    )
                    inverse[pl.ds(extra, 1), :] = ninth[normal : normal + 1]

    def update(step, g, total):
        spans = [((plane * 4 + g) * GROUP, 9, plane < 2) for plane in range(3)]
        lowers = [j_of(g, jj) for jj in range(2)]
        spans += [(Y_START + plane * GROUP, 9, True) for plane in lowers]
        spans += [(Y_START + (j + 1) * GROUP, 9, False) for j in lowers if j + 1 not in lowers]
        spans += [(Z_START + (plane * 4 + g) * Z_GROUP, 5, plane < 4) for plane in range(5)]
        for begin, tiles, owned in spans:
            for tile in range(tiles):
                place = pl.ds(begin + tile * 8, 8)
                value = low[step, place, :] + up[step, place, :]
                scaled = inverse[place, :] * value
                if step == 0:
                    fields[0, place, :] = scaled
                    if owned:
                        total = total + value * scaled
                else:
                    fields[step, place, :] = scaled - fields[step - 1, place, :]
        return total

    def operate(step, g, totals):
        for item in copies_xz(step, g):
            item.wait_recv()
        if g == 0:
            for side in range(2):
                copy_y(step, side).wait_recv()
        totals[0] = update(step, g, totals[0])
        for u, (i, jj, k) in enumerate(EACH):
            pieces = gathered(fields.at[step], facet_rows(g, i, jj, k))
            vector = jnp.concatenate(pieces + [jnp.zeros((8, COLS), F32)], axis=0)
            vectors[step, element_index(g, i, jj, k)] = vector
            high, low_part = halves(vector)
            weights[u, 0:TR, :] = high
            weights[u, TR : 2 * TR, :] = low_part
            weights[u, 2 * TR : 3 * TR, :] = high
        for u, (i, jj, k) in enumerate(EACH):
            e = element_index(g, i, jj, k)
            values = jnp.dot(lmat[e], weights[u], preferred_element_type=F32)
            for which in range(1 if step == 0 else 2):
                products = vectors[step - which, e] * values
                parts = [products[8 * tile : 8 * tile + 8] for tile in range(7)]
                part = (parts[0] + parts[1]) + (parts[2] + parts[3])
                part = part + ((parts[4] + parts[5]) + parts[6])
                totals[1 + which] = totals[1 + which] + part
            if step < 2:
                scatter(values, low.at[step + 1], up.at[step + 1], facet_rows(g, i, jj, k))
        if step < 2:
            send_chunk(step + 1, g)

    moments = []
    for step in range(3):
        totals = [zero] * 3
        for g in range(4):
            operate(step, g, totals)
        moments += [totals[:2], totals[1:], totals[1:]][step]

    sublane = rows_of((8, COLS))
    tile = zero
    for which, moment in enumerate(moments):
        line = jnp.broadcast_to(jnp.sum(moment, axis=0, keepdims=True), (8, COLS))
        tile = jnp.where(sublane == which, line, tile)

    def recovery(batch):
        for u in range(BATCH):
            e = batch * BATCH + u
            fill_right(u, e)
        for u in range(BATCH):
            e = batch * BATCH + u
            left = jnp.concatenate([highs[e, TR:AR, :], lows[e, TR:AR, :]], axis=1)
            both, rest = packed_pair(jnp.dot(left, right[u], preferred_element_type=F32))
            hmat[e, :, 0:128] = both.astype(BF16)
            hmat[e, :, 128:256] = rest

    def drain():
        @pl.loop(0, 4)
        def _(g):
            for stage in range(3):
                for item in copies_xz(stage, g):
                    item.wait_send()

        for stage in range(3):
            for side in range(2):
                copy_y(stage, side).wait_send()

    batches = ELEMENTS // BATCH
    for stage, (ring, parts) in enumerate(zip(rings, (parts_a, parts_b))):
        mine[stage] = tile
        for n, partner in enumerate(ring):
            remote(mine.at[stage], parts.at[n], send_sum.at[stage], recv_sum.at[stage], partner).start()
        span = (0, batches // 2) if stage == 0 else (batches // 2, batches)
        pl.loop(*span)(recovery)
        place = pl.ds(span[0] * BATCH, (span[1] - span[0]) * BATCH)
        out_copies.append(pltpu.make_async_copy(hmat.at[place], hmat_hbm.at[place], out_sems.at[1 + stage]))
        out_copies[-1].start()
        if stage == 1:
            drain()
        pltpu.make_async_copy(parts, parts, recv_sum.at[stage]).wait()
        terms = [tile] + [parts[n] for n in range(len(ring))]
        while len(terms) > 1:
            terms = [sum(terms[n : n + 2][1:], terms[n]) for n in range(0, len(terms), 2)]
        tile = terms[0]
        pltpu.make_async_copy(parts, parts, send_sum.at[stage]).wait()

    b0, g00, g11, g01, g22, g12 = [tile[n : n + 1] for n in range(6)]
    b1 = g00 - b0
    b2 = g01 - b1
    g02 = g11
    l1, l2 = g01 / g00, g02 / g00
    h11, h12, h22 = g11 - l1 * g01, g12 - l1 * g02, g22 - l2 * g02
    d1, d2 = b1 - l1 * b0, b2 - l2 * b0
    sound = h11 > 2e-6 * g11
    m = jnp.where(sound, h12 / h11, 0.0)
    k22 = h22 - m * h12
    c2 = jnp.where(k22 > 2e-6 * g22, (d2 - m * d1) / k22, 0.0)
    c1 = jnp.where(sound, (d1 - h12 * c2) / h11, 0.0)
    c0 = (b0 - g01 * c1 - g02 * c2) / g00
    c0, c1, c2 = [jnp.broadcast_to(c, (8, COLS)) for c in (c0, c1, c2)]

    for part in range(2):
        @pl.loop(8 * part, 8 * part + 8)
        def combine(step):
            for u in range(4):
                e = 4 * step + u
                for tile in range(7):
                    place = slice(8 * tile, 8 * tile + 8)
                    lam[e, place, :] = (
                        c0 * vectors[0, e, place, :] + c1 * vectors[1, e, place, :] + c2 * vectors[2, e, place, :]
                    )

        place = pl.ds(32 * part, 32)
        out_copies.append(pltpu.make_async_copy(lam.at[place], lam_hbm.at[place], out_sems.at[3 + part]))
        out_copies[-1].start()

    for item in out_copies:
        item.wait()


def solve(sizes, *arguments):
    hbm = pl.BlockSpec(memory_space=pltpu.HBM)
    _, geometry, rock, permeability, mass_inv, div_map, trace_map, dirichlet = arguments
    dma = pltpu.SemaphoreType.DMA
    return pl.pallas_call(
        functools.partial(solver_kernel, sizes),
        out_shape=(
            jax.ShapeDtypeStruct((ELEMENTS, 56, COLS), F32),
            jax.ShapeDtypeStruct((ELEMENTS, FR, 256), BF16),
            jax.ShapeDtypeStruct((ELEMENTS, PR, COLS), BF16),
        ),
        in_specs=[hbm] * 8,
        out_specs=[hbm] * 3,
        scratch_shapes=[
            pltpu.VMEM((ELEMENTS, TR, 256), BF16),
            pltpu.VMEM((ELEMENTS, FR, 256), BF16),
            pltpu.VMEM((ELEMENTS, PR, COLS), BF16),
            pltpu.VMEM((ELEMENTS, 128), F32),
            pltpu.VMEM((ELEMENTS, AR, 128), BF16),
            pltpu.VMEM((ELEMENTS, AR, 128), BF16),
            pltpu.VMEM((ELEMENTS, TR, 256), BF16),
            pltpu.VMEM((BATCH, 256, 256), BF16),
            pltpu.VMEM((3, FIELD, COLS), F32),
            pltpu.VMEM((3, FIELD, COLS), F32),
            pltpu.VMEM((FIELD, COLS), F32),
            pltpu.VMEM((3, FIELD, COLS), F32),
            pltpu.VMEM((3, ELEMENTS, TR, COLS), F32),
            pltpu.VMEM((len(EACH), 256, COLS), BF16),
            pltpu.VMEM((ELEMENTS, 56, COLS), F32),
            pltpu.VMEM((6, ELEMENTS, 128), F32),
            pltpu.VMEM((32, 128), F32),
            pltpu.VMEM((2, 8, COLS), F32),
            pltpu.VMEM((sizes[0] * sizes[1] - 1, 8, COLS), F32),
            pltpu.VMEM((sizes[2] - 1, 8, COLS), F32),
            dma((8,)), dma((5,)),
            dma((3, 4, 4)), dma((3, 4, 4)), dma((3, 2)), dma((3, 2)), dma((6,)), dma((6,)), dma((2,)), dma((2,)),
            pltpu.VMEM(geometry.shape, F32),
            pltpu.SMEM(rock.shape, jnp.int32),
            pltpu.VMEM(permeability.shape, F32),
            pltpu.VMEM(mass_inv.shape, F32),
            pltpu.VMEM(div_map.shape, F32),
            pltpu.VMEM(trace_map.shape, F32),
            pltpu.SMEM(dirichlet.shape, jnp.int32),
            pltpu.VMEM((ELEMENTS * PRESS, COLS), BF16),
            pltpu.VMEM((ELEMENTS, 128), F32),
            pltpu.VMEM((128, 128), F32),
            pltpu.VMEM((128, 128), F32),
            pltpu.VMEM((128, 128), F32),
            pltpu.VMEM((128, 128), F32),
            pltpu.VMEM((FR, 384), BF16),
            pltpu.VMEM((TR + PR, 384), BF16),
            pltpu.VMEM((ELEMENTS * PR, 128), F32),
            pltpu.VMEM((ELEMENTS * PR, 128), F32),
            pltpu.VMEM((16, 128), F32),
            pltpu.VMEM((4, 432, 128), F32),
            pltpu.VMEM((WIDE // 2, FR, 256), F32),
            pltpu.VMEM((WIDE // 2, 384, 256), BF16),
            pltpu.VMEM((WIDE // 2, 384, 256), BF16),
            pltpu.VMEM((WIDE, 128, 128), BF16),
            pltpu.VMEM((14, PR, 128), F32),
        ],
        compiler_params=pltpu.CompilerParams(
            collective_id=0, has_side_effects=True, vmem_limit_bytes=GRANT
        ),
        name="solver",
    )(*arguments)


def recover_kernel(lam_hbm, hmat_hbm, forcing_hbm, traces_hbm, flux_hbm,
                   lam, hmat, forcing, traces, flux, weights, spread, load_sems, out_sems):
    pitch = 5
    first = rows_of((8, COLS)) < 4
    parts = ELEMENTS // BATCH
    rows_t, rows_f = BATCH * PRESS, BATCH * FLUX

    def loads(n):
        place = pl.ds(n * BATCH, BATCH)
        return [
            pltpu.make_async_copy(source.at[place], target.at[place], load_sems.at[n, which])
            for which, (source, target) in enumerate(
                ((lam_hbm, lam), (hmat_hbm, hmat), (forcing_hbm, forcing))
            )
        ]

    def stores(n):
        return [
            pltpu.make_async_copy(
                source.at[pl.ds(n * rows, rows)], target.at[pl.ds(n * rows, rows)], out_sems.at[n, which]
            )
            for which, (source, target, rows) in enumerate(
                ((traces, traces_hbm, rows_t), (flux, flux_hbm, rows_f))
            )
        ]

    for n in range(parts):
        for item in loads(n):
            item.start()

    @pl.loop(0, parts)
    def part(n):
        for item in loads(n):
            item.wait()
        for u in range(BATCH):
            e = n * BATCH + u
            tiles = [lam[e, 8 * tile : 8 * tile + 8, :] for tile in range(7)]
            start = n * rows_t + 108 * (u // 4) + u % 4
            for normal in range(3):
                traces[pl.ds(start + 36 * normal, 8, stride=4), :] = tiles[normal]
                traces[pl.ds(start + 36 * normal + 32, 1), :] = tiles[6][normal : normal + 1]
            high, low = halves(jnp.concatenate(tiles + [jnp.zeros((8, COLS), F32)], axis=0))
            weights[u, 0:TR, :] = high
            weights[u, TR : 2 * TR, :] = low
            weights[u, 2 * TR : 3 * TR, :] = high
            weights[u, 3 * TR : 3 * TR + PR, :] = forcing[e]
            weights[u, 3 * TR + PR :, :] = forcing[e]
        for u in range(BATCH):
            values = jnp.dot(hmat[n * BATCH + u], weights[u], preferred_element_type=F32)
            spread[pl.ds(FLUX * pitch * (u // 4) + u % 4, FLUX, stride=pitch), :] = -values[0:FLUX]
        for quad in range(BATCH * FLUX // 16):
            tiles = []
            for half in range(2):
                at = pitch * (4 * quad + 2 * half)
                tiles.append(jnp.where(first, spread[at : at + 8, :], spread[at + 1 : at + 9, :]))
            place = pl.ds(pl.multiple_of(n * rows_f + 16 * quad, 16), 16)
            flux[place, :] = jnp.concatenate(tiles, axis=0).astype(BF16)
        for item in stores(n):
            item.start()

    for n in range(parts):
        for item in stores(n):
            item.wait()


def recover(lam, hmat, forcing):
    hbm = pl.BlockSpec(memory_space=pltpu.HBM)
    out_shape = (
        jax.ShapeDtypeStruct((ELEMENTS * PRESS, COLS), F32),
        jax.ShapeDtypeStruct((ELEMENTS * FLUX, COLS), BF16),
    )
    return pl.pallas_call(
        recover_kernel,
        out_shape=out_shape,
        in_specs=[hbm] * 3,
        out_specs=[hbm] * 2,
        scratch_shapes=[
            pltpu.VMEM(item.shape, item.dtype) for item in (lam, hmat, forcing) + out_shape
        ] + [
            pltpu.VMEM((BATCH, 256, COLS), BF16),
            pltpu.VMEM((5 * BATCH * FLUX // 4 + 8, COLS), F32),
            pltpu.SemaphoreType.DMA((ELEMENTS // BATCH, 3)),
            pltpu.SemaphoreType.DMA((ELEMENTS // BATCH, 2)),
        ],
        compiler_params=pltpu.CompilerParams(vmem_limit_bytes=GRANT),
        name="recover",
    )(lam, hmat, forcing)


def body(sizes, sources, geometry, rock_class, permeability, mass_inv, div_map, trace_map, dirichlet):
    interleaved = sources.transpose(0, 1, 3, 2, 4).reshape(ELEMENTS * PRESS, COLS)
    lam, hmat, forcing = solve(
        sizes, interleaved, geometry, rock_class.transpose(0, 2, 1), permeability.T,
        mass_inv, div_map, trace_map, dirichlet.transpose(0, 3, 2, 1),
    )
    traces, flux = recover(lam, hmat, forcing)
    return (
        traces.reshape(BX, BY, PRESS, BZ, COLS).transpose(0, 1, 3, 2, 4),
        flux.reshape(BX, BY, FLUX, BZ, COLS).transpose(0, 1, 3, 2, 4),
    )


def solution(mesh):
    sizes = (mesh.shape["gx"], mesh.shape["gy"], mesh.shape["gz"])
    placed = (
        P("gx", "gy", "gz", None, None),
        P("gx", "gy", "gz", None),
        P("gx", "gy", "gz"),
        P(),
        P(),
        P(),
        P(),
        P("gx", "gy", "gz", None),
    )
    return jax.shard_map(
        functools.partial(body, sizes),
        mesh=mesh,
        in_specs=placed,
        out_specs=(P("gx", "gy", "gz", None, None), P("gx", "gy", "gz", None, None)),
        check_vma=False,
    )
```
